128 devices in a mesh: grp: 4 (over z), gz: 32 (over x, y, core).
Axes of the slice: x: 4, y: 4, z: 4, core: 2. Of those that a mesh axis runs over, the one named last changes fastest.
Arguments:
- load: float32 [3, 1024, 64, 128], P(None, ('grp', 'gz')), may hold values from -128 to 128
- phases: int32 [1024, 64, 128], P(('grp', 'gz')), may hold values from 0 to 3
- clamp: int32 [64, 128], replicated, may hold values 0 or 1
- phase_moduli: float32 [4], replicated, may hold values from 0.05 to 1
Outputs:
- displacement: float32 [3, 1024, 64, 128], P(None, ('grp', 'gz'))
- residual: float32 [3, 1024, 64, 128], P(None, ('grp', 'gz'))
The draws below stay inside these ranges and needn't reach their ends.
All inputs are finite; a program needn't handle non-finite values.
Results may differ from the reference program's by a relative error of at most 0.0003.
Values sent between devices are 32-bit elements; how exact they have to be, the bound alone decides.
No kernel may reach another device: no remote copies, remote signals or barrier semaphores. Data moves between devices by JAX's collectives and lax.ppermute only.
A program may use at most 128 MiB of HBM per device.

```python
import math
import jax
import jax.numpy as jnp
import numpy as np
from jax import lax

NX = 128
NY = 64
PHASES = 4
COARSEN = 8
CHEB = 4
ITERS = 2
NZ = 1024
COARSE_Y = 8
COARSE_X = 16
GROUP_COARSE = 32
N_GRP = 4


def draw_load(key, part):
    keys = jax.random.split(key, 2)
    shape = (3, NZ, NY, NX)
    base = jnp.clip(jax.random.normal(keys[0], shape, jnp.float32), -4.0, 4.0)
    rough = jnp.exp(jax.random.uniform(keys[1], shape, jnp.float32, -0.7, 0.7))
    depth = jnp.arange(NZ, dtype=jnp.float32)[None, :, None, None] / float(max(NZ - 1, 1))
    rising = jnp.exp(depth * math.log(3.0))
    return 0.5 * base * rough * rising


def place_ends(result, stream_key, least, largest):
    index_at = [jax.random.randint(jax.random.fold_in(stream_key, axis), (), 0, length) for axis, length in enumerate(result.shape)]
    main_axis = result.shape.index(max(result.shape))
    beside = index_at[:main_axis] + [(index_at[main_axis] + 1) % result.shape[main_axis]] + index_at[main_axis + 1:]
    return result.at[tuple(index_at)].set(least).at[tuple(beside)].set(largest)


def setup_inputs(seed: int = 0) -> dict:
    arg_keys = jax.random.split(jax.random.key(seed), 5)
    return {
        "load": draw_load(jax.random.fold_in(arg_keys[4], 71), 0),
        "phases": place_ends(jax.random.randint(arg_keys[1], (NZ, NY, NX), 0, PHASES), jax.random.fold_in(arg_keys[1], 1), 0, PHASES - 1).astype(jnp.int32),
        "clamp": place_ends((jax.random.randint(arg_keys[2], (NY, NX), 0, 4) < 3).astype(jnp.int32), jax.random.fold_in(arg_keys[2], 1), 0, 1),
        "phase_moduli": jnp.clip(jnp.exp(jax.random.uniform(arg_keys[3], (PHASES,), jnp.float32, math.log(0.05), math.log(1.0))), 0.05, 1.0),
    }


CORNER_OFFSETS = [(along_z, along_y, along_x) for along_z in (0, 1) for along_y in (0, 1) for along_x in (0, 1)]

def element_matrix():
    poisson = 0.3
    lame_first = poisson / ((1.0 + poisson) * (1.0 - 2.0 * poisson))
    shear = 1.0 / (2.0 * (1.0 + poisson))
    elastic = np.zeros((6, 6))
    elastic[:3, :3] = lame_first
    for axis_one in range(3):
        elastic[axis_one, axis_one] = lame_first + 2.0 * shear
        elastic[axis_one + 3, axis_one + 3] = shear
    points = [0.5 - 0.5 / math.sqrt(3.0), 0.5 + 0.5 / math.sqrt(3.0)]
    pairs = [(0, 1), (1, 2), (0, 2)]
    matrix = np.zeros((24, 24))
    for first_point in points:
        for second_point in points:
            for third_point in points:
                spot = (first_point, second_point, third_point)
                strain = np.zeros((6, 24))
                for corner, offset in enumerate(CORNER_OFFSETS):
                    values = [spot[axis_one] if offset[axis_one] else 1.0 - spot[axis_one] for axis_one in range(3)]
                    slopes = [1.0 if offset[axis_one] else -1.0 for axis_one in range(3)]
                    slants = []
                    for axis_one in range(3):
                        others = [values[axis_two] for axis_two in range(3) if axis_two != axis_one]
                        slants.append(slopes[axis_one] * others[0] * others[1])
                        strain[axis_one, 3 * corner + axis_one] = slants[axis_one]
                    for position, pair in enumerate(pairs):
                        strain[3 + position, 3 * corner + pair[0]] = slants[pair[1]]
                        strain[3 + position, 3 * corner + pair[1]] = slants[pair[0]]
                matrix = matrix + 0.125 * (strain.T @ elastic @ strain)
    return matrix

def spectral_bound(numbers):
    diagonal_part = np.array([numbers[index, index] for index in range(numbers.shape[0])])
    return float(np.max(np.sum(np.abs(numbers), axis=1) / diagonal_part))

def element_forces(extended, moduli, matrix):
    layers = moduli.shape[0]
    width = min(4, layers)
    blocks = (layers + width - 1) // width
    extra = blocks * width - layers
    plane = tuple(extended.shape[2:])
    if extra > 0:
        moduli = jnp.concatenate([moduli, jnp.zeros((extra,) + tuple(moduli.shape[1:]), moduli.dtype)], 0)
        extended = jnp.concatenate([extended, jnp.zeros((3, extra) + plane, extended.dtype)], 1)

    def add_block(total, index):
        start = index * width
        nodes = lax.dynamic_slice_in_dim(extended, start, width + 1, 1)
        weights = lax.dynamic_slice_in_dim(moduli, start, width, 0)
        gathered = jnp.stack([jnp.roll(nodes[:, along_z:along_z + width], (-along_y, -along_x), (2, 3)) for along_z, along_y, along_x in CORNER_OFFSETS], 0)
        gathered = gathered.reshape((24, width) + plane)
        forces = jnp.einsum('ij,jzyx->izyx', matrix, gathered, precision=lax.Precision.HIGHEST) * weights
        forces = forces.reshape((8, 3, width) + plane)
        update = jnp.zeros((3, width + 1) + plane, jnp.float32)
        for corner, offset in enumerate(CORNER_OFFSETS):
            update = update.at[:, offset[0]:offset[0] + width].add(jnp.roll(forces[corner], (offset[1], offset[2]), (2, 3)))
        current = lax.dynamic_slice_in_dim(total, start, width + 1, 1)
        return (lax.dynamic_update_slice_in_dim(total, current + update, start, 1), None)
    initial = jnp.zeros(extended.shape, jnp.float32)
    total, unused = lax.scan(add_block, initial, jnp.arange(blocks, dtype=jnp.int32))
    return total[:, :layers + 1]

def node_diagonal(lower, moduli, matrix):
    layers = moduli.shape[0]
    extended = jnp.concatenate([lower, moduli], 0)
    entries = jnp.diagonal(matrix).reshape(8, 3)
    total = jnp.zeros((3,) + tuple(moduli.shape), jnp.float32)
    for corner, offset in enumerate(CORNER_OFFSETS):
        shifted = jnp.roll(extended[1 - offset[0]:1 - offset[0] + layers], (offset[1], offset[2]), (1, 2))
        total = total + entries[corner][:, None, None, None] * shifted[None]
    return total

def chebyshev(rhs, coarse_apply, coarse_inverse, bound, sweeps):
    top = bound
    bottom = bound / 20.0
    center = 0.5 * (top + bottom)
    radius = 0.5 * (top - bottom)
    sigma = center / radius
    rho = 1.0 / sigma
    update = coarse_inverse * rhs / center
    correction = update
    remainder = rhs
    for sweep in range(sweeps - 1):
        remainder = remainder - coarse_apply(update)
        rho_next = 1.0 / (2.0 * sigma - rho)
        update = rho_next * rho * update + 2.0 * rho_next / radius * coarse_inverse * remainder
        correction = correction + update
        rho = rho_next
    return correction

def restrict(field, factor):
    comps, layers, height, breadth = field.shape
    return field.reshape(comps, layers // factor, factor, height // factor, factor, breadth // factor, factor).sum((2, 4, 6))

def prolong(coarse, factor):
    comps, layers, height, breadth = coarse.shape
    expanded = jnp.broadcast_to(coarse[:, :, None, :, None, :, None], (comps, layers, factor, height, factor, breadth, factor))
    return expanded.reshape(comps, layers * factor, height * factor, breadth * factor)

def reference(load, phases, clamp, phase_moduli):
    numbers = element_matrix()
    matrix = jnp.asarray(numbers, jnp.float32)
    bound = spectral_bound(numbers)
    omega = 1.2 / bound
    depth = jnp.arange(NZ, dtype=jnp.int32)[:, None, None]
    rows_at = jnp.arange(NY, dtype=jnp.int32)[None, :, None]
    columns_at = jnp.arange(NX, dtype=jnp.int32)[None, None, :]
    picked = jnp.zeros((NZ, NY, NX), jnp.float32)
    for phase in range(PHASES):
        picked = picked + jnp.where(phases == phase, phase_moduli[phase], jnp.float32(0.0))
    outside = (depth == NZ - 1) | (rows_at == NY - 1) | (columns_at == NX - 1)
    moduli = jnp.where(outside, jnp.float32(0.0), picked)
    free = jnp.where((depth == 0) & (clamp[None] == 1), 0.0, 1.0).astype(jnp.float32)
    edge = jnp.zeros((1, NY, NX), jnp.float32)
    inverse = 1.0 / (free * node_diagonal(edge, moduli, matrix) + 1.0 - free)
    top_layer = jnp.zeros((3, 1, NY, NX), jnp.float32)

    def operator(field):
        total = element_forces(jnp.concatenate([free * field, top_layer], 1), moduli, matrix)
        return free * total[:, :-1] + (1.0 - free) * field
    factor = COARSEN
    block_mean = moduli.reshape(NZ // factor, factor, COARSE_Y, factor, COARSE_X, factor).mean((1, 3, 5))
    coarse_depth = jnp.arange(NZ // factor, dtype=jnp.int32)[:, None, None]
    coarse_rows = jnp.arange(COARSE_Y, dtype=jnp.int32)[None, :, None]
    coarse_columns = jnp.arange(COARSE_X, dtype=jnp.int32)[None, None, :]
    coarse_edge = (coarse_depth % GROUP_COARSE == GROUP_COARSE - 1) | (coarse_rows == COARSE_Y - 1) | (coarse_columns == COARSE_X - 1)
    group_moduli = jnp.where(coarse_edge, jnp.float32(0.0), block_mean).reshape(N_GRP, GROUP_COARSE, COARSE_Y, COARSE_X)
    coarse_matrix = factor * matrix
    coarse_bottom = jnp.zeros((1, COARSE_Y, COARSE_X), jnp.float32)
    coarse_top = jnp.zeros((3, 1, COARSE_Y, COARSE_X), jnp.float32)
    coarse_inverse = jax.vmap(lambda weights: 1.0 / node_diagonal(coarse_bottom, weights, coarse_matrix))(group_moduli)

    def solve_one(rhs, weights, group_inverse):

        def coarse_apply(field):
            return element_forces(jnp.concatenate([field, coarse_top], 1), weights, coarse_matrix)[:, :-1]
        return chebyshev(rhs, coarse_apply, group_inverse, bound, CHEB)

    def precondition(current):
        first = omega * current * inverse
        defect = current - operator(first)
        restricted = restrict(defect, factor).reshape(3, N_GRP, GROUP_COARSE, COARSE_Y, COARSE_X)
        solved = jax.vmap(solve_one)(jnp.moveaxis(restricted, 1, 0), group_moduli, coarse_inverse)
        own = jnp.moveaxis(solved, 0, 1).reshape(3, NZ // factor, COARSE_Y, COARSE_X)
        second = first + free * prolong(own, factor)
        return second + omega * (current - operator(second)) * inverse
    rhs = free * load
    displacement = jnp.zeros_like(rhs)
    residual = rhs
    preconditioned = precondition(residual)
    direction = preconditioned
    gamma = jnp.sum(residual * preconditioned)
    for step in range(ITERS):
        image = operator(direction)
        alpha = gamma / jnp.sum(direction * image)
        displacement = displacement + alpha * direction
        residual = residual - alpha * image
        if step + 1 < ITERS:
            preconditioned = precondition(residual)
            following = jnp.sum(residual * preconditioned)
            direction = preconditioned + following / gamma * direction
            gamma = following
    return (displacement, residual)
```

```python
import functools
import math

import jax
import jax.numpy as jnp
import numpy as np
from jax import lax
from jax.experimental import pallas as pl
from jax.experimental.pallas import tpu as pltpu
from jax.sharding import PartitionSpec as P

COARSEN = 8
CHEB = 4
BOTH = ("grp", "gz")
GROUP = 32
H = 5
EXT = 17
WINDOW = 16
CORNER_OFFSETS = [(a, b, c) for a in (0, 1) for b in (0, 1) for c in (0, 1)]


def element_matrix():
    poisson = 0.3
    lame_first = poisson / ((1.0 + poisson) * (1.0 - 2.0 * poisson))
    shear = 1.0 / (2.0 * (1.0 + poisson))
    elastic = np.zeros((6, 6))
    elastic[:3, :3] = lame_first
    for axis_one in range(3):
        elastic[axis_one, axis_one] = lame_first + 2.0 * shear
        elastic[axis_one + 3, axis_one + 3] = shear
    points = [0.5 - 0.5 / math.sqrt(3.0), 0.5 + 0.5 / math.sqrt(3.0)]
    pairs = [(0, 1), (1, 2), (0, 2)]
    matrix = np.zeros((24, 24))
    for first_point in points:
        for second_point in points:
            for third_point in points:
                spot = (first_point, second_point, third_point)
                strain = np.zeros((6, 24))
                for corner, offset in enumerate(CORNER_OFFSETS):
                    values = [spot[i] if offset[i] else 1.0 - spot[i] for i in range(3)]
                    slopes = [1.0 if offset[i] else -1.0 for i in range(3)]
                    slants = []
                    for axis_one in range(3):
                        others = [values[i] for i in range(3) if i != axis_one]
                        slants.append(slopes[axis_one] * others[0] * others[1])
                        strain[axis_one, 3 * corner + axis_one] = slants[axis_one]
                    for position, pair in enumerate(pairs):
                        strain[3 + position, 3 * corner + pair[0]] = slants[pair[1]]
                        strain[3 + position, 3 * corner + pair[1]] = slants[pair[0]]
                matrix = matrix + 0.125 * (strain.T @ elastic @ strain)
    return matrix


NUMBERS = element_matrix()
BOUND = float(np.max(np.sum(np.abs(NUMBERS), axis=1) / np.diag(NUMBERS)))
OMEGA = 1.2 / BOUND
DIAGONAL = float(np.mean(np.diag(NUMBERS)))


def mode_matrix():
    haar = np.array([[1.0, 1.0], [-1.0, 1.0]])
    change = np.kron(np.kron(np.kron(haar, haar), haar), np.eye(3))
    return change @ NUMBERS @ change.T / 64.0


def mode_groups():
    modes = mode_matrix()
    near = np.abs(modes) > 1e-9
    left = [i for i in range(24) if near[i].any()]
    groups = []
    while left:
        group = [left[0]]
        for i in group:
            group += [j for j in left if near[i, j] and j not in group]
        groups.append(sorted(group))
        left = [i for i in left if i not in group]
    return modes, groups


MODES, MODE_GROUPS = mode_groups()


def mode_forces(value, scale):
    force = [None] * 24
    for group in MODE_GROUPS:
        diagonal = [float(MODES[i, i]) * scale for i in group]
        if len(group) == 1:
            force[group[0]] = diagonal[0] * value[group[0]]
            continue
        across = float(MODES[group[0], group[1]]) * scale
        apart = diagonal[0] - across
        total = value[group[0]]
        for i in group[1:]:
            total = total + value[i]
        total = across * total
        for i in group:
            if abs(apart) < 1e-9:
                force[i] = total
            else:
                force[i] = apart * value[i] + total
    return force


def lanes(value, by):
    return pltpu.roll(value, by % value.shape[1], 1)


def rows(value, by):
    return pltpu.roll(value, by % value.shape[0], 0)


def at(j):
    return slice(8 * j, 8 * j + 8)


def stiff(low, high, field, finish, moduli_ref, along_ref, up_ref, free):
    row = lax.broadcasted_iota(jnp.int32, (8, 128), 0)
    first_row = row == 0
    last_row = row == 7

    def x_modes(n, j):
        held = free(n, j)
        result = []
        for value in field(n, j):
            value = value * held
            beside = lanes(value, -1)
            result += [value + beside, beside - value]
        return result

    def xy_modes(n, j, here):
        if j < 7:
            values = x_modes(n, j + 1)
            after = (values, [rows(v, -1) for v in values])
        else:
            zero = jnp.zeros((8, 128), jnp.float32)
            after = ([zero] * 6, [zero] * 6)
        result = []
        for value, rolled, rolled_after in zip(here[0], here[1], after[1]):
            beside = jnp.where(last_row, rolled_after, rolled)
            result += [value + beside, beside - value]
        return result, after

    def start(n):
        values = x_modes(n, 0)
        return values, [rows(v, -1) for v in values]

    def layer(n, begin):
        here = start(n)
        carried = [jnp.zeros((8, 128), jnp.float32)] * 6
        for j in range(8):
            now, here = xy_modes(n, j, here)
            before = [along_ref[q, at(j), :] for q in range(12)]
            for q in range(12):
                along_ref[q, at(j), :] = now[q]
            weight = moduli_ref[n - 1, at(j), :]
            value = [None] * 24
            for k in range(3):
                for c in range(2):
                    for b in range(2):
                        q = 4 * k + 2 * c + b
                        value[3 * (2 * b + c) + k] = before[q] + now[q]
                        value[3 * (4 + 2 * b + c) + k] = now[q] - before[q]
            force = mode_forces(value, 1.0)
            done = {}
            weighted = []
            for i in range(24):
                f = force[i]
                if f is None:
                    weighted.append(None)
                    continue
                if id(f) not in done:
                    done[id(f)] = weight * f
                weighted.append(done[id(f)])
            totals = []
            for k in range(3):
                for c in range(2):
                    for b in range(2):
                        q = 4 * k + 2 * c + b
                        same = weighted[3 * (2 * b + c) + k]
                        change = weighted[3 * (4 + 2 * b + c) + k]
                        if not begin:
                            total = up_ref[q, at(j), :] - change
                            totals.append(total if same is None else total + same)
                        up_ref[q, at(j), :] = change if same is None else same + change
            if begin:
                continue
            out = []
            for k in range(3):
                parts = []
                for c in range(2):
                    same, change = totals[4 * k + 2 * c], totals[4 * k + 2 * c + 1]
                    over = rows(same + change, 1)
                    parts.append(same - change + jnp.where(first_row, carried[2 * k + c], over))
                    carried[2 * k + c] = over
                out.append(parts[0] - parts[1] + lanes(parts[0] + parts[1], 1))
            finish(n - 1, j, out)

    here = start(low - 1)
    for j in range(8):
        now, here = xy_modes(low - 1, j, here)
        for q in range(12):
            along_ref[q, at(j), :] = now[q]
    layer(low, True)

    def step(n, unused):
        layer(n, False)
        return unused

    lax.fori_loop(low + 1, high + 1, step, 0)


def free_of(keep_ref, tile):
    def free(n, j):
        inside = jnp.where(tile * 8 + n == H, jnp.float32(0.0), jnp.float32(1.0))
        return jnp.maximum(keep_ref[at(j), :], inside)

    return free


def tile_index():
    return lax.axis_index("grp") * lax.axis_size("gz") + lax.axis_index("gz")


def coarse_pattern():
    fine = lax.broadcasted_iota(jnp.int32, (128, 128), 0)
    lane = lax.broadcasted_iota(jnp.int32, (128, 128), 1)
    return jnp.where((fine >> 3) == (lane & 15), 1.0, 0.0).astype(jnp.float32)


def exact_dot(a, b, contract):
    return lax.dot_general(
        a, b, (contract, ((), ())), precision=lax.Precision.HIGHEST,
        preferred_element_type=jnp.float32,
    )


def block_sums(planes):
    count = planes.shape[0] // 64
    summed = exact_dot(planes, coarse_pattern(), ((1,), (0,)))
    row = lax.broadcasted_iota(jnp.int32, (64, 128), 0)
    lane = lax.broadcasted_iota(jnp.int32, (64, 128), 1)
    own = (row >> 3) == (lane >> 4)
    return [
        jnp.sum(jnp.where(own, summed[64 * k : 64 * k + 64], 0.0), axis=0, keepdims=True)
        for k in range(count)
    ]


def send_rows(out_ref, four):
    block = jnp.concatenate(four + four, 0)
    for i in range(out_ref.shape[0] // 8):
        out_ref[at(i), :] = block


def coarse_solve(gathered_ref, coarse_ref, tile, window_ref, solved_ref, spread_ref):
    begin = window_begin(tile)
    window_ref[...] = gathered_ref[pl.ds(pl.multiple_of(4 * begin, 8), 4 * WINDOW), :]
    rhs = [window_ref[pl.ds(k, WINDOW, stride=4), :] for k in range(3)]
    if coarse_ref is None:
        moduli = window_ref[pl.ds(3, WINDOW, stride=4), :]
        row = lax.broadcasted_iota(jnp.int32, (WINDOW, 128), 0)
        moduli = jnp.where(row == WINDOW - 1, 0.0, moduli)
    else:
        moduli = coarse_ref[...]
    summed = moduli + lanes(moduli, 1)
    summed = summed + lanes(summed, 16)
    summed = DIAGONAL * COARSEN * (summed + rows(summed, 1))
    inverse = jnp.where(summed > 0.0, 1.0 / jnp.where(summed > 0.0, summed, 1.0), 0.0)

    def apply(field):
        value = [None] * 24
        for k in range(3):
            near = lanes(field[k], -1)
            for c, along_x in enumerate((field[k] + near, near - field[k])):
                near_y = lanes(along_x, -16)
                for b, along_y in enumerate((along_x + near_y, near_y - along_x)):
                    near_z = rows(along_y, -1)
                    value[3 * (2 * b + c) + k] = along_y + near_z
                    value[3 * (4 + 2 * b + c) + k] = near_z - along_y
        force = [None if f is None else moduli * f for f in mode_forces(value, COARSEN)]
        result = []
        for k in range(3):
            parts_x = []
            for c in range(2):
                parts_y = []
                for b in range(2):
                    same, change = force[3 * (2 * b + c) + k], force[3 * (4 + 2 * b + c) + k]
                    if same is None:
                        parts_y.append(rows(change, 1) - change)
                    else:
                        parts_y.append(same - change + rows(same + change, 1))
                parts_x.append(parts_y[0] - parts_y[1] + lanes(parts_y[0] + parts_y[1], 16))
            result.append(parts_x[0] - parts_x[1] + lanes(parts_x[0] + parts_x[1], 1))
        return result

    bottom = BOUND / 20.0
    center = 0.5 * (BOUND + bottom)
    radius = 0.5 * (BOUND - bottom)
    sigma = center / radius
    rho = 1.0 / sigma
    update = [inverse * (s * (1.0 / center)) for s in rhs]
    correction = update
    remainder = rhs
    for sweep in range(CHEB - 1):
        image = apply(update)
        remainder = [r - a for r, a in zip(remainder, image)]
        rho_next = 1.0 / (2.0 * sigma - rho)
        update = [
            (rho_next * rho) * u + (2.0 * rho_next / radius) * (inverse * r)
            for u, r in zip(update, remainder)
        ]
        correction = [c + u for c, u in zip(correction, update)]
        rho = rho_next
    row = lax.broadcasted_iota(jnp.int32, (8, 128), 0)
    lane = lax.broadcasted_iota(jnp.int32, (8, 128), 1)
    own = row == (lane >> 4)
    for k in range(3):
        solved_ref[WINDOW * k : WINDOW * (k + 1), :] = correction[k]
    blocks = []
    for which in range(3):
        place = jnp.clip(tile - begin + which - 1, 0, WINDOW - 1)
        for k in range(3):
            line = solved_ref[pl.ds(WINDOW * k + place, 1), :]
            blocks.append(jnp.where(own, jnp.broadcast_to(line, (8, 128)), 0.0))
    spread_ref[...] = exact_dot(
        jnp.concatenate(blocks, 0), coarse_pattern(), ((1,), (1,))
    )
    return moduli


def window_begin(tile):
    return 2 * jnp.minimum(jnp.maximum(tile - 7, 0) >> 1, (128 - WINDOW) // 2)


def correction_of(spread_ref):
    def correction(n, j):
        which = jnp.where(n < H, 0, jnp.where(n < H + 8, 1, 2))
        return [
            jnp.broadcast_to(spread_ref[pl.ds((3 * which + k) * 8 + j, 1), :], (8, 128))
            for k in range(3)
        ]

    return correction


def set_up_kernel(load_ref, phases_ref, below_ref, above_ref, clamp_ref, table_ref,
                  rhs_ref, moduli_ref, inverse_ref, keep_ref, send_ref,
                  along_ref, up_ref, sum_ref):
    tile = tile_index()
    keep_ref[...] = 1.0 - clamp_ref[...].astype(jnp.float32)
    row = lax.broadcasted_iota(jnp.int32, (64, 128), 0)
    lane = lax.broadcasted_iota(jnp.int32, (64, 128), 1)
    interior = (row < 63) & (lane < 127)
    table = [table_ref[i] for i in range(4)]

    def pick(labels, n):
        depth = tile * 8 + n
        inside = interior & ((depth >= 0) & (depth < 1023))
        value = jnp.zeros((64, 128), jnp.float32)
        for i in range(4):
            value = jnp.where(labels == i, table[i], value)
        return jnp.where(inside, value, 0.0)

    for n in range(-5, 0):
        moduli_ref[n + H] = pick(below_ref[12 + n + 5].astype(jnp.int32), n)
    total = jnp.zeros((64, 128), jnp.float32)
    for n in range(8):
        value = pick(phases_ref[n], n)
        moduli_ref[n + H] = value
        total = total + value
    for n in range(8, 12):
        moduli_ref[n + H] = pick(above_ref[12 + n - 8].astype(jnp.int32), n)
    sum_ref[3] = total
    free = free_of(keep_ref, tile)

    for n in range(-4, 12):
        depth = tile * 8 + n
        both = moduli_ref[n - 1 + H] + moduli_ref[n + H]
        both = both + rows(both, 1)
        both = DIAGONAL * (both + lanes(both, 1))
        inside = jnp.where(depth == 0, jnp.float32(0.0), jnp.float32(1.0))
        held = jnp.maximum(keep_ref[...], inside)
        both = held * both + 1.0 - held
        exists = (depth >= 0) & (depth < 1024)
        both = jnp.where(exists, both, 1.0)
        inverse_ref[n + H] = jnp.where(exists, 1.0 / both, 0.0)
        for k in range(3):
            if n < 0:
                value = below_ref[4 * k + n + 4]
            elif n < 8:
                value = load_ref[k, n]
            else:
                value = above_ref[4 * k + n - 8]
            rhs_ref[k, n + H] = held * value

    for k in range(3):
        sum_ref[k] = jnp.zeros((64, 128), jnp.float32)

    def first(n, j):
        scaled = OMEGA * inverse_ref[n, at(j), :]
        return [rhs_ref[k, n, at(j), :] * scaled for k in range(3)]

    def finish(n, j, out):
        held = free(n, j) > 0.0
        value = first(n, j)
        for k in range(3):
            image = jnp.where(held, out[k], value[k])
            sum_ref[k, at(j), :] += rhs_ref[k, n, at(j), :] - image

    stiff(5, 13, first, finish, moduli_ref, along_ref, up_ref, free)
    four = block_sums(sum_ref[...].reshape(256, 128))
    lane = lax.broadcasted_iota(jnp.int32, (1, 128), 1)
    edge = (lane >= 112) | ((lane & 15) == 15) | (lax.rem(tile, GROUP) == GROUP - 1)
    four[3] = jnp.where(edge, 0.0, four[3] * (1.0 / 512.0))
    send_rows(send_ref, four)


def middle_kernel(gathered_ref, rhs_ref, moduli_ref, inverse_ref, keep_ref,
                  ahead_ref, image_ref, coarse_ref, send_ref,
                  along_ref, up_ref, sum_ref, dots_ref, window_ref, solved_ref, spread_ref):
    tile = tile_index()
    free = free_of(keep_ref, tile)
    coarse_ref[...] = coarse_solve(gathered_ref, None, tile, window_ref, solved_ref, spread_ref)
    correction = correction_of(spread_ref)

    def second(n, j):
        scaled = OMEGA * inverse_ref[n, at(j), :]
        held = free(n, j)
        result = []
        for k, coarse_value in enumerate(correction(n, j)):
            value = rhs_ref[k, n, at(j), :] * scaled + held * coarse_value
            result.append(value)
        return result

    def smooth(n, j, out):
        held = free(n, j) > 0.0
        scaled = OMEGA * inverse_ref[n, at(j), :]
        for k, value in enumerate(second(n, j)):
            image = jnp.where(held, out[k], value)
            ahead_ref[k, n, at(j), :] = value + (rhs_ref[k, n, at(j), :] - image) * scaled

    stiff(2, 16, second, smooth, moduli_ref, along_ref, up_ref, free)

    def ahead(n, j):
        return [ahead_ref[k, n, at(j), :] for k in range(3)]

    def keep_image(n, j, out):
        held = free(n, j) > 0.0
        for k in range(3):
            image_ref[k, n, at(j), :] = jnp.where(
                held, out[k], ahead_ref[k, n, at(j), :]
            )

    stiff(3, 15, ahead, keep_image, moduli_ref, along_ref, up_ref, free)

    for k in range(3):
        sum_ref[k] = jnp.zeros((64, 128), jnp.float32)
    dots_ref[...] = jnp.zeros_like(dots_ref)

    def first(n, j):
        scaled = OMEGA * inverse_ref[n, at(j), :]
        return [image_ref[k, n, at(j), :] * scaled for k in range(3)]

    def finish(n, j, out):
        held = free(n, j) > 0.0
        value = first(n, j)
        for k in range(3):
            image = image_ref[k, n, at(j), :]
            sum_ref[k, at(j), :] += image - jnp.where(held, out[k], value[k])
            now = ahead_ref[k, n, at(j), :]
            dots_ref[0, k] += now * rhs_ref[k, n, at(j), :]
            dots_ref[1, k] += now * image

    stiff(5, 13, first, finish, moduli_ref, along_ref, up_ref, free)
    three = block_sums(sum_ref[...].reshape(192, 128))
    lane = lax.broadcasted_iota(jnp.int32, (1, 128), 1)
    gamma = jnp.sum(dots_ref[0])
    energy = jnp.sum(dots_ref[1])
    dots = jnp.where(lane == 0, gamma, jnp.where(lane == 1, energy, 0.0))
    send_rows(send_ref, three + [dots])


def lane_value(line, i):
    lane = lax.broadcasted_iota(jnp.int32, line.shape, 1)
    return jnp.sum(jnp.where(lane == i, line, 0.0))


def last_kernel(gathered_ref, rhs_ref, moduli_ref, inverse_ref, keep_ref, ahead_ref, image_ref,
                coarse_ref,
                next_ref, next_image_ref, scalars_ref, send_ref,
                whole_ref, along_ref, up_ref, dots_ref, window_ref, solved_ref, spread_ref):
    tile = tile_index()
    free = free_of(keep_ref, tile)
    dots = jnp.sum(gathered_ref[pl.ds(3, 128, stride=4), :], axis=0, keepdims=True)
    scalars_ref[...] = jnp.broadcast_to(dots, (8, 128))
    alpha = lane_value(dots, 0) / lane_value(dots, 1)
    coarse_solve(gathered_ref, coarse_ref, tile, window_ref, solved_ref, spread_ref)
    correction = correction_of(spread_ref)

    def second(n, j):
        scaled = OMEGA * inverse_ref[n, at(j), :]
        held = free(n, j)
        result = []
        for k, coarse_value in enumerate(correction(n, j)):
            value = image_ref[k, n, at(j), :] * scaled + held * coarse_value
            result.append(value)
        return result

    def smooth(n, j, out):
        held = free(n, j) > 0.0
        scaled = OMEGA * inverse_ref[n, at(j), :]
        for k, value in enumerate(second(n, j)):
            image = jnp.where(held, out[k], value)
            value = value + (image_ref[k, n, at(j), :] - image) * scaled
            whole_ref[k, n, at(j), :] = ahead_ref[k, n, at(j), :] - alpha * value

    stiff(4, 14, second, smooth, moduli_ref, along_ref, up_ref, free)
    dots_ref[...] = jnp.zeros_like(dots_ref)

    def ahead(n, j):
        return [whole_ref[k, n, at(j), :] for k in range(3)]

    def finish(n, j, out):
        held = free(n, j) > 0.0
        for k in range(3):
            value = whole_ref[k, n, at(j), :]
            image = jnp.where(held, out[k], value)
            next_ref[k, n - H, at(j), :] = value
            next_image_ref[k, n - H, at(j), :] = image
            before = image_ref[k, n, at(j), :]
            dots_ref[0, k] += value * (rhs_ref[k, n, at(j), :] - alpha * before)
            dots_ref[1, k] += value * image
            dots_ref[2, k] += value * before

    stiff(5, 13, ahead, finish, moduli_ref, along_ref, up_ref, free)
    lane = lax.broadcasted_iota(jnp.int32, (8, 128), 1)
    line = jnp.zeros((8, 128), jnp.float32)
    for i in range(3):
        line = jnp.where(lane == i, jnp.sum(dots_ref[i]), line)
    for i in range(16):
        send_ref[at(i), :] = line


def close_kernel(gathered_ref, scalars_ref, rhs_ref, ahead_ref, image_ref, next_ref,
                 next_image_ref, displacement_ref, residual_ref):
    before = scalars_ref[0:1, :]
    gamma, energy = lane_value(before, 0), lane_value(before, 1)
    dots = jnp.sum(gathered_ref[...], axis=0, keepdims=True)
    following, own, cross = (lane_value(dots, i) for i in range(3))
    alpha = gamma / energy
    beta = following / gamma
    alpha_next = following / (own + 2.0 * beta * cross + beta * beta * energy)

    def step(n, unused):
        for k in range(3):
            ahead = ahead_ref[k, n + H]
            image = image_ref[k, n + H]
            direction = next_ref[k, n] + beta * ahead
            displacement_ref[k, n] = alpha * ahead + alpha_next * direction
            residual = rhs_ref[k, n + H] - alpha * image
            residual_ref[k, n] = residual - alpha_next * (next_image_ref[k, n] + beta * image)
        return unused

    lax.fori_loop(0, 8, step, 0)


def call(kernel, outs, scratch, *args, smem=()):
    spaces = [
        pl.BlockSpec(memory_space=pltpu.SMEM if i in smem else pltpu.VMEM)
        for i in range(len(args))
    ]
    return pl.pallas_call(
        kernel,
        out_shape=[jax.ShapeDtypeStruct(s, jnp.float32) for s in outs],
        in_specs=spaces,
        out_specs=[pl.BlockSpec(memory_space=pltpu.VMEM)] * len(outs),
        scratch_shapes=[pltpu.VMEM(s, jnp.float32) for s in scratch],
        compiler_params=pltpu.CompilerParams(vmem_limit_bytes=40 * 2**20),
    )(*args)


def to_all(block):
    count = block.shape[0] // 128
    parts = lax.all_to_all(block.reshape(128, count, 128), BOTH, 0, 0)
    return parts.reshape(block.shape)


def body(load, phases, clamp, phase_moduli):
    size = lax.axis_size(BOTH)
    labels = phases.astype(jnp.float32)
    top = jnp.concatenate([load[:, 4:].reshape(12, 64, 128), labels[3:]], 0)
    low = jnp.concatenate([load[:, :4].reshape(12, 64, 128), labels[:4]], 0)
    below = lax.ppermute(top, BOTH, [(i, i + 1) for i in range(size - 1)])
    above = lax.ppermute(low, BOTH, [(i + 1, i) for i in range(size - 1)])

    plane = (64, 128)
    field = (3, EXT) + plane
    work = [(12,) + plane, (12,) + plane]
    rhs, moduli, inverse, keep, send = call(
        set_up_kernel,
        [field, (EXT,) + plane, (EXT,) + plane, plane, (512, 128)],
        work + [(4,) + plane],
        load, phases, below, above, clamp, phase_moduli, smem=(5,),
    )
    gathered = to_all(send)
    ahead, image, coarse, send = call(
        middle_kernel,
        [field, field, (WINDOW, 128), (512, 128)],
        work + [(3,) + plane, (2, 3, 8, 128), (4 * WINDOW, 128), (3 * WINDOW, 128), (72, 128)],
        gathered, rhs, moduli, inverse, keep,
    )
    gathered = to_all(send)
    own = (3, 8) + plane
    following, following_image, scalars, send = call(
        last_kernel,
        [own, own, (8, 128), (128, 128)],
        [field] + work + [(3, 3, 8, 128), (4 * WINDOW, 128), (3 * WINDOW, 128), (72, 128)],
        gathered, rhs, moduli, inverse, keep, ahead, image, coarse,
    )
    gathered = to_all(send)
    displacement, residual = call(
        close_kernel, [own, own], [],
        gathered, scalars, rhs, ahead, image, following, following_image,
    )
    return displacement, residual


def solution(mesh):
    placed = (P(None, BOTH, None, None), P(BOTH, None, None), P(), P())
    return jax.shard_map(
        body,
        mesh=mesh,
        in_specs=placed,
        out_specs=(P(None, BOTH, None, None), P(None, BOTH, None, None)),
        check_vma=False,
    )
```

```python
import functools
import math

import jax
import jax.numpy as jnp
import numpy as np
from jax import lax
from jax.experimental import pallas as pl
from jax.experimental.pallas import tpu as pltpu
from jax.sharding import PartitionSpec as P

COARSEN = 8
CHEB = 4
BOTH = ("grp", "gz")
GROUP = 32
H = 5
EXT = 17
WINDOW = 16
CORNER_OFFSETS = [(a, b, c) for a in (0, 1) for b in (0, 1) for c in (0, 1)]


def element_matrix():
    poisson = 0.3
    lame_first = poisson / ((1.0 + poisson) * (1.0 - 2.0 * poisson))
    shear = 1.0 / (2.0 * (1.0 + poisson))
    elastic = np.zeros((6, 6))
    elastic[:3, :3] = lame_first
    for axis_one in range(3):
        elastic[axis_one, axis_one] = lame_first + 2.0 * shear
        elastic[axis_one + 3, axis_one + 3] = shear
    points = [0.5 - 0.5 / math.sqrt(3.0), 0.5 + 0.5 / math.sqrt(3.0)]
    pairs = [(0, 1), (1, 2), (0, 2)]
    matrix = np.zeros((24, 24))
    for first_point in points:
        for second_point in points:
            for third_point in points:
                spot = (first_point, second_point, third_point)
                strain = np.zeros((6, 24))
                for corner, offset in enumerate(CORNER_OFFSETS):
                    values = [spot[i] if offset[i] else 1.0 - spot[i] for i in range(3)]
                    slopes = [1.0 if offset[i] else -1.0 for i in range(3)]
                    slants = []
                    for axis_one in range(3):
                        others = [values[i] for i in range(3) if i != axis_one]
                        slants.append(slopes[axis_one] * others[0] * others[1])
                        strain[axis_one, 3 * corner + axis_one] = slants[axis_one]
                    for position, pair in enumerate(pairs):
                        strain[3 + position, 3 * corner + pair[0]] = slants[pair[1]]
                        strain[3 + position, 3 * corner + pair[1]] = slants[pair[0]]
                matrix = matrix + 0.125 * (strain.T @ elastic @ strain)
    return matrix


NUMBERS = element_matrix()
BOUND = float(np.max(np.sum(np.abs(NUMBERS), axis=1) / np.diag(NUMBERS)))
OMEGA = 1.2 / BOUND
DIAGONAL = float(np.mean(np.diag(NUMBERS)))


def mode_matrix():
    haar = np.array([[1.0, 1.0], [-1.0, 1.0]])
    change = np.kron(np.kron(np.kron(haar, haar), haar), np.eye(3))
    return change @ NUMBERS @ change.T / 64.0


def mode_groups():
    modes = mode_matrix()
    near = np.abs(modes) > 1e-9
    left = [i for i in range(24) if near[i].any()]
    groups = []
    while left:
        group = [left[0]]
        for i in group:
            group += [j for j in left if near[i, j] and j not in group]
        groups.append(sorted(group))
        left = [i for i in left if i not in group]
    return modes, groups


MODES, MODE_GROUPS = mode_groups()


def mode_forces(value, scale):
    force = [None] * 24
    for group in MODE_GROUPS:
        diagonal = [float(MODES[i, i]) * scale for i in group]
        if len(group) == 1:
            force[group[0]] = diagonal[0] * value[group[0]]
            continue
        across = float(MODES[group[0], group[1]]) * scale
        apart = diagonal[0] - across
        total = value[group[0]]
        for i in group[1:]:
            total = total + value[i]
        total = across * total
        for i in group:
            if abs(apart) < 1e-9:
                force[i] = total
            else:
                force[i] = apart * value[i] + total
    return force


def lanes(value, by):
    return pltpu.roll(value, by % value.shape[1], 1)


def rows(value, by):
    return pltpu.roll(value, by % value.shape[0], 0)


def at(j):
    return slice(8 * j, 8 * j + 8)


def stiff(low, high, field, finish, moduli_ref, along_ref, up_ref, free, x_ref, late_ref):
    row = lax.broadcasted_iota(jnp.int32, (8, 128), 0)
    first_row = row == 0
    last_row = row == 7

    def x_modes(n, j):
        held = free(n, j)
        for k, value in enumerate(field(n, j)):
            value = value * held
            beside = lanes(value, -1)
            x_ref[2 * k, at(j), :] = value + beside
            x_ref[2 * k + 1, at(j), :] = beside - value

    def take(j):
        values = [x_ref[q, at(j), :] for q in range(6)]
        return values, [rows(v, -1) for v in values]

    def xy_modes(here, after):
        result = []
        for value, rolled, rolled_after in zip(here[0], here[1], after[1]):
            beside = jnp.where(last_row, rolled_after, rolled)
            result += [value + beside, beside - value]
        return result

    def flush(n, j):
        late = [late_ref[q, at(j), :] for q in range(6)]
        finish(n, j, [late[2 * k] + lanes(late[2 * k + 1], 1) for k in range(3)])

    def layer(n, stage):
        here = take(0)
        carried = [jnp.zeros((8, 128), jnp.float32)] * 6
        zero = jnp.zeros((8, 128), jnp.float32)
        for j in range(8):
            after = take(j + 1) if j < 7 else ([zero] * 6, [zero] * 6)
            now = xy_modes(here, after)
            here = after
            x_modes(jnp.minimum(n + 1, high), j)
            if stage > 2:
                flush(n - 2, j)
            before = [along_ref[q, at(j), :] for q in range(12)]
            for q in range(12):
                along_ref[q, at(j), :] = now[q]
            if stage == 0:
                continue
            weight = moduli_ref[n - 1, at(j), :]
            value = [None] * 24
            for k in range(3):
                for c in range(2):
                    for b in range(2):
                        q = 4 * k + 2 * c + b
                        value[3 * (2 * b + c) + k] = before[q] + now[q]
                        value[3 * (4 + 2 * b + c) + k] = now[q] - before[q]
            force = mode_forces(value, 1.0)
            done = {}
            weighted = []
            for i in range(24):
                f = force[i]
                if f is None:
                    weighted.append(None)
                    continue
                if id(f) not in done:
                    done[id(f)] = weight * f
                weighted.append(done[id(f)])
            totals = []
            for k in range(3):
                for c in range(2):
                    for b in range(2):
                        q = 4 * k + 2 * c + b
                        same = weighted[3 * (2 * b + c) + k]
                        change = weighted[3 * (4 + 2 * b + c) + k]
                        if stage > 1:
                            total = up_ref[q, at(j), :] - change
                            totals.append(total if same is None else total + same)
                        up_ref[q, at(j), :] = change if same is None else same + change
            if stage == 1:
                continue
            for k in range(3):
                parts = []
                for c in range(2):
                    same, change = totals[4 * k + 2 * c], totals[4 * k + 2 * c + 1]
                    over = rows(same + change, 1)
                    parts.append(same - change + jnp.where(first_row, carried[2 * k + c], over))
                    carried[2 * k + c] = over
                late_ref[2 * k, at(j), :] = parts[0] - parts[1]
                late_ref[2 * k + 1, at(j), :] = parts[0] + parts[1]

    for j in range(8):
        x_modes(low - 1, j)
    for stage in range(3):
        layer(low - 1 + stage, stage)

    def step(i, unused):
        layer(low + 2 + 2 * i, 3)
        layer(low + 3 + 2 * i, 3)
        return unused

    pairs = (high - low - 1) // 2
    lax.fori_loop(0, pairs, step, 0)
    if low + 2 + 2 * pairs == high:
        layer(high, 3)
    for j in range(8):
        flush(high - 1, j)


def free_of(keep_ref, tile):
    def free(n, j):
        inside = jnp.where(tile * 8 + n == H, jnp.float32(0.0), jnp.float32(1.0))
        return jnp.maximum(keep_ref[at(j), :], inside)

    return free


def tile_index():
    return lax.axis_index("grp") * lax.axis_size("gz") + lax.axis_index("gz")


def coarse_pattern():
    fine = lax.broadcasted_iota(jnp.int32, (128, 128), 0)
    lane = lax.broadcasted_iota(jnp.int32, (128, 128), 1)
    return jnp.where((fine >> 3) == (lane & 15), 1.0, 0.0).astype(jnp.float32)


def exact_dot(a, b, contract):
    return lax.dot_general(
        a, b, (contract, ((), ())), precision=lax.Precision.HIGHEST,
        preferred_element_type=jnp.float32,
    )


def block_sums(planes):
    count = planes.shape[0] // 64
    summed = exact_dot(planes, coarse_pattern(), ((1,), (0,)))
    row = lax.broadcasted_iota(jnp.int32, (64, 128), 0)
    lane = lax.broadcasted_iota(jnp.int32, (64, 128), 1)
    own = (row >> 3) == (lane >> 4)
    return [
        jnp.sum(jnp.where(own, summed[64 * k : 64 * k + 64], 0.0), axis=0, keepdims=True)
        for k in range(count)
    ]


def send_rows(out_ref, four):
    block = jnp.concatenate(four + four, 0)
    for i in range(out_ref.shape[0] // 8):
        out_ref[at(i), :] = block


def coarse_solve(gathered_ref, coarse_ref, tile, window_ref, solved_ref, spread_ref):
    begin = window_begin(tile)
    window_ref[...] = gathered_ref[pl.ds(pl.multiple_of(4 * begin, 8), 4 * WINDOW), :]
    rhs = [window_ref[pl.ds(k, WINDOW, stride=4), :] for k in range(3)]
    if coarse_ref is None:
        moduli = window_ref[pl.ds(3, WINDOW, stride=4), :]
        row = lax.broadcasted_iota(jnp.int32, (WINDOW, 128), 0)
        moduli = jnp.where(row == WINDOW - 1, 0.0, moduli)
    else:
        moduli = coarse_ref[...]
    summed = moduli + lanes(moduli, 1)
    summed = summed + lanes(summed, 16)
    summed = DIAGONAL * COARSEN * (summed + rows(summed, 1))
    inverse = jnp.where(summed > 0.0, 1.0 / jnp.where(summed > 0.0, summed, 1.0), 0.0)

    def apply(field):
        value = [None] * 24
        for k in range(3):
            near = lanes(field[k], -1)
            for c, along_x in enumerate((field[k] + near, near - field[k])):
                near_y = lanes(along_x, -16)
                for b, along_y in enumerate((along_x + near_y, near_y - along_x)):
                    near_z = rows(along_y, -1)
                    value[3 * (2 * b + c) + k] = along_y + near_z
                    value[3 * (4 + 2 * b + c) + k] = near_z - along_y
        force = [None if f is None else moduli * f for f in mode_forces(value, COARSEN)]
        result = []
        for k in range(3):
            parts_x = []
            for c in range(2):
                parts_y = []
                for b in range(2):
                    same, change = force[3 * (2 * b + c) + k], force[3 * (4 + 2 * b + c) + k]
                    if same is None:
                        parts_y.append(rows(change, 1) - change)
                    else:
                        parts_y.append(same - change + rows(same + change, 1))
                parts_x.append(parts_y[0] - parts_y[1] + lanes(parts_y[0] + parts_y[1], 16))
            result.append(parts_x[0] - parts_x[1] + lanes(parts_x[0] + parts_x[1], 1))
        return result

    bottom = BOUND / 20.0
    center = 0.5 * (BOUND + bottom)
    radius = 0.5 * (BOUND - bottom)
    sigma = center / radius
    rho = 1.0 / sigma
    update = [inverse * (s * (1.0 / center)) for s in rhs]
    correction = update
    remainder = rhs
    for sweep in range(CHEB - 1):
        image = apply(update)
        remainder = [r - a for r, a in zip(remainder, image)]
        rho_next = 1.0 / (2.0 * sigma - rho)
        update = [
            (rho_next * rho) * u + (2.0 * rho_next / radius) * (inverse * r)
            for u, r in zip(update, remainder)
        ]
        correction = [c + u for c, u in zip(correction, update)]
        rho = rho_next
    row = lax.broadcasted_iota(jnp.int32, (8, 128), 0)
    lane = lax.broadcasted_iota(jnp.int32, (8, 128), 1)
    own = row == (lane >> 4)
    for k in range(3):
        solved_ref[WINDOW * k : WINDOW * (k + 1), :] = correction[k]
    blocks = []
    for which in range(3):
        place = jnp.clip(tile - begin + which - 1, 0, WINDOW - 1)
        for k in range(3):
            line = solved_ref[pl.ds(WINDOW * k + place, 1), :]
            blocks.append(jnp.where(own, jnp.broadcast_to(line, (8, 128)), 0.0))
    spread_ref[...] = exact_dot(
        jnp.concatenate(blocks, 0), coarse_pattern(), ((1,), (1,))
    )
    return moduli


def window_begin(tile):
    return 2 * jnp.minimum(jnp.maximum(tile - 7, 0) >> 1, (128 - WINDOW) // 2)


def correction_of(spread_ref):
    def correction(n, j):
        which = jnp.where(n < H, 0, jnp.where(n < H + 8, 1, 2))
        return [
            jnp.broadcast_to(spread_ref[pl.ds((3 * which + k) * 8 + j, 1), :], (8, 128))
            for k in range(3)
        ]

    return correction


def set_up(low, high, load_ref, phases_ref, below_refs, above_refs, table_ref, keep_ref,
           rhs_ref, moduli_ref, inverse_ref, tile):
    row = lax.broadcasted_iota(jnp.int32, (64, 128), 0)
    lane = lax.broadcasted_iota(jnp.int32, (64, 128), 1)
    interior = (row < 63) & (lane < 127)
    table = [table_ref[i] for i in range(4)]

    def label(n):
        if n < -2:
            return below_refs[1][9 + n + 5].astype(jnp.int32)
        if n < 0:
            return below_refs[0][3 + n + 2].astype(jnp.int32)
        if n < 8:
            return phases_ref[n]
        if n < 9:
            return above_refs[0][3].astype(jnp.int32)
        return above_refs[1][9 + n - 9].astype(jnp.int32)

    def load(k, n):
        if n < -1:
            return below_refs[1][3 * k + n + 4]
        if n < 0:
            return below_refs[0][k]
        if n < 8:
            return load_ref[k, n]
        if n < 9:
            return above_refs[0][k]
        return above_refs[1][3 * k + n - 9]

    before = None
    for n in range(low - 1, high):
        depth = tile * 8 + n
        inside = interior & ((depth >= 0) & (depth < 1023))
        labels = label(n)
        value = jnp.zeros((64, 128), jnp.float32)
        for i in range(4):
            value = jnp.where(labels == i, table[i], value)
        value = jnp.where(inside, value, 0.0)
        moduli_ref[n + H] = value
        if n >= low:
            both = before + value
            both = both + rows(both, 1)
            both = DIAGONAL * (both + lanes(both, 1))
            inside = jnp.where(depth == 0, jnp.float32(0.0), jnp.float32(1.0))
            held = jnp.maximum(keep_ref[...], inside)
            both = held * both + 1.0 - held
            exists = (depth >= 0) & (depth < 1024)
            both = jnp.where(exists, both, 1.0)
            inverse_ref[n + H] = jnp.where(exists, 1.0 / both, 0.0)
            for k in range(3):
                rhs_ref[k, n + H] = held * load(k, n)
        before = value


def first_kernel(load_ref, phases_ref, below_ref, above_ref, clamp_ref, table_ref,
                 send_ref,
                 rhs_ref, moduli_ref, inverse_ref, keep_ref,
                 along_ref, up_ref, x_ref, late_ref, sum_ref):
    tile = tile_index()
    keep_ref[...] = 1.0 - clamp_ref[...].astype(jnp.float32)
    set_up(-1, 9, load_ref, phases_ref, (below_ref,), (above_ref,), table_ref, keep_ref,
           rhs_ref, moduli_ref, inverse_ref, tile)
    free = free_of(keep_ref, tile)
    total = moduli_ref[H]
    for n in range(1, 8):
        total = total + moduli_ref[n + H]
    sum_ref[3] = total
    for k in range(3):
        sum_ref[k] = jnp.zeros((64, 128), jnp.float32)

    def first(n, j):
        scaled = OMEGA * inverse_ref[n, at(j), :]
        return [rhs_ref[k, n, at(j), :] * scaled for k in range(3)]

    def finish(n, j, out):
        held = free(n, j) > 0.0
        value = first(n, j)
        for k in range(3):
            image = jnp.where(held, out[k], value[k])
            sum_ref[k, at(j), :] += rhs_ref[k, n, at(j), :] - image

    stiff(5, 13, first, finish, moduli_ref, along_ref, up_ref, free, x_ref, late_ref)
    four = block_sums(sum_ref[...].reshape(256, 128))
    lane = lax.broadcasted_iota(jnp.int32, (1, 128), 1)
    edge = (lane >= 112) | ((lane & 15) == 15) | (lax.rem(tile, GROUP) == GROUP - 1)
    four[3] = jnp.where(edge, 0.0, four[3] * (1.0 / 512.0))
    send_rows(send_ref, four)


def ready_kernel(load_ref, phases_ref, below_ref, above_ref, far_below_ref, far_above_ref,
                 clamp_ref, table_ref,
                 rhs_ref, moduli_ref, inverse_ref, keep_ref):
    keep_ref[...] = 1.0 - clamp_ref[...].astype(jnp.float32)
    set_up(-4, 12, load_ref, phases_ref, (below_ref, far_below_ref),
           (above_ref, far_above_ref), table_ref, keep_ref,
           rhs_ref, moduli_ref, inverse_ref, tile_index())


def middle_kernel(gathered_ref, rhs_ref, moduli_ref, inverse_ref, keep_ref,
                  ahead_ref, image_ref, coarse_ref, send_ref,
                  along_ref, up_ref, x_ref, late_ref, sum_ref, dots_ref, window_ref, solved_ref, spread_ref):
    tile = tile_index()
    free = free_of(keep_ref, tile)
    coarse_ref[...] = coarse_solve(gathered_ref, None, tile, window_ref, solved_ref, spread_ref)
    correction = correction_of(spread_ref)

    def second(n, j):
        scaled = OMEGA * inverse_ref[n, at(j), :]
        held = free(n, j)
        result = []
        for k, coarse_value in enumerate(correction(n, j)):
            value = rhs_ref[k, n, at(j), :] * scaled + held * coarse_value
            result.append(value)
        return result

    def smooth(n, j, out):
        held = free(n, j) > 0.0
        scaled = OMEGA * inverse_ref[n, at(j), :]
        for k, value in enumerate(second(n, j)):
            image = jnp.where(held, out[k], value)
            ahead_ref[k, n, at(j), :] = value + (rhs_ref[k, n, at(j), :] - image) * scaled

    stiff(2, 16, second, smooth, moduli_ref, along_ref, up_ref, free, x_ref, late_ref)

    def ahead(n, j):
        return [ahead_ref[k, n, at(j), :] for k in range(3)]

    def keep_image(n, j, out):
        held = free(n, j) > 0.0
        for k in range(3):
            image_ref[k, n, at(j), :] = jnp.where(
                held, out[k], ahead_ref[k, n, at(j), :]
            )

    stiff(3, 15, ahead, keep_image, moduli_ref, along_ref, up_ref, free, x_ref, late_ref)

    for k in range(3):
        sum_ref[k] = jnp.zeros((64, 128), jnp.float32)
    dots_ref[...] = jnp.zeros_like(dots_ref)

    def first(n, j):
        scaled = OMEGA * inverse_ref[n, at(j), :]
        return [image_ref[k, n, at(j), :] * scaled for k in range(3)]

    def finish(n, j, out):
        held = free(n, j) > 0.0
        value = first(n, j)
        for k in range(3):
            image = image_ref[k, n, at(j), :]
            sum_ref[k, at(j), :] += image - jnp.where(held, out[k], value[k])
            now = ahead_ref[k, n, at(j), :]
            dots_ref[0, k] += now * rhs_ref[k, n, at(j), :]
            dots_ref[1, k] += now * image

    stiff(5, 13, first, finish, moduli_ref, along_ref, up_ref, free, x_ref, late_ref)
    three = block_sums(sum_ref[...].reshape(192, 128))
    lane = lax.broadcasted_iota(jnp.int32, (1, 128), 1)
    gamma = jnp.sum(dots_ref[0])
    energy = jnp.sum(dots_ref[1])
    dots = jnp.where(lane == 0, gamma, jnp.where(lane == 1, energy, 0.0))
    send_rows(send_ref, three + [dots])


def lane_value(line, i):
    lane = lax.broadcasted_iota(jnp.int32, line.shape, 1)
    return jnp.sum(jnp.where(lane == i, line, 0.0))


def last_kernel(gathered_ref, rhs_ref, moduli_ref, inverse_ref, keep_ref, ahead_ref, image_ref,
                coarse_ref,
                next_ref, next_image_ref, scalars_ref, send_ref,
                whole_ref, along_ref, up_ref, x_ref, late_ref, dots_ref, window_ref, solved_ref, spread_ref):
    tile = tile_index()
    free = free_of(keep_ref, tile)
    dots = jnp.sum(gathered_ref[pl.ds(3, 128, stride=4), :], axis=0, keepdims=True)
    scalars_ref[...] = jnp.broadcast_to(dots, (8, 128))
    alpha = lane_value(dots, 0) / lane_value(dots, 1)
    coarse_solve(gathered_ref, coarse_ref, tile, window_ref, solved_ref, spread_ref)
    correction = correction_of(spread_ref)

    def second(n, j):
        scaled = OMEGA * inverse_ref[n, at(j), :]
        held = free(n, j)
        result = []
        for k, coarse_value in enumerate(correction(n, j)):
            value = image_ref[k, n, at(j), :] * scaled + held * coarse_value
            result.append(value)
        return result

    def smooth(n, j, out):
        held = free(n, j) > 0.0
        scaled = OMEGA * inverse_ref[n, at(j), :]
        for k, value in enumerate(second(n, j)):
            image = jnp.where(held, out[k], value)
            value = value + (image_ref[k, n, at(j), :] - image) * scaled
            whole_ref[k, n, at(j), :] = ahead_ref[k, n, at(j), :] - alpha * value

    stiff(4, 14, second, smooth, moduli_ref, along_ref, up_ref, free, x_ref, late_ref)
    dots_ref[...] = jnp.zeros_like(dots_ref)

    def ahead(n, j):
        return [whole_ref[k, n, at(j), :] for k in range(3)]

    def finish(n, j, out):
        held = free(n, j) > 0.0
        for k in range(3):
            value = whole_ref[k, n, at(j), :]
            image = jnp.where(held, out[k], value)
            next_ref[k, n - H, at(j), :] = value
            next_image_ref[k, n - H, at(j), :] = image
            before = image_ref[k, n, at(j), :]
            dots_ref[0, k] += value * (rhs_ref[k, n, at(j), :] - alpha * before)
            dots_ref[1, k] += value * image
            dots_ref[2, k] += value * before

    stiff(5, 13, ahead, finish, moduli_ref, along_ref, up_ref, free, x_ref, late_ref)
    lane = lax.broadcasted_iota(jnp.int32, (8, 128), 1)
    line = jnp.zeros((8, 128), jnp.float32)
    for i in range(3):
        line = jnp.where(lane == i, jnp.sum(dots_ref[i]), line)
    for i in range(16):
        send_ref[at(i), :] = line


def close_kernel(gathered_ref, scalars_ref, rhs_ref, ahead_ref, image_ref, next_ref,
                 next_image_ref, displacement_ref, residual_ref):
    before = scalars_ref[0:1, :]
    gamma, energy = lane_value(before, 0), lane_value(before, 1)
    dots = jnp.sum(gathered_ref[...], axis=0, keepdims=True)
    following, own, cross = (lane_value(dots, i) for i in range(3))
    alpha = gamma / energy
    beta = following / gamma
    alpha_next = following / (own + 2.0 * beta * cross + beta * beta * energy)

    def step(n, unused):
        for k in range(3):
            ahead = ahead_ref[k, n + H]
            image = image_ref[k, n + H]
            direction = next_ref[k, n] + beta * ahead
            displacement_ref[k, n] = alpha * ahead + alpha_next * direction
            residual = rhs_ref[k, n + H] - alpha * image
            residual_ref[k, n] = residual - alpha_next * (next_image_ref[k, n] + beta * image)
        return unused

    lax.fori_loop(0, 8, step, 0)


def call(kernel, outs, scratch, *args, smem=()):
    spaces = [
        pl.BlockSpec(memory_space=pltpu.SMEM if i in smem else pltpu.VMEM)
        for i in range(len(args))
    ]
    return pl.pallas_call(
        kernel,
        out_shape=[jax.ShapeDtypeStruct(s, jnp.float32) for s in outs],
        in_specs=spaces,
        out_specs=[pl.BlockSpec(memory_space=pltpu.VMEM)] * len(outs),
        scratch_shapes=[pltpu.VMEM(s, jnp.float32) for s in scratch],
        compiler_params=pltpu.CompilerParams(vmem_limit_bytes=14 * 2**20),
    )(*args)


def to_all(block):
    count = block.shape[0] // 128
    parts = lax.all_to_all(block.reshape(128, count, 128), BOTH, 0, 0)
    return parts.reshape(block.shape)


def body(load, phases, clamp, phase_moduli):
    size = lax.axis_size(BOTH)
    up = [(i, i + 1) for i in range(size - 1)]
    down = [(i + 1, i) for i in range(size - 1)]

    def pack(load, phases, first, last, first_phase, last_phase=None):
        nodes = load[:, first:last].reshape(3 * (last - first), 64, 128)
        labels = phases[first_phase : last_phase or last].astype(jnp.float32)
        return jnp.concatenate([nodes, labels], 0)

    near_top, near_low = pack(load, phases, 7, 8, 6), pack(load, phases, 0, 1, 0)
    below = lax.ppermute(near_top, BOTH, up)
    above = lax.ppermute(near_low, BOTH, down)
    far_load, far_phases, unused = lax.optimization_barrier((load, phases, (near_top, near_low)))
    far_below = lax.ppermute(pack(far_load, far_phases, 4, 7, 3, 6), BOTH, up)
    far_above = lax.ppermute(pack(far_load, far_phases, 1, 4, 1), BOTH, down)

    plane = (64, 128)
    field = (3, EXT) + plane
    ready = [field, (EXT,) + plane, (EXT,) + plane, plane]
    work = [(12,) + plane, (12,) + plane, (6,) + plane, (6,) + plane]
    (send,) = call(
        first_kernel,
        [(512, 128)],
        ready + work + [(4,) + plane],
        load, phases, below, above, clamp, phase_moduli, smem=(5,),
    )
    gathered = to_all(send)
    rhs, moduli, inverse, keep = call(
        ready_kernel, ready, [],
        load, phases, below, above, far_below, far_above, clamp, phase_moduli, smem=(7,),
    )
    ahead, image, coarse, send = call(
        middle_kernel,
        [field, field, (WINDOW, 128), (512, 128)],
        work + [(3,) + plane, (2, 3, 8, 128), (4 * WINDOW, 128), (3 * WINDOW, 128), (72, 128)],
        gathered, rhs, moduli, inverse, keep,
    )
    gathered = to_all(send)
    own = (3, 8) + plane
    following, following_image, scalars, send = call(
        last_kernel,
        [own, own, (8, 128), (128, 128)],
        [field] + work + [(3, 3, 8, 128), (4 * WINDOW, 128), (3 * WINDOW, 128), (72, 128)],
        gathered, rhs, moduli, inverse, keep, ahead, image, coarse,
    )
    gathered = to_all(send)
    displacement, residual = call(
        close_kernel, [own, own], [],
        gathered, scalars, rhs, ahead, image, following, following_image,
    )
    return displacement, residual


def solution(mesh):
    placed = (P(None, BOTH, None, None), P(BOTH, None, None), P(), P())
    return jax.shard_map(
        body,
        mesh=mesh,
        in_specs=placed,
        out_specs=(P(None, BOTH, None, None), P(None, BOTH, None, None)),
        check_vma=False,
    )
```

```python
import functools
import math

import jax
import jax.numpy as jnp
import numpy as np
from jax import lax
from jax.experimental import pallas as pl
from jax.experimental.pallas import tpu as pltpu
from jax.sharding import PartitionSpec as P

COARSEN = 8
CHEB = 4
BOTH = ("grp", "gz")
GROUP = 32
H = 5
EXT = 17
WINDOW = 16
CORNER_OFFSETS = [(a, b, c) for a in (0, 1) for b in (0, 1) for c in (0, 1)]


def element_matrix():
    poisson = 0.3
    lame_first = poisson / ((1.0 + poisson) * (1.0 - 2.0 * poisson))
    shear = 1.0 / (2.0 * (1.0 + poisson))
    elastic = np.zeros((6, 6))
    elastic[:3, :3] = lame_first
    for axis_one in range(3):
        elastic[axis_one, axis_one] = lame_first + 2.0 * shear
        elastic[axis_one + 3, axis_one + 3] = shear
    points = [0.5 - 0.5 / math.sqrt(3.0), 0.5 + 0.5 / math.sqrt(3.0)]
    pairs = [(0, 1), (1, 2), (0, 2)]
    matrix = np.zeros((24, 24))
    for first_point in points:
        for second_point in points:
            for third_point in points:
                spot = (first_point, second_point, third_point)
                strain = np.zeros((6, 24))
                for corner, offset in enumerate(CORNER_OFFSETS):
                    values = [spot[i] if offset[i] else 1.0 - spot[i] for i in range(3)]
                    slopes = [1.0 if offset[i] else -1.0 for i in range(3)]
                    slants = []
                    for axis_one in range(3):
                        others = [values[i] for i in range(3) if i != axis_one]
                        slants.append(slopes[axis_one] * others[0] * others[1])
                        strain[axis_one, 3 * corner + axis_one] = slants[axis_one]
                    for position, pair in enumerate(pairs):
                        strain[3 + position, 3 * corner + pair[0]] = slants[pair[1]]
                        strain[3 + position, 3 * corner + pair[1]] = slants[pair[0]]
                matrix = matrix + 0.125 * (strain.T @ elastic @ strain)
    return matrix


NUMBERS = element_matrix()
BOUND = float(np.max(np.sum(np.abs(NUMBERS), axis=1) / np.diag(NUMBERS)))
OMEGA = 1.2 / BOUND
DIAGONAL = float(np.mean(np.diag(NUMBERS)))


def mode_matrix():
    haar = np.array([[1.0, 1.0], [-1.0, 1.0]])
    change = np.kron(np.kron(np.kron(haar, haar), haar), np.eye(3))
    return change @ NUMBERS @ change.T / 64.0


def mode_groups():
    modes = mode_matrix()
    near = np.abs(modes) > 1e-9
    left = [i for i in range(24) if near[i].any()]
    groups = []
    while left:
        group = [left[0]]
        for i in group:
            group += [j for j in left if near[i, j] and j not in group]
        groups.append(sorted(group))
        left = [i for i in left if i not in group]
    return modes, groups


MODES, MODE_GROUPS = mode_groups()


def mode_forces(value, scale):
    force = [None] * 24
    for group in MODE_GROUPS:
        diagonal = [float(MODES[i, i]) * scale for i in group]
        if len(group) == 1:
            force[group[0]] = diagonal[0] * value[group[0]]
            continue
        across = float(MODES[group[0], group[1]]) * scale
        apart = diagonal[0] - across
        total = value[group[0]]
        for i in group[1:]:
            total = total + value[i]
        total = across * total
        for i in group:
            if abs(apart) < 1e-9:
                force[i] = total
            else:
                force[i] = apart * value[i] + total
    return force


def lanes(value, by):
    return pltpu.roll(value, by % value.shape[1], 1)


def rows(value, by):
    return pltpu.roll(value, by % value.shape[0], 0)


def at(j):
    return slice(8 * j, 8 * j + 8)


def stiff(low, high, field, finish, moduli_ref, along_ref, up_ref, free, x_ref, late_ref):
    row = lax.broadcasted_iota(jnp.int32, (8, 128), 0)
    first_row = row == 0
    last_row = row == 7

    def x_modes(n, j):
        held = free(n, j)
        for k, value in enumerate(field(n, j)):
            value = value * held
            beside = lanes(value, -1)
            x_ref[2 * k, at(j), :] = value + beside
            x_ref[2 * k + 1, at(j), :] = beside - value

    def take(j):
        values = [x_ref[q, at(j), :] for q in range(6)]
        return values, [rows(v, -1) for v in values]

    def xy_modes(here, after):
        result = []
        for value, rolled, rolled_after in zip(here[0], here[1], after[1]):
            beside = jnp.where(last_row, rolled_after, rolled)
            result += [value + beside, beside - value]
        return result

    def flush(n, j):
        late = [late_ref[q, at(j), :] for q in range(6)]
        finish(n, j, [late[2 * k] + lanes(late[2 * k + 1], 1) for k in range(3)])

    def layer(n, stage):
        here = take(0)
        carried = [jnp.zeros((8, 128), jnp.float32)] * 6
        zero = jnp.zeros((8, 128), jnp.float32)
        for j in range(8):
            after = take(j + 1) if j < 7 else ([zero] * 6, [zero] * 6)
            now = xy_modes(here, after)
            here = after
            x_modes(jnp.minimum(n + 1, high), j)
            if stage > 2:
                flush(n - 2, j)
            before = [along_ref[q, at(j), :] for q in range(12)]
            for q in range(12):
                along_ref[q, at(j), :] = now[q]
            if stage == 0:
                continue
            weight = moduli_ref[n - 1, at(j), :]
            value = [None] * 24
            for k in range(3):
                for c in range(2):
                    for b in range(2):
                        q = 4 * k + 2 * c + b
                        value[3 * (2 * b + c) + k] = before[q] + now[q]
                        value[3 * (4 + 2 * b + c) + k] = now[q] - before[q]
            force = mode_forces(value, 1.0)
            done = {}
            weighted = []
            for i in range(24):
                f = force[i]
                if f is None:
                    weighted.append(None)
                    continue
                if id(f) not in done:
                    done[id(f)] = weight * f
                weighted.append(done[id(f)])
            totals = []
            for k in range(3):
                for c in range(2):
                    for b in range(2):
                        q = 4 * k + 2 * c + b
                        same = weighted[3 * (2 * b + c) + k]
                        change = weighted[3 * (4 + 2 * b + c) + k]
                        if stage > 1:
                            total = up_ref[q, at(j), :] - change
                            totals.append(total if same is None else total + same)
                        up_ref[q, at(j), :] = change if same is None else same + change
            if stage == 1:
                continue
            for k in range(3):
                parts = []
                for c in range(2):
                    same, change = totals[4 * k + 2 * c], totals[4 * k + 2 * c + 1]
                    over = rows(same + change, 1)
                    parts.append(same - change + jnp.where(first_row, carried[2 * k + c], over))
                    carried[2 * k + c] = over
                late_ref[2 * k, at(j), :] = parts[0] - parts[1]
                late_ref[2 * k + 1, at(j), :] = parts[0] + parts[1]

    for j in range(8):
        x_modes(low - 1, j)
    for stage in range(3):
        layer(low - 1 + stage, stage)

    def step(i, unused):
        layer(low + 2 + 2 * i, 3)
        layer(low + 3 + 2 * i, 3)
        return unused

    pairs = (high - low - 1) // 2
    lax.fori_loop(0, pairs, step, 0)
    if low + 2 + 2 * pairs == high:
        layer(high, 3)
    for j in range(8):
        flush(high - 1, j)


def free_of(keep_ref, tile):
    def free(n, j):
        inside = jnp.where(tile * 8 + n == H, jnp.float32(0.0), jnp.float32(1.0))
        return jnp.maximum(keep_ref[at(j), :], inside)

    return free


def tile_index():
    return lax.axis_index("grp") * lax.axis_size("gz") + lax.axis_index("gz")


def coarse_pattern():
    fine = lax.broadcasted_iota(jnp.int32, (128, 128), 0)
    lane = lax.broadcasted_iota(jnp.int32, (128, 128), 1)
    return jnp.where((fine >> 3) == (lane & 15), 1.0, 0.0).astype(jnp.float32)


def exact_dot(a, b, contract):
    return lax.dot_general(
        a, b, (contract, ((), ())), precision=lax.Precision.HIGHEST,
        preferred_element_type=jnp.float32,
    )


def block_sums(planes):
    count = planes.shape[0] // 64
    summed = exact_dot(planes, coarse_pattern(), ((1,), (0,)))
    row = lax.broadcasted_iota(jnp.int32, (64, 128), 0)
    lane = lax.broadcasted_iota(jnp.int32, (64, 128), 1)
    own = (row >> 3) == (lane >> 4)
    return [
        jnp.sum(jnp.where(own, summed[64 * k : 64 * k + 64], 0.0), axis=0, keepdims=True)
        for k in range(count)
    ]


def send_rows(out_ref, four):
    block = jnp.concatenate(four + four, 0)
    for i in range(out_ref.shape[0] // 8):
        out_ref[at(i), :] = block


def coarse_solve(gathered_ref, coarse_ref, tile, window_ref, solved_ref, spread_ref):
    begin = window_begin(tile)
    window_ref[...] = gathered_ref[pl.ds(pl.multiple_of(4 * begin, 8), 4 * WINDOW), :]
    rhs = [window_ref[pl.ds(k, WINDOW, stride=4), :] for k in range(3)]
    if coarse_ref is None:
        moduli = window_ref[pl.ds(3, WINDOW, stride=4), :]
        row = lax.broadcasted_iota(jnp.int32, (WINDOW, 128), 0)
        moduli = jnp.where(row == WINDOW - 1, 0.0, moduli)
    else:
        moduli = coarse_ref[...]
    summed = moduli + lanes(moduli, 1)
    summed = summed + lanes(summed, 16)
    summed = DIAGONAL * COARSEN * (summed + rows(summed, 1))
    inverse = jnp.where(summed > 0.0, 1.0 / jnp.where(summed > 0.0, summed, 1.0), 0.0)

    def apply(field):
        value = [None] * 24
        for k in range(3):
            near = lanes(field[k], -1)
            for c, along_x in enumerate((field[k] + near, near - field[k])):
                near_y = lanes(along_x, -16)
                for b, along_y in enumerate((along_x + near_y, near_y - along_x)):
                    near_z = rows(along_y, -1)
                    value[3 * (2 * b + c) + k] = along_y + near_z
                    value[3 * (4 + 2 * b + c) + k] = near_z - along_y
        force = [None if f is None else moduli * f for f in mode_forces(value, COARSEN)]
        result = []
        for k in range(3):
            parts_x = []
            for c in range(2):
                parts_y = []
                for b in range(2):
                    same, change = force[3 * (2 * b + c) + k], force[3 * (4 + 2 * b + c) + k]
                    if same is None:
                        parts_y.append(rows(change, 1) - change)
                    else:
                        parts_y.append(same - change + rows(same + change, 1))
                parts_x.append(parts_y[0] - parts_y[1] + lanes(parts_y[0] + parts_y[1], 16))
            result.append(parts_x[0] - parts_x[1] + lanes(parts_x[0] + parts_x[1], 1))
        return result

    bottom = BOUND / 20.0
    center = 0.5 * (BOUND + bottom)
    radius = 0.5 * (BOUND - bottom)
    sigma = center / radius
    rho = 1.0 / sigma
    update = [inverse * (s * (1.0 / center)) for s in rhs]
    correction = update
    remainder = rhs
    for sweep in range(CHEB - 1):
        image = apply(update)
        remainder = [r - a for r, a in zip(remainder, image)]
        rho_next = 1.0 / (2.0 * sigma - rho)
        update = [
            (rho_next * rho) * u + (2.0 * rho_next / radius) * (inverse * r)
            for u, r in zip(update, remainder)
        ]
        correction = [c + u for c, u in zip(correction, update)]
        rho = rho_next
    row = lax.broadcasted_iota(jnp.int32, (8, 128), 0)
    lane = lax.broadcasted_iota(jnp.int32, (8, 128), 1)
    own = row == (lane >> 4)
    for k in range(3):
        solved_ref[WINDOW * k : WINDOW * (k + 1), :] = correction[k]
    blocks = []
    for which in range(3):
        place = jnp.clip(tile - begin + which - 1, 0, WINDOW - 1)
        for k in range(3):
            line = solved_ref[pl.ds(WINDOW * k + place, 1), :]
            blocks.append(jnp.where(own, jnp.broadcast_to(line, (8, 128)), 0.0))
    spread_ref[...] = exact_dot(
        jnp.concatenate(blocks, 0), coarse_pattern(), ((1,), (1,))
    )
    return moduli


def window_begin(tile):
    return 2 * jnp.minimum(jnp.maximum(tile - 7, 0) >> 1, (128 - WINDOW) // 2)


def correction_of(spread_ref):
    def correction(n, j):
        which = jnp.where(n < H, 0, jnp.where(n < H + 8, 1, 2))
        return [
            jnp.broadcast_to(spread_ref[pl.ds((3 * which + k) * 8 + j, 1), :], (8, 128))
            for k in range(3)
        ]

    return correction


def pack_kernel(load_ref, phases_ref, table_ref,
                top_ref, low_ref, far_top_ref, far_low_ref, moduli_ref):
    tile = tile_index()
    row = lax.broadcasted_iota(jnp.int32, (64, 128), 0)
    lane = lax.broadcasted_iota(jnp.int32, (64, 128), 1)
    interior = (row < 63) & (lane < 127)
    table = [table_ref[i] for i in range(4)]
    for n in range(8):
        value = jnp.zeros((64, 128), jnp.float32)
        for i in range(4):
            value = jnp.where(phases_ref[n] == i, table[i], value)
        inside = interior if n < 7 else interior & (tile < 127)
        value = jnp.where(inside, value, 0.0)
        moduli_ref[n] = value
        if n >= 6:
            top_ref[3 + n - 6] = value
        elif n >= 3:
            far_top_ref[9 + n - 3] = value
        if n == 0:
            low_ref[3] = value
        elif n < 4:
            far_low_ref[9 + n - 1] = value
        if n == 1:
            low_ref[4] = value
    for k in range(3):
        top_ref[k] = load_ref[k, 7]
        low_ref[k] = load_ref[k, 0]
        for n in range(3):
            far_top_ref[3 * k + n] = load_ref[k, 4 + n]
            far_low_ref[3 * k + n] = load_ref[k, 1 + n]


def set_up(low, high, load_ref, own_ref, below_refs, above_refs, keep_ref,
           rhs_ref, moduli_ref, inverse_ref, tile):
    def moduli(n):
        if n < -2:
            return below_refs[1][9 + n + 5]
        if n < 0:
            return below_refs[0][3 + n + 2]
        if n < 8:
            return own_ref[n]
        if n < 9:
            return above_refs[0][3]
        return above_refs[1][9 + n - 9]

    def load(k, n):
        if n < -1:
            return below_refs[1][3 * k + n + 4]
        if n < 0:
            return below_refs[0][k]
        if n < 8:
            return load_ref[k, n]
        if n < 9:
            return above_refs[0][k]
        return above_refs[1][3 * k + n - 9]

    before = None
    for n in range(low - 1, high):
        depth = tile * 8 + n
        value = moduli(n)
        moduli_ref[n + H] = value
        if n >= low:
            both = before + value
            both = both + rows(both, 1)
            both = DIAGONAL * (both + lanes(both, 1))
            inside = jnp.where(depth == 0, jnp.float32(0.0), jnp.float32(1.0))
            held = jnp.maximum(keep_ref[...], inside)
            both = held * both + 1.0 - held
            exists = (depth >= 0) & (depth < 1024)
            both = jnp.where(exists, both, 1.0)
            inverse_ref[n + H] = jnp.where(exists, 1.0 / both, 0.0)
            for k in range(3):
                rhs_ref[k, n + H] = held * load(k, n)
        before = value


def first_kernel(load_ref, own_ref, below_ref, above_ref, clamp_ref,
                 send_ref,
                 rhs_ref, moduli_ref, inverse_ref, keep_ref,
                 along_ref, up_ref, x_ref, late_ref, sum_ref):
    tile = tile_index()
    keep_ref[...] = 1.0 - clamp_ref[...].astype(jnp.float32)
    set_up(-1, 9, load_ref, own_ref, (below_ref,), (above_ref,), keep_ref,
           rhs_ref, moduli_ref, inverse_ref, tile)
    free = free_of(keep_ref, tile)
    total = moduli_ref[H]
    for n in range(1, 8):
        total = total + moduli_ref[n + H]
    sum_ref[3] = total
    for k in range(3):
        sum_ref[k] = jnp.zeros((64, 128), jnp.float32)

    def first(n, j):
        scaled = OMEGA * inverse_ref[n, at(j), :]
        return [rhs_ref[k, n, at(j), :] * scaled for k in range(3)]

    def finish(n, j, out):
        held = free(n, j) > 0.0
        value = first(n, j)
        for k in range(3):
            image = jnp.where(held, out[k], value[k])
            sum_ref[k, at(j), :] += rhs_ref[k, n, at(j), :] - image

    stiff(5, 13, first, finish, moduli_ref, along_ref, up_ref, free, x_ref, late_ref)
    four = block_sums(sum_ref[...].reshape(256, 128))
    lane = lax.broadcasted_iota(jnp.int32, (1, 128), 1)
    edge = (lane >= 112) | ((lane & 15) == 15) | (lax.rem(tile, GROUP) == GROUP - 1)
    four[3] = jnp.where(edge, 0.0, four[3] * (1.0 / 512.0))
    send_rows(send_ref, four)


def middle_kernel(gathered_ref, load_ref, own_ref, below_ref, above_ref,
                  far_below_ref, far_above_ref, clamp_ref,
                  ahead_ref, image_ref, coarse_ref, send_ref,
                  rhs_ref, moduli_ref, inverse_ref, keep_ref,
                  along_ref, up_ref, x_ref, late_ref,
                  sum_ref, dots_ref, window_ref, solved_ref, spread_ref):
    tile = tile_index()
    keep_ref[...] = 1.0 - clamp_ref[...].astype(jnp.float32)
    set_up(-4, 12, load_ref, own_ref, (below_ref, far_below_ref),
           (above_ref, far_above_ref), keep_ref, rhs_ref, moduli_ref, inverse_ref, tile)
    free = free_of(keep_ref, tile)
    coarse_ref[...] = coarse_solve(gathered_ref, None, tile, window_ref, solved_ref, spread_ref)
    correction = correction_of(spread_ref)

    def second(n, j):
        scaled = OMEGA * inverse_ref[n, at(j), :]
        held = free(n, j)
        result = []
        for k, coarse_value in enumerate(correction(n, j)):
            value = rhs_ref[k, n, at(j), :] * scaled + held * coarse_value
            result.append(value)
        return result

    def smooth(n, j, out):
        held = free(n, j) > 0.0
        scaled = OMEGA * inverse_ref[n, at(j), :]
        for k, value in enumerate(second(n, j)):
            image = jnp.where(held, out[k], value)
            ahead_ref[k, n, at(j), :] = value + (rhs_ref[k, n, at(j), :] - image) * scaled

    stiff(2, 16, second, smooth, moduli_ref, along_ref, up_ref, free, x_ref, late_ref)

    def ahead(n, j):
        return [ahead_ref[k, n, at(j), :] for k in range(3)]

    def keep_image(n, j, out):
        held = free(n, j) > 0.0
        for k in range(3):
            image_ref[k, n, at(j), :] = jnp.where(
                held, out[k], ahead_ref[k, n, at(j), :]
            )

    stiff(3, 15, ahead, keep_image, moduli_ref, along_ref, up_ref, free, x_ref, late_ref)

    for k in range(3):
        sum_ref[k] = jnp.zeros((64, 128), jnp.float32)
    dots_ref[...] = jnp.zeros_like(dots_ref)

    def first(n, j):
        scaled = OMEGA * inverse_ref[n, at(j), :]
        return [image_ref[k, n, at(j), :] * scaled for k in range(3)]

    def finish(n, j, out):
        held = free(n, j) > 0.0
        value = first(n, j)
        for k in range(3):
            image = image_ref[k, n, at(j), :]
            sum_ref[k, at(j), :] += image - jnp.where(held, out[k], value[k])
            now = ahead_ref[k, n, at(j), :]
            dots_ref[0, k] += now * rhs_ref[k, n, at(j), :]
            dots_ref[1, k] += now * image

    stiff(5, 13, first, finish, moduli_ref, along_ref, up_ref, free, x_ref, late_ref)
    three = block_sums(sum_ref[...].reshape(192, 128))
    lane = lax.broadcasted_iota(jnp.int32, (1, 128), 1)
    gamma = jnp.sum(dots_ref[0])
    energy = jnp.sum(dots_ref[1])
    dots = jnp.where(lane == 0, gamma, jnp.where(lane == 1, energy, 0.0))
    send_rows(send_ref, three + [dots])


def lane_value(line, i):
    lane = lax.broadcasted_iota(jnp.int32, line.shape, 1)
    return jnp.sum(jnp.where(lane == i, line, 0.0))


def last_kernel(gathered_ref, rhs_ref, moduli_ref, inverse_ref, keep_ref, ahead_ref, image_ref,
                coarse_ref,
                next_ref, next_image_ref, scalars_ref, send_ref,
                whole_ref, along_ref, up_ref, x_ref, late_ref, dots_ref, window_ref, solved_ref, spread_ref):
    tile = tile_index()
    free = free_of(keep_ref, tile)
    dots = jnp.sum(gathered_ref[pl.ds(3, 128, stride=4), :], axis=0, keepdims=True)
    scalars_ref[...] = jnp.broadcast_to(dots, (8, 128))
    alpha = lane_value(dots, 0) / lane_value(dots, 1)
    coarse_solve(gathered_ref, coarse_ref, tile, window_ref, solved_ref, spread_ref)
    correction = correction_of(spread_ref)

    def second(n, j):
        scaled = OMEGA * inverse_ref[n, at(j), :]
        held = free(n, j)
        result = []
        for k, coarse_value in enumerate(correction(n, j)):
            value = image_ref[k, n, at(j), :] * scaled + held * coarse_value
            result.append(value)
        return result

    def smooth(n, j, out):
        held = free(n, j) > 0.0
        scaled = OMEGA * inverse_ref[n, at(j), :]
        for k, value in enumerate(second(n, j)):
            image = jnp.where(held, out[k], value)
            value = value + (image_ref[k, n, at(j), :] - image) * scaled
            whole_ref[k, n, at(j), :] = ahead_ref[k, n, at(j), :] - alpha * value

    stiff(4, 14, second, smooth, moduli_ref, along_ref, up_ref, free, x_ref, late_ref)
    dots_ref[...] = jnp.zeros_like(dots_ref)

    def ahead(n, j):
        return [whole_ref[k, n, at(j), :] for k in range(3)]

    def finish(n, j, out):
        held = free(n, j) > 0.0
        for k in range(3):
            value = whole_ref[k, n, at(j), :]
            image = jnp.where(held, out[k], value)
            next_ref[k, n - H, at(j), :] = value
            next_image_ref[k, n - H, at(j), :] = image
            before = image_ref[k, n, at(j), :]
            dots_ref[0, k] += value * (rhs_ref[k, n, at(j), :] - alpha * before)
            dots_ref[1, k] += value * image
            dots_ref[2, k] += value * before

    stiff(5, 13, ahead, finish, moduli_ref, along_ref, up_ref, free, x_ref, late_ref)
    lane = lax.broadcasted_iota(jnp.int32, (8, 128), 1)
    line = jnp.zeros((8, 128), jnp.float32)
    for i in range(3):
        line = jnp.where(lane == i, jnp.sum(dots_ref[i]), line)
    for i in range(16):
        send_ref[at(i), :] = line


def close_kernel(gathered_ref, scalars_ref, rhs_ref, ahead_ref, image_ref, next_ref,
                 next_image_ref, displacement_ref, residual_ref):
    before = scalars_ref[0:1, :]
    gamma, energy = lane_value(before, 0), lane_value(before, 1)
    dots = jnp.sum(gathered_ref[...], axis=0, keepdims=True)
    following, own, cross = (lane_value(dots, i) for i in range(3))
    alpha = gamma / energy
    beta = following / gamma
    alpha_next = following / (own + 2.0 * beta * cross + beta * beta * energy)

    def step(n, unused):
        for k in range(3):
            ahead = ahead_ref[k, n + H]
            image = image_ref[k, n + H]
            direction = next_ref[k, n] + beta * ahead
            displacement_ref[k, n] = alpha * ahead + alpha_next * direction
            residual = rhs_ref[k, n + H] - alpha * image
            residual_ref[k, n] = residual - alpha_next * (next_image_ref[k, n] + beta * image)
        return unused

    lax.fori_loop(0, 8, step, 0)


def call(kernel, outs, scratch, *args, smem=()):
    spaces = [
        pl.BlockSpec(memory_space=pltpu.SMEM if i in smem else pltpu.VMEM)
        for i in range(len(args))
    ]
    return pl.pallas_call(
        kernel,
        out_shape=[jax.ShapeDtypeStruct(s, jnp.float32) for s in outs],
        in_specs=spaces,
        out_specs=[pl.BlockSpec(memory_space=pltpu.VMEM)] * len(outs),
        scratch_shapes=[pltpu.VMEM(s, jnp.float32) for s in scratch],
        compiler_params=pltpu.CompilerParams(vmem_limit_bytes=14 * 2**20),
    )(*args)


def to_all(block):
    count = block.shape[0] // 128
    parts = lax.all_to_all(block.reshape(128, count, 128), BOTH, 0, 0)
    return parts.reshape(block.shape)


def body(load, phases, clamp, phase_moduli):
    size = lax.axis_size(BOTH)
    up = [(i, i + 1) for i in range(size - 1)]
    down = [(i + 1, i) for i in range(size - 1)]

    plane = (64, 128)
    field = (3, EXT) + plane
    ready = [field, (EXT,) + plane, (EXT,) + plane, plane]
    work = [(12,) + plane, (12,) + plane, (6,) + plane, (6,) + plane]
    top, low, far_top, far_low, moduli_own = call(
        pack_kernel,
        [(5,) + plane, (5,) + plane, (12,) + plane, (12,) + plane, (8,) + plane], [],
        load, phases, phase_moduli, smem=(2,),
    )
    below = lax.ppermute(top, BOTH, up)
    above = lax.ppermute(low, BOTH, down)
    far_below = lax.ppermute(far_top, BOTH, up)
    far_above = lax.ppermute(far_low, BOTH, down)
    (send,) = call(
        first_kernel, [(512, 128)], ready + work + [(4,) + plane],
        load, moduli_own, below, above, clamp,
    )
    gathered = to_all(send)
    ahead, image, coarse, send, rhs, moduli, inverse, keep = call(
        middle_kernel,
        [field, field, (WINDOW, 128), (512, 128)] + ready,
        work + [(3,) + plane, (2, 3, 8, 128), (4 * WINDOW, 128), (3 * WINDOW, 128), (72, 128)],
        gathered, load, moduli_own, below, above, far_below, far_above, clamp,
    )
    gathered = to_all(send)
    own = (3, 8) + plane
    following, following_image, scalars, send = call(
        last_kernel,
        [own, own, (8, 128), (128, 128)],
        [field] + work + [(3, 3, 8, 128), (4 * WINDOW, 128), (3 * WINDOW, 128), (72, 128)],
        gathered, rhs, moduli, inverse, keep, ahead, image, coarse,
    )
    gathered = to_all(send)
    displacement, residual = call(
        close_kernel, [own, own], [],
        gathered, scalars, rhs, ahead, image, following, following_image,
    )
    return displacement, residual


def solution(mesh):
    placed = (P(None, BOTH, None, None), P(BOTH, None, None), P(), P())
    return jax.shard_map(
        body,
        mesh=mesh,
        in_specs=placed,
        out_specs=(P(None, BOTH, None, None), P(None, BOTH, None, None)),
        check_vma=False,
    )
```

```python
import functools
import math

import jax
import jax.numpy as jnp
import numpy as np
from jax import lax
from jax.experimental import pallas as pl
from jax.experimental.pallas import tpu as pltpu
from jax.sharding import PartitionSpec as P

COARSEN = 8
CHEB = 4
BOTH = ("grp", "gz")
GROUP = 32
H = 5
EXT = 17
WINDOW = 16
CORNER_OFFSETS = [(a, b, c) for a in (0, 1) for b in (0, 1) for c in (0, 1)]


def element_matrix():
    poisson = 0.3
    lame_first = poisson / ((1.0 + poisson) * (1.0 - 2.0 * poisson))
    shear = 1.0 / (2.0 * (1.0 + poisson))
    elastic = np.zeros((6, 6))
    elastic[:3, :3] = lame_first
    for axis_one in range(3):
        elastic[axis_one, axis_one] = lame_first + 2.0 * shear
        elastic[axis_one + 3, axis_one + 3] = shear
    points = [0.5 - 0.5 / math.sqrt(3.0), 0.5 + 0.5 / math.sqrt(3.0)]
    pairs = [(0, 1), (1, 2), (0, 2)]
    matrix = np.zeros((24, 24))
    for first_point in points:
        for second_point in points:
            for third_point in points:
                spot = (first_point, second_point, third_point)
                strain = np.zeros((6, 24))
                for corner, offset in enumerate(CORNER_OFFSETS):
                    values = [spot[i] if offset[i] else 1.0 - spot[i] for i in range(3)]
                    slopes = [1.0 if offset[i] else -1.0 for i in range(3)]
                    slants = []
                    for axis_one in range(3):
                        others = [values[i] for i in range(3) if i != axis_one]
                        slants.append(slopes[axis_one] * others[0] * others[1])
                        strain[axis_one, 3 * corner + axis_one] = slants[axis_one]
                    for position, pair in enumerate(pairs):
                        strain[3 + position, 3 * corner + pair[0]] = slants[pair[1]]
                        strain[3 + position, 3 * corner + pair[1]] = slants[pair[0]]
                matrix = matrix + 0.125 * (strain.T @ elastic @ strain)
    return matrix


NUMBERS = element_matrix()
BOUND = float(np.max(np.sum(np.abs(NUMBERS), axis=1) / np.diag(NUMBERS)))
OMEGA = 1.2 / BOUND
DIAGONAL = float(np.mean(np.diag(NUMBERS)))


def mode_matrix():
    haar = np.array([[1.0, 1.0], [-1.0, 1.0]])
    change = np.kron(np.kron(np.kron(haar, haar), haar), np.eye(3))
    return change @ NUMBERS @ change.T / 64.0


def mode_groups():
    modes = mode_matrix()
    near = np.abs(modes) > 1e-9
    left = [i for i in range(24) if near[i].any()]
    groups = []
    while left:
        group = [left[0]]
        for i in group:
            group += [j for j in left if near[i, j] and j not in group]
        groups.append(sorted(group))
        left = [i for i in left if i not in group]
    return modes, groups


MODES, MODE_GROUPS = mode_groups()


def mode_forces(value, scale):
    force = [None] * 24
    for group in MODE_GROUPS:
        diagonal = [float(MODES[i, i]) * scale for i in group]
        if len(group) == 1:
            force[group[0]] = diagonal[0] * value[group[0]]
            continue
        across = float(MODES[group[0], group[1]]) * scale
        apart = diagonal[0] - across
        total = value[group[0]]
        for i in group[1:]:
            total = total + value[i]
        total = across * total
        for i in group:
            if abs(apart) < 1e-9:
                force[i] = total
            else:
                force[i] = apart * value[i] + total
    return force


def lanes(value, by):
    return pltpu.roll(value, by % value.shape[1], 1)


def rows(value, by):
    return pltpu.roll(value, by % value.shape[0], 0)


def at(j):
    return slice(8 * j, 8 * j + 8)


def stiff(low, high, field, finish, moduli_ref, along_ref, up_ref, free, x_ref, late_ref):
    row = lax.broadcasted_iota(jnp.int32, (8, 128), 0)
    first_row = row == 0
    last_row = row == 7

    def x_modes(n, j):
        held = free(n, j)
        for k, value in enumerate(field(n, j)):
            value = value * held
            beside = lanes(value, -1)
            x_ref[2 * k, at(j), :] = value + beside
            x_ref[2 * k + 1, at(j), :] = beside - value

    def take(j):
        values = [x_ref[q, at(j), :] for q in range(6)]
        return values, [rows(v, -1) for v in values]

    def xy_modes(here, after):
        result = []
        for value, rolled, rolled_after in zip(here[0], here[1], after[1]):
            beside = jnp.where(last_row, rolled_after, rolled)
            result += [value + beside, beside - value]
        return result

    def flush(n, j):
        late = [late_ref[q, at(j), :] for q in range(6)]
        finish(n, j, [late[2 * k] + lanes(late[2 * k + 1], 1) for k in range(3)])

    def layer(n, stage):
        here = take(0)
        carried = [jnp.zeros((8, 128), jnp.float32)] * 6
        zero = jnp.zeros((8, 128), jnp.float32)
        for j in range(8):
            after = take(j + 1) if j < 7 else ([zero] * 6, [zero] * 6)
            now = xy_modes(here, after)
            here = after
            x_modes(jnp.minimum(n + 1, high), j)
            if stage > 2:
                flush(n - 2, j)
            before = [along_ref[q, at(j), :] for q in range(12)]
            for q in range(12):
                along_ref[q, at(j), :] = now[q]
            if stage == 0:
                continue
            weight = moduli_ref[n - 1, at(j), :]
            value = [None] * 24
            for k in range(3):
                for c in range(2):
                    for b in range(2):
                        q = 4 * k + 2 * c + b
                        value[3 * (2 * b + c) + k] = before[q] + now[q]
                        value[3 * (4 + 2 * b + c) + k] = now[q] - before[q]
            force = mode_forces(value, 1.0)
            done = {}
            weighted = []
            for i in range(24):
                f = force[i]
                if f is None:
                    weighted.append(None)
                    continue
                if id(f) not in done:
                    done[id(f)] = weight * f
                weighted.append(done[id(f)])
            totals = []
            for k in range(3):
                for c in range(2):
                    for b in range(2):
                        q = 4 * k + 2 * c + b
                        same = weighted[3 * (2 * b + c) + k]
                        change = weighted[3 * (4 + 2 * b + c) + k]
                        if stage > 1:
                            total = up_ref[q, at(j), :] - change
                            totals.append(total if same is None else total + same)
                        up_ref[q, at(j), :] = change if same is None else same + change
            if stage == 1:
                continue
            for k in range(3):
                parts = []
                for c in range(2):
                    same, change = totals[4 * k + 2 * c], totals[4 * k + 2 * c + 1]
                    over = rows(same + change, 1)
                    parts.append(same - change + jnp.where(first_row, carried[2 * k + c], over))
                    carried[2 * k + c] = over
                late_ref[2 * k, at(j), :] = parts[0] - parts[1]
                late_ref[2 * k + 1, at(j), :] = parts[0] + parts[1]

    for j in range(8):
        x_modes(low - 1, j)
    for stage in range(3):
        layer(low - 1 + stage, stage)

    def step(i, unused):
        layer(low + 2 + 2 * i, 3)
        layer(low + 3 + 2 * i, 3)
        return unused

    pairs = (high - low - 1) // 2
    lax.fori_loop(0, pairs, step, 0)
    if low + 2 + 2 * pairs == high:
        layer(high, 3)
    for j in range(8):
        flush(high - 1, j)


def free_of(keep_ref, tile):
    def free(n, j):
        inside = jnp.where(tile * 8 + n == H, jnp.float32(0.0), jnp.float32(1.0))
        return jnp.maximum(keep_ref[at(j), :], inside)

    return free


def tile_index():
    return lax.axis_index("grp") * lax.axis_size("gz") + lax.axis_index("gz")


def coarse_pattern():
    fine = lax.broadcasted_iota(jnp.int32, (128, 128), 0)
    lane = lax.broadcasted_iota(jnp.int32, (128, 128), 1)
    return jnp.where((fine >> 3) == (lane & 15), 1.0, 0.0).astype(jnp.float32)


def exact_dot(a, b, contract):
    return lax.dot_general(
        a, b, (contract, ((), ())), precision=lax.Precision.HIGHEST,
        preferred_element_type=jnp.float32,
    )


def block_sums(planes):
    count = planes.shape[0] // 64
    summed = exact_dot(planes, coarse_pattern(), ((1,), (0,)))
    row = lax.broadcasted_iota(jnp.int32, (64, 128), 0)
    lane = lax.broadcasted_iota(jnp.int32, (64, 128), 1)
    own = (row >> 3) == (lane >> 4)
    return [
        jnp.sum(jnp.where(own, summed[64 * k : 64 * k + 64], 0.0), axis=0, keepdims=True)
        for k in range(count)
    ]


def send_rows(out_ref, four):
    block = jnp.concatenate(four + four, 0)
    for i in range(out_ref.shape[0] // 8):
        out_ref[at(i), :] = block


def coarse_solve(gathered_ref, coarse_ref, tile, window_ref, solved_ref, spread_ref):
    begin = window_begin(tile)
    window_ref[...] = gathered_ref[pl.ds(pl.multiple_of(4 * begin, 8), 4 * WINDOW), :]
    rhs = [window_ref[pl.ds(k, WINDOW, stride=4), :] for k in range(3)]
    if coarse_ref is None:
        moduli = window_ref[pl.ds(3, WINDOW, stride=4), :]
        row = lax.broadcasted_iota(jnp.int32, (WINDOW, 128), 0)
        moduli = jnp.where(row == WINDOW - 1, 0.0, moduli)
    else:
        moduli = coarse_ref[...]
    summed = moduli + lanes(moduli, 1)
    summed = summed + lanes(summed, 16)
    summed = DIAGONAL * COARSEN * (summed + rows(summed, 1))
    inverse = jnp.where(summed > 0.0, 1.0 / jnp.where(summed > 0.0, summed, 1.0), 0.0)

    def apply(field):
        value = [None] * 24
        for k in range(3):
            near = lanes(field[k], -1)
            for c, along_x in enumerate((field[k] + near, near - field[k])):
                near_y = lanes(along_x, -16)
                for b, along_y in enumerate((along_x + near_y, near_y - along_x)):
                    near_z = rows(along_y, -1)
                    value[3 * (2 * b + c) + k] = along_y + near_z
                    value[3 * (4 + 2 * b + c) + k] = near_z - along_y
        force = [None if f is None else moduli * f for f in mode_forces(value, COARSEN)]
        result = []
        for k in range(3):
            parts_x = []
            for c in range(2):
                parts_y = []
                for b in range(2):
                    same, change = force[3 * (2 * b + c) + k], force[3 * (4 + 2 * b + c) + k]
                    if same is None:
                        parts_y.append(rows(change, 1) - change)
                    else:
                        parts_y.append(same - change + rows(same + change, 1))
                parts_x.append(parts_y[0] - parts_y[1] + lanes(parts_y[0] + parts_y[1], 16))
            result.append(parts_x[0] - parts_x[1] + lanes(parts_x[0] + parts_x[1], 1))
        return result

    bottom = BOUND / 20.0
    center = 0.5 * (BOUND + bottom)
    radius = 0.5 * (BOUND - bottom)
    sigma = center / radius
    rho = 1.0 / sigma
    update = [inverse * (s * (1.0 / center)) for s in rhs]
    correction = update
    remainder = rhs
    for sweep in range(CHEB - 1):
        image = apply(update)
        remainder = [r - a for r, a in zip(remainder, image)]
        rho_next = 1.0 / (2.0 * sigma - rho)
        update = [
            (rho_next * rho) * u + (2.0 * rho_next / radius) * (inverse * r)
            for u, r in zip(update, remainder)
        ]
        correction = [c + u for c, u in zip(correction, update)]
        rho = rho_next
    row = lax.broadcasted_iota(jnp.int32, (8, 128), 0)
    lane = lax.broadcasted_iota(jnp.int32, (8, 128), 1)
    own = row == (lane >> 4)
    for k in range(3):
        solved_ref[WINDOW * k : WINDOW * (k + 1), :] = correction[k]
    blocks = []
    for which in range(3):
        place = jnp.clip(tile - begin + which - 1, 0, WINDOW - 1)
        for k in range(3):
            line = solved_ref[pl.ds(WINDOW * k + place, 1), :]
            blocks.append(jnp.where(own, jnp.broadcast_to(line, (8, 128)), 0.0))
    spread_ref[...] = exact_dot(
        jnp.concatenate(blocks, 0), coarse_pattern(), ((1,), (1,))
    )
    return moduli


def window_begin(tile):
    return 2 * jnp.minimum(jnp.maximum(tile - 7, 0) >> 1, (128 - WINDOW) // 2)


def correction_of(spread_ref):
    def correction(n, j):
        which = jnp.where(n < H, 0, jnp.where(n < H + 8, 1, 2))
        return [
            jnp.broadcast_to(spread_ref[pl.ds((3 * which + k) * 8 + j, 1), :], (8, 128))
            for k in range(3)
        ]

    return correction


def pack_kernel(load_hbm, phases_hbm, table_ref,
                chip_ref, link_ref, moduli_ref,
                load_ref, phases_ref, arrived):
    fetch_phases = pltpu.make_async_copy(phases_hbm, phases_ref, arrived.at[0])
    fetch_load = pltpu.make_async_copy(load_hbm, load_ref, arrived.at[1])
    fetch_phases.start()
    fetch_load.start()
    tile = tile_index()
    row = lax.broadcasted_iota(jnp.int32, (64, 128), 0)
    lane = lax.broadcasted_iota(jnp.int32, (64, 128), 1)
    interior = (row < 63) & (lane < 127)
    table = [table_ref[i] for i in range(4)]
    fetch_phases.wait()
    for n in range(8):
        value = jnp.zeros((64, 128), jnp.float32)
        for i in range(4):
            value = jnp.where(phases_ref[n] == i, table[i], value)
        inside = interior if n < 7 else interior & (tile < 127)
        moduli_ref[n] = jnp.where(inside, value, 0.0)
    fetch_load.wait()

    def fill(top_ref, low_ref):
        for k in range(3):
            top_ref[k] = load_ref[k, 7]
            low_ref[k] = load_ref[k, 0]
            for n in range(3):
                top_ref[5 + 3 * k + n] = load_ref[k, 4 + n]
                low_ref[5 + 3 * k + n] = load_ref[k, 1 + n]
        for n in range(2):
            top_ref[3 + n] = moduli_ref[6 + n]
            low_ref[3 + n] = moduli_ref[n]
        for n in range(3):
            top_ref[14 + n] = moduli_ref[3 + n]
            low_ref[14 + n] = moduli_ref[1 + n]

    @pl.when((tile & 1) == 0)
    def even():
        fill(chip_ref, link_ref)

    @pl.when((tile & 1) == 1)
    def odd():
        fill(link_ref, chip_ref)


def own_kernel(load_ref, own_ref, clamp_ref, rhs_ref, moduli_ref, keep_ref):
    keep_ref[...] = 1.0 - clamp_ref[...].astype(jnp.float32)
    moduli_ref[...] = own_ref[...]
    for k in range(3):
        rhs_ref[k] = load_ref[k]
        held = jnp.where(tile_index() == 0, keep_ref[...], 1.0)
        rhs_ref[k, 0] = held * load_ref[k, 0]


def set_up(low, high, load_ref, own_ref, chip_ref, link_ref, keep_ref,
           rhs_ref, moduli_ref, inverse_ref, tile):
    even = (tile & 1) == 0

    def below(i):
        return jnp.where(even, link_ref[i], chip_ref[i])

    def above(i):
        return jnp.where(even, chip_ref[i], link_ref[i])

    def moduli(n):
        if n < -2:
            return below(14 + n + 5)
        if n < 0:
            return below(3 + n + 2)
        if n < 8:
            return own_ref[n]
        if n < 9:
            return above(3)
        return above(14 + n - 9)

    def load(k, n):
        if n < -1:
            return below(5 + 3 * k + n + 4)
        if n < 0:
            return below(k)
        if n < 8:
            return load_ref[k, n]
        if n < 9:
            return above(k)
        return above(5 + 3 * k + n - 9)

    before = None
    for n in range(low - 1, high):
        depth = tile * 8 + n
        value = moduli(n)
        moduli_ref[n + H] = value
        if n >= low:
            both = before + value
            both = both + rows(both, 1)
            both = DIAGONAL * (both + lanes(both, 1))
            inside = jnp.where(depth == 0, jnp.float32(0.0), jnp.float32(1.0))
            held = jnp.maximum(keep_ref[...], inside)
            both = held * both + 1.0 - held
            exists = (depth >= 0) & (depth < 1024)
            both = jnp.where(exists, both, 1.0)
            inverse_ref[n + H] = jnp.where(exists, 1.0 / both, 0.0)
            for k in range(3):
                rhs_ref[k, n + H] = held * load(k, n)
        before = value


def first_kernel(link_ref, chip_ref, load_ref, own_ref, keep_ref,
                 send_ref,
                 rhs_ref, moduli_ref, inverse_ref,
                 along_ref, up_ref, x_ref, late_ref, sum_ref):
    tile = tile_index()
    set_up(-1, 9, load_ref, own_ref, chip_ref, link_ref, keep_ref,
           rhs_ref, moduli_ref, inverse_ref, tile)
    free = free_of(keep_ref, tile)
    total = moduli_ref[H]
    for n in range(1, 8):
        total = total + moduli_ref[n + H]
    sum_ref[3] = total
    for k in range(3):
        sum_ref[k] = jnp.zeros((64, 128), jnp.float32)

    def first(n, j):
        scaled = OMEGA * inverse_ref[n, at(j), :]
        return [rhs_ref[k, n, at(j), :] * scaled for k in range(3)]

    def finish(n, j, out):
        held = free(n, j) > 0.0
        value = first(n, j)
        for k in range(3):
            image = jnp.where(held, out[k], value[k])
            sum_ref[k, at(j), :] += rhs_ref[k, n, at(j), :] - image

    stiff(5, 13, first, finish, moduli_ref, along_ref, up_ref, free, x_ref, late_ref)
    four = block_sums(sum_ref[...].reshape(256, 128))
    lane = lax.broadcasted_iota(jnp.int32, (1, 128), 1)
    edge = (lane >= 112) | ((lane & 15) == 15) | (lax.rem(tile, GROUP) == GROUP - 1)
    four[3] = jnp.where(edge, 0.0, four[3] * (1.0 / 512.0))
    send_rows(send_ref, four)


def middle_kernel(gathered_ref, link_ref, chip_ref, load_ref, own_ref, keep_ref,
                  ahead_ref, image_ref, coarse_ref, send_ref,
                  rhs_ref, moduli_ref, inverse_ref,
                  along_ref, up_ref, x_ref, late_ref,
                  sum_ref, dots_ref, window_ref, solved_ref, spread_ref):
    tile = tile_index()
    set_up(-4, 12, load_ref, own_ref, chip_ref, link_ref, keep_ref,
           rhs_ref, moduli_ref, inverse_ref, tile)
    free = free_of(keep_ref, tile)
    coarse_ref[...] = coarse_solve(gathered_ref, None, tile, window_ref, solved_ref, spread_ref)
    correction = correction_of(spread_ref)

    def second(n, j):
        scaled = OMEGA * inverse_ref[n, at(j), :]
        held = free(n, j)
        result = []
        for k, coarse_value in enumerate(correction(n, j)):
            value = rhs_ref[k, n, at(j), :] * scaled + held * coarse_value
            result.append(value)
        return result

    def smooth(n, j, out):
        held = free(n, j) > 0.0
        scaled = OMEGA * inverse_ref[n, at(j), :]
        for k, value in enumerate(second(n, j)):
            image = jnp.where(held, out[k], value)
            ahead_ref[k, n, at(j), :] = value + (rhs_ref[k, n, at(j), :] - image) * scaled

    stiff(2, 16, second, smooth, moduli_ref, along_ref, up_ref, free, x_ref, late_ref)

    def ahead(n, j):
        return [ahead_ref[k, n, at(j), :] for k in range(3)]

    def keep_image(n, j, out):
        held = free(n, j) > 0.0
        for k in range(3):
            image_ref[k, n, at(j), :] = jnp.where(
                held, out[k], ahead_ref[k, n, at(j), :]
            )

    stiff(3, 15, ahead, keep_image, moduli_ref, along_ref, up_ref, free, x_ref, late_ref)

    for k in range(3):
        sum_ref[k] = jnp.zeros((64, 128), jnp.float32)
    dots_ref[...] = jnp.zeros_like(dots_ref)

    def first(n, j):
        scaled = OMEGA * inverse_ref[n, at(j), :]
        return [image_ref[k, n, at(j), :] * scaled for k in range(3)]

    def finish(n, j, out):
        held = free(n, j) > 0.0
        value = first(n, j)
        for k in range(3):
            image = image_ref[k, n, at(j), :]
            sum_ref[k, at(j), :] += image - jnp.where(held, out[k], value[k])
            now = ahead_ref[k, n, at(j), :]
            dots_ref[0, k] += now * rhs_ref[k, n, at(j), :]
            dots_ref[1, k] += now * image

    stiff(5, 13, first, finish, moduli_ref, along_ref, up_ref, free, x_ref, late_ref)
    three = block_sums(sum_ref[...].reshape(192, 128))
    lane = lax.broadcasted_iota(jnp.int32, (1, 128), 1)
    gamma = jnp.sum(dots_ref[0])
    energy = jnp.sum(dots_ref[1])
    dots = jnp.where(lane == 0, gamma, jnp.where(lane == 1, energy, 0.0))
    send_rows(send_ref, three + [dots])


def lane_value(line, i):
    lane = lax.broadcasted_iota(jnp.int32, line.shape, 1)
    return jnp.sum(jnp.where(lane == i, line, 0.0))


def last_kernel(gathered_ref, rhs_ref, moduli_ref, inverse_ref, keep_ref, ahead_ref, image_ref,
                coarse_ref,
                next_ref, next_image_ref, scalars_ref, send_ref,
                whole_ref, along_ref, up_ref, x_ref, late_ref, dots_ref, window_ref, solved_ref, spread_ref):
    tile = tile_index()
    free = free_of(keep_ref, tile)
    dots = jnp.sum(gathered_ref[pl.ds(3, 128, stride=4), :], axis=0, keepdims=True)
    scalars_ref[...] = jnp.broadcast_to(dots, (8, 128))
    alpha = lane_value(dots, 0) / lane_value(dots, 1)
    coarse_solve(gathered_ref, coarse_ref, tile, window_ref, solved_ref, spread_ref)
    correction = correction_of(spread_ref)

    def second(n, j):
        scaled = OMEGA * inverse_ref[n, at(j), :]
        held = free(n, j)
        result = []
        for k, coarse_value in enumerate(correction(n, j)):
            value = image_ref[k, n, at(j), :] * scaled + held * coarse_value
            result.append(value)
        return result

    def smooth(n, j, out):
        held = free(n, j) > 0.0
        scaled = OMEGA * inverse_ref[n, at(j), :]
        for k, value in enumerate(second(n, j)):
            image = jnp.where(held, out[k], value)
            value = value + (image_ref[k, n, at(j), :] - image) * scaled
            whole_ref[k, n, at(j), :] = ahead_ref[k, n, at(j), :] - alpha * value

    stiff(4, 14, second, smooth, moduli_ref, along_ref, up_ref, free, x_ref, late_ref)
    dots_ref[...] = jnp.zeros_like(dots_ref)

    def ahead(n, j):
        return [whole_ref[k, n, at(j), :] for k in range(3)]

    def finish(n, j, out):
        held = free(n, j) > 0.0
        for k in range(3):
            value = whole_ref[k, n, at(j), :]
            image = jnp.where(held, out[k], value)
            next_ref[k, n - H, at(j), :] = value
            next_image_ref[k, n - H, at(j), :] = image
            before = image_ref[k, n, at(j), :]
            dots_ref[0, k] += value * (rhs_ref[k, n, at(j), :] - alpha * before)
            dots_ref[1, k] += value * image
            dots_ref[2, k] += value * before

    stiff(5, 13, ahead, finish, moduli_ref, along_ref, up_ref, free, x_ref, late_ref)
    lane = lax.broadcasted_iota(jnp.int32, (8, 128), 1)
    line = jnp.zeros((8, 128), jnp.float32)
    for i in range(3):
        line = jnp.where(lane == i, jnp.sum(dots_ref[i]), line)
    for i in range(16):
        send_ref[at(i), :] = line


def close_kernel(gathered_ref, scalars_ref, rhs_ref, ahead_ref, image_ref, next_ref,
                 next_image_ref, displacement_ref, residual_ref):
    before = scalars_ref[0:1, :]
    gamma, energy = lane_value(before, 0), lane_value(before, 1)
    dots = jnp.sum(gathered_ref[...], axis=0, keepdims=True)
    following, own, cross = (lane_value(dots, i) for i in range(3))
    alpha = gamma / energy
    beta = following / gamma
    alpha_next = following / (own + 2.0 * beta * cross + beta * beta * energy)

    def step(n, unused):
        for k in range(3):
            ahead = ahead_ref[k, n + H]
            image = image_ref[k, n + H]
            direction = next_ref[k, n] + beta * ahead
            displacement_ref[k, n] = alpha * ahead + alpha_next * direction
            residual = rhs_ref[k, n + H] - alpha * image
            residual_ref[k, n] = residual - alpha_next * (next_image_ref[k, n] + beta * image)
        return unused

    lax.fori_loop(0, 8, step, 0)


def call(kernel, outs, scratch, *args, smem=(), cost=None):
    spaces = [
        pl.BlockSpec(memory_space=pltpu.SMEM if i in smem else pltpu.VMEM)
        for i in range(len(args))
    ]
    return pl.pallas_call(
        kernel,
        out_shape=[jax.ShapeDtypeStruct(s, jnp.float32) for s in outs],
        in_specs=spaces,
        out_specs=[pl.BlockSpec(memory_space=pltpu.VMEM)] * len(outs),
        scratch_shapes=[pltpu.VMEM(s, jnp.float32) for s in scratch],
        cost_estimate=cost,
        compiler_params=pltpu.CompilerParams(vmem_limit_bytes=14 * 2**20),
    )(*args)


def to_all(block):
    count = block.shape[0] // 128
    parts = lax.all_to_all(block.reshape(128, count, 128), BOTH, 0, 0)
    return parts.reshape(block.shape)


def body(load, phases, clamp, phase_moduli):
    size = lax.axis_size(BOTH)
    pairs = [(i, i ^ 1) for i in range(size)]
    links = [(i, i + (1 if i % 2 else -1)) for i in range(1, size - 1)]
    plane = (64, 128)
    field = (3, EXT) + plane
    ready = [field, (EXT,) + plane, (EXT,) + plane]
    work = [(12,) + plane, (12,) + plane, (6,) + plane, (6,) + plane]
    halo = (17,) + plane
    vmem = pl.BlockSpec(memory_space=pltpu.VMEM)
    to_chip, to_link, moduli_own = pl.pallas_call(
        pack_kernel,
        out_shape=[jax.ShapeDtypeStruct(s, jnp.float32) for s in (halo, halo, (8,) + plane)],
        in_specs=[pl.BlockSpec(memory_space=pltpu.HBM)] * 2
        + [pl.BlockSpec(memory_space=pltpu.SMEM)],
        out_specs=[vmem, vmem, vmem],
        scratch_shapes=[
            pltpu.VMEM(load.shape, jnp.float32),
            pltpu.VMEM(phases.shape, jnp.int32),
            pltpu.SemaphoreType.DMA((2,)),
        ],
        compiler_params=pltpu.CompilerParams(vmem_limit_bytes=60 * 2**20),
    )(load, phases, phase_moduli)
    from_link = lax.ppermute(to_link, BOTH, links)
    from_chip = lax.ppermute(to_chip, BOTH, pairs)
    own = (3, 8) + plane
    rhs_own, moduli_own, keep = call(
        own_kernel, [own, (8,) + plane, plane], [], load, moduli_own, clamp,
        cost=pl.CostEstimate(flops=20_000_000, bytes_accessed=20_000_000, transcendentals=0),
    )
    (send,) = call(
        first_kernel, [(512, 128)], ready + work + [(4,) + plane],
        from_link, from_chip, rhs_own, moduli_own, keep,
    )
    gathered = to_all(send)
    ahead, image, coarse, send, rhs, moduli, inverse = call(
        middle_kernel,
        [field, field, (WINDOW, 128), (512, 128)] + ready,
        work + [(3,) + plane, (2, 3, 8, 128), (4 * WINDOW, 128), (3 * WINDOW, 128), (72, 128)],
        gathered, from_link, from_chip, rhs_own, moduli_own, keep,
    )
    gathered = to_all(send)
    following, following_image, scalars, send = call(
        last_kernel,
        [own, own, (8, 128), (128, 128)],
        [field] + work + [(3, 3, 8, 128), (4 * WINDOW, 128), (3 * WINDOW, 128), (72, 128)],
        gathered, rhs, moduli, inverse, keep, ahead, image, coarse,
    )
    gathered = to_all(send)
    displacement, residual = call(
        close_kernel, [own, own], [],
        gathered, scalars, rhs, ahead, image, following, following_image,
    )
    return displacement, residual


def solution(mesh):
    placed = (P(None, BOTH, None, None), P(BOTH, None, None), P(), P())
    return jax.shard_map(
        body,
        mesh=mesh,
        in_specs=placed,
        out_specs=(P(None, BOTH, None, None), P(None, BOTH, None, None)),
        check_vma=False,
    )
```

```python
import functools
import math

import jax
import jax.numpy as jnp
import numpy as np
from jax import lax
from jax.experimental import pallas as pl
from jax.experimental.pallas import tpu as pltpu
from jax.sharding import PartitionSpec as P

COARSEN = 8
CHEB = 4
BOTH = ("grp", "gz")
GROUP = 32
H = 5
EXT = 17
WINDOW = 16
CORNER_OFFSETS = [(a, b, c) for a in (0, 1) for b in (0, 1) for c in (0, 1)]


def element_matrix():
    poisson = 0.3
    lame_first = poisson / ((1.0 + poisson) * (1.0 - 2.0 * poisson))
    shear = 1.0 / (2.0 * (1.0 + poisson))
    elastic = np.zeros((6, 6))
    elastic[:3, :3] = lame_first
    for axis_one in range(3):
        elastic[axis_one, axis_one] = lame_first + 2.0 * shear
        elastic[axis_one + 3, axis_one + 3] = shear
    points = [0.5 - 0.5 / math.sqrt(3.0), 0.5 + 0.5 / math.sqrt(3.0)]
    pairs = [(0, 1), (1, 2), (0, 2)]
    matrix = np.zeros((24, 24))
    for first_point in points:
        for second_point in points:
            for third_point in points:
                spot = (first_point, second_point, third_point)
                strain = np.zeros((6, 24))
                for corner, offset in enumerate(CORNER_OFFSETS):
                    values = [spot[i] if offset[i] else 1.0 - spot[i] for i in range(3)]
                    slopes = [1.0 if offset[i] else -1.0 for i in range(3)]
                    slants = []
                    for axis_one in range(3):
                        others = [values[i] for i in range(3) if i != axis_one]
                        slants.append(slopes[axis_one] * others[0] * others[1])
                        strain[axis_one, 3 * corner + axis_one] = slants[axis_one]
                    for position, pair in enumerate(pairs):
                        strain[3 + position, 3 * corner + pair[0]] = slants[pair[1]]
                        strain[3 + position, 3 * corner + pair[1]] = slants[pair[0]]
                matrix = matrix + 0.125 * (strain.T @ elastic @ strain)
    return matrix


NUMBERS = element_matrix()
BOUND = float(np.max(np.sum(np.abs(NUMBERS), axis=1) / np.diag(NUMBERS)))
OMEGA = 1.2 / BOUND
DIAGONAL = float(np.mean(np.diag(NUMBERS)))


def mode_matrix():
    haar = np.array([[1.0, 1.0], [-1.0, 1.0]])
    change = np.kron(np.kron(np.kron(haar, haar), haar), np.eye(3))
    return change @ NUMBERS @ change.T / 64.0


def mode_groups():
    modes = mode_matrix()
    near = np.abs(modes) > 1e-9
    left = [i for i in range(24) if near[i].any()]
    groups = []
    while left:
        group = [left[0]]
        for i in group:
            group += [j for j in left if near[i, j] and j not in group]
        groups.append(sorted(group))
        left = [i for i in left if i not in group]
    return modes, groups


MODES, MODE_GROUPS = mode_groups()


def mode_forces(value, scale):
    force = [None] * 24
    for group in MODE_GROUPS:
        diagonal = [float(MODES[i, i]) * scale for i in group]
        if len(group) == 1:
            force[group[0]] = diagonal[0] * value[group[0]]
            continue
        across = float(MODES[group[0], group[1]]) * scale
        apart = diagonal[0] - across
        total = value[group[0]]
        for i in group[1:]:
            total = total + value[i]
        total = across * total
        for i in group:
            if abs(apart) < 1e-9:
                force[i] = total
            else:
                force[i] = apart * value[i] + total
    return force


def lanes(value, by):
    return pltpu.roll(value, by % value.shape[1], 1)


def rows(value, by):
    return pltpu.roll(value, by % value.shape[0], 0)


def at(j):
    return slice(8 * j, 8 * j + 8)


def stiff(low, high, field, finish, moduli_ref, along_ref, up_ref, free, x_ref, late_ref):
    row = lax.broadcasted_iota(jnp.int32, (8, 128), 0)
    first_row = row == 0
    last_row = row == 7

    def x_modes(n, j):
        held = free(n, j)
        for k, value in enumerate(field(n, j)):
            value = value * held
            beside = lanes(value, -1)
            x_ref[2 * k, at(j), :] = value + beside
            x_ref[2 * k + 1, at(j), :] = beside - value

    def take(j):
        values = [x_ref[q, at(j), :] for q in range(6)]
        return values, [rows(v, -1) for v in values]

    def xy_modes(here, after):
        result = []
        for value, rolled, rolled_after in zip(here[0], here[1], after[1]):
            beside = jnp.where(last_row, rolled_after, rolled)
            result += [value + beside, beside - value]
        return result

    def flush(n, j):
        late = [late_ref[q, at(j), :] for q in range(6)]
        finish(n, j, [late[2 * k] + lanes(late[2 * k + 1], 1) for k in range(3)])

    def layer(n, stage):
        here = take(0)
        carried = [jnp.zeros((8, 128), jnp.float32)] * 6
        zero = jnp.zeros((8, 128), jnp.float32)
        for j in range(8):
            after = take(j + 1) if j < 7 else ([zero] * 6, [zero] * 6)
            now = xy_modes(here, after)
            here = after
            x_modes(jnp.minimum(n + 1, high), j)
            if stage > 2:
                flush(n - 2, j)
            before = [along_ref[q, at(j), :] for q in range(12)]
            for q in range(12):
                along_ref[q, at(j), :] = now[q]
            if stage == 0:
                continue
            weight = moduli_ref[n - 1, at(j), :]
            value = [None] * 24
            for k in range(3):
                for c in range(2):
                    for b in range(2):
                        q = 4 * k + 2 * c + b
                        value[3 * (2 * b + c) + k] = before[q] + now[q]
                        value[3 * (4 + 2 * b + c) + k] = now[q] - before[q]
            force = mode_forces(value, 1.0)
            done = {}
            weighted = []
            for i in range(24):
                f = force[i]
                if f is None:
                    weighted.append(None)
                    continue
                if id(f) not in done:
                    done[id(f)] = weight * f
                weighted.append(done[id(f)])
            totals = []
            for k in range(3):
                for c in range(2):
                    for b in range(2):
                        q = 4 * k + 2 * c + b
                        same = weighted[3 * (2 * b + c) + k]
                        change = weighted[3 * (4 + 2 * b + c) + k]
                        if stage > 1:
                            total = up_ref[q, at(j), :] - change
                            totals.append(total if same is None else total + same)
                        up_ref[q, at(j), :] = change if same is None else same + change
            if stage == 1:
                continue
            for k in range(3):
                parts = []
                for c in range(2):
                    same, change = totals[4 * k + 2 * c], totals[4 * k + 2 * c + 1]
                    over = rows(same + change, 1)
                    parts.append(same - change + jnp.where(first_row, carried[2 * k + c], over))
                    carried[2 * k + c] = over
                late_ref[2 * k, at(j), :] = parts[0] - parts[1]
                late_ref[2 * k + 1, at(j), :] = parts[0] + parts[1]

    for j in range(8):
        x_modes(low - 1, j)
    for stage in range(3):
        layer(low - 1 + stage, stage)

    def step(i, unused):
        layer(low + 2 + 2 * i, 3)
        layer(low + 3 + 2 * i, 3)
        return unused

    pairs = (high - low - 1) // 2
    lax.fori_loop(0, pairs, step, 0)
    if low + 2 + 2 * pairs == high:
        layer(high, 3)
    for j in range(8):
        flush(high - 1, j)


def block_forces(field, moduli_ref, along_ref, free, x_ref, total_ref):
    row = lax.broadcasted_iota(jnp.int32, (8, 128), 0)
    last_row = row == 7

    def x_modes(n, j):
        held = free(n, j)
        for k, value in enumerate(field(n, j)):
            value = value * held
            beside = lanes(value, -1)
            x_ref[2 * k, at(j), :] = value + beside
            x_ref[2 * k + 1, at(j), :] = beside - value

    def take(j):
        values = [x_ref[q, at(j), :] for q in range(6)]
        return values, [rows(v, -1) for v in values]

    def planes(following):
        here = take(0)
        zero = jnp.zeros((8, 128), jnp.float32)
        for j in range(8):
            after = take(j + 1) if j < 7 else ([zero] * 6, [zero] * 6)
            now = []
            for value, rolled, rolled_after in zip(here[0], here[1], after[1]):
                beside = jnp.where(last_row, rolled_after, rolled)
                now += [value + beside, beside - value]
            here = after
            x_modes(following, j)
            yield j, now

    def begin(n, following):
        for j in range(8):
            x_modes(n, j)
        for j, now in planes(following):
            for q in range(12):
                along_ref[q, at(j), :] = now[q]

    def add(n, following, kind):
        for j, now in planes(following):
            before = [along_ref[q, at(j), :] for q in range(12)]
            for q in range(12):
                along_ref[q, at(j), :] = now[q]
            weight = moduli_ref[n - 1, at(j), :]
            value = [None] * 24
            for k in range(3):
                for c in range(2):
                    for b in range(2):
                        q = 4 * k + 2 * c + b
                        value[3 * (2 * b + c) + k] = before[q] + now[q]
                        value[3 * (4 + 2 * b + c) + k] = now[q] - before[q]
            force = mode_forces(value, 1.0)
            for k in range(3):
                for c in range(2):
                    for b in range(2):
                        q = 4 * k + 2 * c + b
                        same = force[3 * (2 * b + c) + k]
                        change = force[3 * (4 + 2 * b + c) + k]
                        if kind == "inner":
                            if same is not None:
                                total_ref[12 + q, at(j), :] += (2.0 * weight) * same
                            continue
                        change = weight * change
                        same = 0.0 if same is None else weight * same
                        if kind == "below":
                            total_ref[q, at(j), :] = same + change
                        elif kind == "lowest":
                            total_ref[q, at(j), :] += same - change
                            total_ref[12 + q, at(j), :] += same + change
                        else:
                            total_ref[12 + q, at(j), :] += same - change

    return begin, add


def block_scatter(total_ref, base, finish):
    first_row = lax.broadcasted_iota(jnp.int32, (8, 128), 0) == 0
    carried = [jnp.zeros((8, 128), jnp.float32)] * 6
    for j in range(8):
        out = []
        for k in range(3):
            parts = []
            for c in range(2):
                same = total_ref[base + 4 * k + 2 * c, at(j), :]
                change = total_ref[base + 4 * k + 2 * c + 1, at(j), :]
                over = rows(same + change, 1)
                parts.append(same - change + jnp.where(first_row, carried[2 * k + c], over))
                carried[2 * k + c] = over
            out.append(parts[0] - parts[1] + lanes(parts[0] + parts[1], 1))
        finish(j, out)


def inner_layers(add):
    def step(i, unused):
        n = H + 2 + 2 * i
        add(n, n + 1, "inner")
        add(n + 1, n + 2, "inner")
        return unused

    lax.fori_loop(0, 3, step, 0)


def free_of(keep_ref, tile):
    def free(n, j):
        inside = jnp.where(tile * 8 + n == H, jnp.float32(0.0), jnp.float32(1.0))
        return jnp.maximum(keep_ref[at(j), :], inside)

    return free


def tile_index():
    return lax.axis_index("grp") * lax.axis_size("gz") + lax.axis_index("gz")


def coarse_pattern():
    fine = lax.broadcasted_iota(jnp.int32, (128, 128), 0)
    lane = lax.broadcasted_iota(jnp.int32, (128, 128), 1)
    return jnp.where((fine >> 3) == (lane & 15), 1.0, 0.0).astype(jnp.float32)


def exact_dot(a, b, contract):
    return lax.dot_general(
        a, b, (contract, ((), ())), precision=lax.Precision.HIGHEST,
        preferred_element_type=jnp.float32,
    )


def block_sums(planes):
    count = planes.shape[0] // 64
    summed = exact_dot(planes, coarse_pattern(), ((1,), (0,)))
    row = lax.broadcasted_iota(jnp.int32, (64, 128), 0)
    lane = lax.broadcasted_iota(jnp.int32, (64, 128), 1)
    own = (row >> 3) == (lane >> 4)
    return [
        jnp.sum(jnp.where(own, summed[64 * k : 64 * k + 64], 0.0), axis=0, keepdims=True)
        for k in range(count)
    ]


def send_rows(out_ref, four):
    block = jnp.concatenate(four + four, 0)
    for i in range(out_ref.shape[0] // 8):
        out_ref[at(i), :] = block


def coarse_solve(gathered_ref, coarse_ref, tile, window_ref, solved_ref, spread_ref):
    begin = window_begin(tile)
    window_ref[...] = gathered_ref[pl.ds(pl.multiple_of(4 * begin, 8), 4 * WINDOW), :]
    rhs = [window_ref[pl.ds(k, WINDOW, stride=4), :] for k in range(3)]
    if coarse_ref is None:
        moduli = window_ref[pl.ds(3, WINDOW, stride=4), :]
        row = lax.broadcasted_iota(jnp.int32, (WINDOW, 128), 0)
        moduli = jnp.where(row == WINDOW - 1, 0.0, moduli)
    else:
        moduli = coarse_ref[...]
    summed = moduli + lanes(moduli, 1)
    summed = summed + lanes(summed, 16)
    summed = DIAGONAL * COARSEN * (summed + rows(summed, 1))
    inverse = jnp.where(summed > 0.0, 1.0 / jnp.where(summed > 0.0, summed, 1.0), 0.0)

    def apply(field):
        value = [None] * 24
        for k in range(3):
            near = lanes(field[k], -1)
            for c, along_x in enumerate((field[k] + near, near - field[k])):
                near_y = lanes(along_x, -16)
                for b, along_y in enumerate((along_x + near_y, near_y - along_x)):
                    near_z = rows(along_y, -1)
                    value[3 * (2 * b + c) + k] = along_y + near_z
                    value[3 * (4 + 2 * b + c) + k] = near_z - along_y
        force = [None if f is None else moduli * f for f in mode_forces(value, COARSEN)]
        result = []
        for k in range(3):
            parts_x = []
            for c in range(2):
                parts_y = []
                for b in range(2):
                    same, change = force[3 * (2 * b + c) + k], force[3 * (4 + 2 * b + c) + k]
                    if same is None:
                        parts_y.append(rows(change, 1) - change)
                    else:
                        parts_y.append(same - change + rows(same + change, 1))
                parts_x.append(parts_y[0] - parts_y[1] + lanes(parts_y[0] + parts_y[1], 16))
            result.append(parts_x[0] - parts_x[1] + lanes(parts_x[0] + parts_x[1], 1))
        return result

    bottom = BOUND / 20.0
    center = 0.5 * (BOUND + bottom)
    radius = 0.5 * (BOUND - bottom)
    sigma = center / radius
    rho = 1.0 / sigma
    update = [inverse * (s * (1.0 / center)) for s in rhs]
    correction = update
    remainder = rhs
    for sweep in range(CHEB - 1):
        image = apply(update)
        remainder = [r - a for r, a in zip(remainder, image)]
        rho_next = 1.0 / (2.0 * sigma - rho)
        update = [
            (rho_next * rho) * u + (2.0 * rho_next / radius) * (inverse * r)
            for u, r in zip(update, remainder)
        ]
        correction = [c + u for c, u in zip(correction, update)]
        rho = rho_next
    row = lax.broadcasted_iota(jnp.int32, (8, 128), 0)
    lane = lax.broadcasted_iota(jnp.int32, (8, 128), 1)
    own = row == (lane >> 4)
    for k in range(3):
        solved_ref[WINDOW * k : WINDOW * (k + 1), :] = correction[k]
    blocks = []
    for which in range(3):
        place = jnp.clip(tile - begin + which - 1, 0, WINDOW - 1)
        for k in range(3):
            line = solved_ref[pl.ds(WINDOW * k + place, 1), :]
            blocks.append(jnp.where(own, jnp.broadcast_to(line, (8, 128)), 0.0))
    spread_ref[...] = exact_dot(
        jnp.concatenate(blocks, 0), coarse_pattern(), ((1,), (1,))
    )
    return moduli


def window_begin(tile):
    return 2 * jnp.minimum(jnp.maximum(tile - 7, 0) >> 1, (128 - WINDOW) // 2)


def correction_of(spread_ref):
    def correction(n, j):
        which = jnp.where(n < H, 0, jnp.where(n < H + 8, 1, 2))
        return [
            jnp.broadcast_to(spread_ref[pl.ds((3 * which + k) * 8 + j, 1), :], (8, 128))
            for k in range(3)
        ]

    return correction


def pack_kernel(load_hbm, phases_hbm, table_ref,
                chip_ref, link_ref, moduli_ref,
                load_ref, phases_ref, arrived):
    fetch_phases = pltpu.make_async_copy(phases_hbm, phases_ref, arrived.at[0])
    fetch_load = pltpu.make_async_copy(load_hbm, load_ref, arrived.at[1])
    fetch_phases.start()
    fetch_load.start()
    tile = tile_index()
    row = lax.broadcasted_iota(jnp.int32, (64, 128), 0)
    lane = lax.broadcasted_iota(jnp.int32, (64, 128), 1)
    interior = (row < 63) & (lane < 127)
    table = [table_ref[i] for i in range(4)]
    fetch_phases.wait()
    for n in range(8):
        value = jnp.zeros((64, 128), jnp.float32)
        for i in range(4):
            value = jnp.where(phases_ref[n] == i, table[i], value)
        inside = interior if n < 7 else interior & (tile < 127)
        moduli_ref[n] = jnp.where(inside, value, 0.0)
    fetch_load.wait()

    def fill(top_ref, low_ref):
        for k in range(3):
            top_ref[k] = load_ref[k, 7]
            low_ref[k] = load_ref[k, 0]
            for n in range(3):
                top_ref[5 + 3 * k + n] = load_ref[k, 4 + n]
                low_ref[5 + 3 * k + n] = load_ref[k, 1 + n]
        for n in range(2):
            top_ref[3 + n] = moduli_ref[6 + n]
            low_ref[3 + n] = moduli_ref[n]
        for n in range(3):
            top_ref[14 + n] = moduli_ref[3 + n]
            low_ref[14 + n] = moduli_ref[1 + n]

    @pl.when((tile & 1) == 0)
    def even():
        fill(chip_ref, link_ref)

    @pl.when((tile & 1) == 1)
    def odd():
        fill(link_ref, chip_ref)


def own_kernel(load_ref, own_ref, clamp_ref, rhs_ref, moduli_ref, keep_ref):
    keep_ref[...] = 1.0 - clamp_ref[...].astype(jnp.float32)
    moduli_ref[...] = own_ref[...]
    for k in range(3):
        rhs_ref[k] = load_ref[k]
        held = jnp.where(tile_index() == 0, keep_ref[...], 1.0)
        rhs_ref[k, 0] = held * load_ref[k, 0]


def inverse_of(before, value, n, keep_ref, tile):
    depth = tile * 8 + n
    both = before + value
    both = both + rows(both, 1)
    both = DIAGONAL * (both + lanes(both, 1))
    inside = jnp.where(depth == 0, jnp.float32(0.0), jnp.float32(1.0))
    held = jnp.maximum(keep_ref[...], inside)
    both = held * both + 1.0 - held
    exists = (depth >= 0) & (depth < 1024)
    both = jnp.where(exists, both, 1.0)
    return jnp.where(exists, 1.0 / both, 0.0)


def first_of(rhs_ref, inverse_ref):
    def first(n, j):
        scaled = OMEGA * inverse_ref[n, at(j), :]
        return [rhs_ref[k, n, at(j), :] * scaled for k in range(3)]

    return first


def own_kernel(load_ref, own_ref, clamp_ref,
               rhs_ref, moduli_ref, inverse_ref, keep_ref, total_ref, sum_ref,
               along_ref, x_ref):
    tile = tile_index()
    keep_ref[...] = 1.0 - clamp_ref[...].astype(jnp.float32)
    total = jnp.zeros((64, 128), jnp.float32)
    before = None
    for n in range(8):
        value = own_ref[n]
        moduli_ref[H + n] = value
        total = total + value
        if n:
            inverse_ref[H + n] = inverse_of(before, value, n, keep_ref, tile)
        before = value
    sum_ref[3] = total
    held = jnp.where(tile == 0, keep_ref[...], 1.0)
    for k in range(3):
        total = held * load_ref[k, 0]
        rhs_ref[k, H] = total
        for n in range(1, 8):
            rhs_ref[k, H + n] = load_ref[k, n]
            total = total + load_ref[k, n]
        sum_ref[k] = total
    total_ref[...] = jnp.zeros_like(total_ref)
    inverse_ref[H + 8] = jnp.zeros((64, 128), jnp.float32)
    for k in range(3):
        rhs_ref[k, H + 8] = jnp.zeros((64, 128), jnp.float32)
    begin, add = block_forces(
        first_of(rhs_ref, inverse_ref), moduli_ref, along_ref, free_of(keep_ref, tile),
        x_ref, total_ref,
    )
    begin(H + 1, H + 2)
    inner_layers(add)


def set_up(link_ref, chip_ref, own_rhs_ref, own_moduli_ref, own_inverse_ref, keep_ref,
           rhs_ref, moduli_ref, inverse_ref, tile):
    even = (tile & 1) == 0

    def below(i):
        return jnp.where(even, link_ref[i], chip_ref[i])

    def above(i):
        return jnp.where(even, chip_ref[i], link_ref[i])

    def moduli(n):
        if n < -2:
            return below(14 + n + 5)
        if n < 0:
            return below(3 + n + 2)
        if n < 8:
            return own_moduli_ref[n + H]
        if n < 9:
            return above(3)
        return above(14 + n - 9)

    def load(k, n):
        if n < -1:
            return below(5 + 3 * k + n + 4)
        if n < 0:
            return below(k)
        if n < 9:
            return above(k)
        return above(5 + 3 * k + n - 9)

    before = None
    for n in range(-5, 12):
        value = moduli(n)
        moduli_ref[n + H] = value
        if 0 < n < 8:
            inverse_ref[n + H] = own_inverse_ref[n + H]
        elif n > -5:
            inverse_ref[n + H] = inverse_of(before, value, n, keep_ref, tile)
        before = value
        if n < -4:
            continue
        for k in range(3):
            if 0 <= n < 8:
                rhs_ref[k, n + H] = own_rhs_ref[k, n + H]
            else:
                depth = tile * 8 + n
                inside = jnp.where(depth == 0, jnp.float32(0.0), jnp.float32(1.0))
                rhs_ref[k, n + H] = jnp.maximum(keep_ref[...], inside) * load(k, n)


def first_kernel(link_ref, chip_ref, own_rhs_ref, own_moduli_ref, own_inverse_ref, keep_ref,
                 inner_ref, own_sum_ref,
                 send_ref, rhs_ref, moduli_ref, inverse_ref,
                 along_ref, x_ref, total_ref, sum_ref):
    tile = tile_index()
    set_up(link_ref, chip_ref, own_rhs_ref, own_moduli_ref, own_inverse_ref, keep_ref,
           rhs_ref, moduli_ref, inverse_ref, tile)
    free = free_of(keep_ref, tile)
    total_ref[...] = inner_ref[...]
    first = first_of(rhs_ref, inverse_ref)
    begin, add = block_forces(first, moduli_ref, along_ref, free, x_ref, total_ref)
    begin(H - 1, H)
    add(H, H + 1, "below")
    add(H + 1, H + 1, "lowest")
    begin(H + 7, H + 8)
    add(H + 8, H + 8, "above")

    def lowest(j, out):
        held = free(H, j) > 0.0
        value = first(H, j)
        for k in range(3):
            image = jnp.where(held, out[k], value[k])
            sum_ref[k, at(j), :] = own_sum_ref[k, at(j), :] - image

    def others(j, out):
        for k in range(3):
            sum_ref[k, at(j), :] -= out[k]

    block_scatter(total_ref, 0, lowest)
    block_scatter(total_ref, 12, others)
    sum_ref[3] = own_sum_ref[3]
    four = block_sums(sum_ref[...].reshape(256, 128))
    lane = lax.broadcasted_iota(jnp.int32, (1, 128), 1)
    edge = (lane >= 112) | ((lane & 15) == 15) | (lax.rem(tile, GROUP) == GROUP - 1)
    four[3] = jnp.where(edge, 0.0, four[3] * (1.0 / 512.0))
    send_rows(send_ref, four)


def middle_kernel(gathered_ref, rhs_ref, moduli_ref, inverse_ref, keep_ref,
                  ahead_ref, image_ref, coarse_ref, send_ref,
                  along_ref, up_ref, x_ref, late_ref, total_ref,
                  sum_ref, dots_ref, window_ref, solved_ref, spread_ref):
    tile = tile_index()
    free = free_of(keep_ref, tile)
    coarse_ref[...] = coarse_solve(gathered_ref, None, tile, window_ref, solved_ref, spread_ref)
    correction = correction_of(spread_ref)

    def second(n, j):
        scaled = OMEGA * inverse_ref[n, at(j), :]
        held = free(n, j)
        result = []
        for k, coarse_value in enumerate(correction(n, j)):
            value = rhs_ref[k, n, at(j), :] * scaled + held * coarse_value
            result.append(value)
        return result

    def smooth(n, j, out):
        held = free(n, j) > 0.0
        scaled = OMEGA * inverse_ref[n, at(j), :]
        for k, value in enumerate(second(n, j)):
            image = jnp.where(held, out[k], value)
            ahead_ref[k, n, at(j), :] = value + (rhs_ref[k, n, at(j), :] - image) * scaled

    stiff(2, 16, second, smooth, moduli_ref, along_ref, up_ref, free, x_ref, late_ref)

    def ahead(n, j):
        return [ahead_ref[k, n, at(j), :] for k in range(3)]

    def keep_image(n, j, out):
        held = free(n, j) > 0.0
        for k in range(3):
            image_ref[k, n, at(j), :] = jnp.where(
                held, out[k], ahead_ref[k, n, at(j), :]
            )

    stiff(3, 15, ahead, keep_image, moduli_ref, along_ref, up_ref, free, x_ref, late_ref)

    total_ref[12:24] = jnp.zeros((12, 64, 128), jnp.float32)
    first = first_of(image_ref, inverse_ref)
    begin, add = block_forces(first, moduli_ref, along_ref, free, x_ref, total_ref)
    begin(H - 1, H)
    add(H, H + 1, "below")
    add(H + 1, H + 2, "lowest")
    inner_layers(add)
    add(H + 8, H + 8, "above")

    def lowest(j, out):
        held = free(H, j) > 0.0
        value = first(H, j)
        for k in range(3):
            sum_ref[k, at(j), :] = -jnp.where(held, out[k], value[k])

    def others(j, out):
        for k in range(3):
            sum_ref[k, at(j), :] -= out[k]

    block_scatter(total_ref, 0, lowest)
    block_scatter(total_ref, 12, others)
    dots_ref[...] = jnp.zeros_like(dots_ref)

    def products(n, unused):
        for k in range(3):
            by_rhs, by_image = [], []
            for j in range(8):
                image = image_ref[k, n, at(j), :]
                now = ahead_ref[k, n, at(j), :]
                sum_ref[k, at(j), :] += image
                by_rhs.append(now * rhs_ref[k, n, at(j), :])
                by_image.append(now * image)
            dots_ref[0, k] += sum(by_rhs[1:], by_rhs[0])
            dots_ref[1, k] += sum(by_image[1:], by_image[0])
        return unused

    lax.fori_loop(H, H + 8, products, 0)
    three = block_sums(sum_ref[...].reshape(192, 128))
    lane = lax.broadcasted_iota(jnp.int32, (1, 128), 1)
    gamma = jnp.sum(dots_ref[0])
    energy = jnp.sum(dots_ref[1])
    dots = jnp.where(lane == 0, gamma, jnp.where(lane == 1, energy, 0.0))
    send_rows(send_ref, three + [dots])


def lane_value(line, i):
    lane = lax.broadcasted_iota(jnp.int32, line.shape, 1)
    return jnp.sum(jnp.where(lane == i, line, 0.0))


def last_kernel(gathered_ref, rhs_ref, moduli_ref, inverse_ref, keep_ref, ahead_ref, image_ref,
                coarse_ref,
                next_ref, next_image_ref, scalars_ref, send_ref,
                whole_ref, along_ref, up_ref, x_ref, late_ref, dots_ref, window_ref, solved_ref, spread_ref):
    tile = tile_index()
    free = free_of(keep_ref, tile)
    dots = jnp.sum(gathered_ref[pl.ds(3, 128, stride=4), :], axis=0, keepdims=True)
    scalars_ref[...] = jnp.broadcast_to(dots, (8, 128))
    alpha = lane_value(dots, 0) / lane_value(dots, 1)
    coarse_solve(gathered_ref, coarse_ref, tile, window_ref, solved_ref, spread_ref)
    correction = correction_of(spread_ref)

    def second(n, j):
        scaled = OMEGA * inverse_ref[n, at(j), :]
        held = free(n, j)
        result = []
        for k, coarse_value in enumerate(correction(n, j)):
            value = image_ref[k, n, at(j), :] * scaled + held * coarse_value
            result.append(value)
        return result

    def smooth(n, j, out):
        held = free(n, j) > 0.0
        scaled = OMEGA * inverse_ref[n, at(j), :]
        for k, value in enumerate(second(n, j)):
            image = jnp.where(held, out[k], value)
            value = value + (image_ref[k, n, at(j), :] - image) * scaled
            whole_ref[k, n, at(j), :] = ahead_ref[k, n, at(j), :] - alpha * value

    stiff(4, 14, second, smooth, moduli_ref, along_ref, up_ref, free, x_ref, late_ref)
    dots_ref[...] = jnp.zeros_like(dots_ref)

    def ahead(n, j):
        return [whole_ref[k, n, at(j), :] for k in range(3)]

    def finish(n, j, out):
        held = free(n, j) > 0.0
        for k in range(3):
            value = whole_ref[k, n, at(j), :]
            image = jnp.where(held, out[k], value)
            next_ref[k, n - H, at(j), :] = value
            next_image_ref[k, n - H, at(j), :] = image
            before = image_ref[k, n, at(j), :]
            dots_ref[0, k] += value * (rhs_ref[k, n, at(j), :] - alpha * before)
            dots_ref[1, k] += value * image
            dots_ref[2, k] += value * before

    stiff(5, 13, ahead, finish, moduli_ref, along_ref, up_ref, free, x_ref, late_ref)
    lane = lax.broadcasted_iota(jnp.int32, (8, 128), 1)
    line = jnp.zeros((8, 128), jnp.float32)
    for i in range(3):
        line = jnp.where(lane == i, jnp.sum(dots_ref[i]), line)
    for i in range(16):
        send_ref[at(i), :] = line


def close_kernel(gathered_ref, scalars_ref, rhs_ref, ahead_ref, image_ref, next_ref,
                 next_image_ref, displacement_ref, residual_ref):
    before = scalars_ref[0:1, :]
    gamma, energy = lane_value(before, 0), lane_value(before, 1)
    dots = jnp.sum(gathered_ref[...], axis=0, keepdims=True)
    following, own, cross = (lane_value(dots, i) for i in range(3))
    alpha = gamma / energy
    beta = following / gamma
    alpha_next = following / (own + 2.0 * beta * cross + beta * beta * energy)

    def step(n, unused):
        for k in range(3):
            ahead = ahead_ref[k, n + H]
            image = image_ref[k, n + H]
            direction = next_ref[k, n] + beta * ahead
            displacement_ref[k, n] = alpha * ahead + alpha_next * direction
            residual = rhs_ref[k, n + H] - alpha * image
            residual_ref[k, n] = residual - alpha_next * (next_image_ref[k, n] + beta * image)
        return unused

    lax.fori_loop(0, 8, step, 0)


def call(kernel, outs, scratch, *args, smem=(), cost=None):
    spaces = [
        pl.BlockSpec(memory_space=pltpu.SMEM if i in smem else pltpu.VMEM)
        for i in range(len(args))
    ]
    return pl.pallas_call(
        kernel,
        out_shape=[jax.ShapeDtypeStruct(s, jnp.float32) for s in outs],
        in_specs=spaces,
        out_specs=[pl.BlockSpec(memory_space=pltpu.VMEM)] * len(outs),
        scratch_shapes=[pltpu.VMEM(s, jnp.float32) for s in scratch],
        cost_estimate=cost,
        compiler_params=pltpu.CompilerParams(vmem_limit_bytes=14 * 2**20),
    )(*args)


def to_all(block):
    count = block.shape[0] // 128
    parts = lax.all_to_all(block.reshape(128, count, 128), BOTH, 0, 0)
    return parts.reshape(block.shape)


def body(load, phases, clamp, phase_moduli):
    size = lax.axis_size(BOTH)
    pairs = [(i, i ^ 1) for i in range(size)]
    links = [(i, i + (1 if i % 2 else -1)) for i in range(1, size - 1)]
    plane = (64, 128)
    field = (3, EXT) + plane
    ready = [field, (EXT,) + plane, (EXT,) + plane]
    work = [(12,) + plane, (12,) + plane, (6,) + plane, (6,) + plane]
    halo = (17,) + plane
    vmem = pl.BlockSpec(memory_space=pltpu.VMEM)
    to_chip, to_link, moduli_own = pl.pallas_call(
        pack_kernel,
        out_shape=[jax.ShapeDtypeStruct(s, jnp.float32) for s in (halo, halo, (8,) + plane)],
        in_specs=[pl.BlockSpec(memory_space=pltpu.HBM)] * 2
        + [pl.BlockSpec(memory_space=pltpu.SMEM)],
        out_specs=[vmem, vmem, vmem],
        scratch_shapes=[
            pltpu.VMEM(load.shape, jnp.float32),
            pltpu.VMEM(phases.shape, jnp.int32),
            pltpu.SemaphoreType.DMA((2,)),
        ],
        compiler_params=pltpu.CompilerParams(vmem_limit_bytes=60 * 2**20),
    )(load, phases, phase_moduli)
    from_link = lax.ppermute(to_link, BOTH, links)
    from_chip = lax.ppermute(to_chip, BOTH, pairs)
    own = (3, 8) + plane
    own_rhs, own_moduli, own_inverse, keep, inner, own_sum = call(
        own_kernel, ready + [plane, (24,) + plane, (4,) + plane],
        [(12,) + plane, (6,) + plane], load, moduli_own, clamp,
        cost=pl.CostEstimate(flops=20_000_000, bytes_accessed=20_000_000, transcendentals=0),
    )
    send, rhs, moduli, inverse = call(
        first_kernel, [(512, 128)] + ready,
        [(12,) + plane, (6,) + plane, (24,) + plane, (4,) + plane],
        from_link, from_chip, own_rhs, own_moduli, own_inverse, keep, inner, own_sum,
    )
    gathered = to_all(send)
    ahead, image, coarse, send = call(
        middle_kernel,
        [field, field, (WINDOW, 128), (512, 128)],
        work + [(24,) + plane, (3,) + plane, (2, 3, 8, 128), (4 * WINDOW, 128),
                (3 * WINDOW, 128), (72, 128)],
        gathered, rhs, moduli, inverse, keep,
    )
    gathered = to_all(send)
    following, following_image, scalars, send = call(
        last_kernel,
        [own, own, (8, 128), (128, 128)],
        [field] + work + [(3, 3, 8, 128), (4 * WINDOW, 128), (3 * WINDOW, 128), (72, 128)],
        gathered, rhs, moduli, inverse, keep, ahead, image, coarse,
    )
    gathered = to_all(send)
    displacement, residual = call(
        close_kernel, [own, own], [],
        gathered, scalars, rhs, ahead, image, following, following_image,
    )
    return displacement, residual


def solution(mesh):
    placed = (P(None, BOTH, None, None), P(BOTH, None, None), P(), P())
    return jax.shard_map(
        body,
        mesh=mesh,
        in_specs=placed,
        out_specs=(P(None, BOTH, None, None), P(None, BOTH, None, None)),
        check_vma=False,
    )
```

```python
import functools
import math

import jax
import jax.numpy as jnp
import numpy as np
from jax import lax
from jax.experimental import pallas as pl
from jax.experimental.pallas import tpu as pltpu
from jax.sharding import PartitionSpec as P

COARSEN = 8
CHEB = 4
BOTH = ("grp", "gz")
GROUP = 32
H = 5
EXT = 17
WINDOW = 16
CORNER_OFFSETS = [(a, b, c) for a in (0, 1) for b in (0, 1) for c in (0, 1)]


def element_matrix():
    poisson = 0.3
    lame_first = poisson / ((1.0 + poisson) * (1.0 - 2.0 * poisson))
    shear = 1.0 / (2.0 * (1.0 + poisson))
    elastic = np.zeros((6, 6))
    elastic[:3, :3] = lame_first
    for axis_one in range(3):
        elastic[axis_one, axis_one] = lame_first + 2.0 * shear
        elastic[axis_one + 3, axis_one + 3] = shear
    points = [0.5 - 0.5 / math.sqrt(3.0), 0.5 + 0.5 / math.sqrt(3.0)]
    pairs = [(0, 1), (1, 2), (0, 2)]
    matrix = np.zeros((24, 24))
    for first_point in points:
        for second_point in points:
            for third_point in points:
                spot = (first_point, second_point, third_point)
                strain = np.zeros((6, 24))
                for corner, offset in enumerate(CORNER_OFFSETS):
                    values = [spot[i] if offset[i] else 1.0 - spot[i] for i in range(3)]
                    slopes = [1.0 if offset[i] else -1.0 for i in range(3)]
                    slants = []
                    for axis_one in range(3):
                        others = [values[i] for i in range(3) if i != axis_one]
                        slants.append(slopes[axis_one] * others[0] * others[1])
                        strain[axis_one, 3 * corner + axis_one] = slants[axis_one]
                    for position, pair in enumerate(pairs):
                        strain[3 + position, 3 * corner + pair[0]] = slants[pair[1]]
                        strain[3 + position, 3 * corner + pair[1]] = slants[pair[0]]
                matrix = matrix + 0.125 * (strain.T @ elastic @ strain)
    return matrix


NUMBERS = element_matrix()
BOUND = float(np.max(np.sum(np.abs(NUMBERS), axis=1) / np.diag(NUMBERS)))
OMEGA = 1.2 / BOUND
DIAGONAL = float(np.mean(np.diag(NUMBERS)))


def mode_matrix():
    haar = np.array([[1.0, 1.0], [-1.0, 1.0]])
    change = np.kron(np.kron(np.kron(haar, haar), haar), np.eye(3))
    return change @ NUMBERS @ change.T / 64.0


def mode_groups():
    modes = mode_matrix()
    near = np.abs(modes) > 1e-9
    left = [i for i in range(24) if near[i].any()]
    groups = []
    while left:
        group = [left[0]]
        for i in group:
            group += [j for j in left if near[i, j] and j not in group]
        groups.append(sorted(group))
        left = [i for i in left if i not in group]
    return modes, groups


MODES, MODE_GROUPS = mode_groups()


def mode_forces(value, scale):
    force = [None] * 24
    for group in MODE_GROUPS:
        diagonal = [float(MODES[i, i]) * scale for i in group]
        if len(group) == 1:
            force[group[0]] = diagonal[0] * value[group[0]]
            continue
        across = float(MODES[group[0], group[1]]) * scale
        apart = diagonal[0] - across
        total = value[group[0]]
        for i in group[1:]:
            total = total + value[i]
        total = across * total
        for i in group:
            if abs(apart) < 1e-9:
                force[i] = total
            else:
                force[i] = apart * value[i] + total
    return force


def lanes(value, by):
    return pltpu.roll(value, by % value.shape[1], 1)


def rows(value, by):
    return pltpu.roll(value, by % value.shape[0], 0)


def at(j):
    return slice(8 * j, 8 * j + 8)


def stiff(low, high, field, finish, moduli_ref, along_ref, up_ref, free, x_ref, late_ref):
    row = lax.broadcasted_iota(jnp.int32, (8, 128), 0)
    first_row = row == 0
    last_row = row == 7

    def x_modes(n, j):
        held = free(n, j)
        for k, value in enumerate(field(n, j)):
            value = value * held
            beside = lanes(value, -1)
            x_ref[2 * k, at(j), :] = value + beside
            x_ref[2 * k + 1, at(j), :] = beside - value

    def take(j):
        values = [x_ref[q, at(j), :] for q in range(6)]
        return values, [rows(v, -1) for v in values]

    def xy_modes(here, after):
        result = []
        for value, rolled, rolled_after in zip(here[0], here[1], after[1]):
            beside = jnp.where(last_row, rolled_after, rolled)
            result += [value + beside, beside - value]
        return result

    def flush(n, j):
        late = [late_ref[q, at(j), :] for q in range(6)]
        finish(n, j, [late[2 * k] + lanes(late[2 * k + 1], 1) for k in range(3)])

    def layer(n, stage):
        here = take(0)
        carried = [jnp.zeros((8, 128), jnp.float32)] * 6
        zero = jnp.zeros((8, 128), jnp.float32)
        for j in range(8):
            after = take(j + 1) if j < 7 else ([zero] * 6, [zero] * 6)
            now = xy_modes(here, after)
            here = after
            x_modes(jnp.minimum(n + 1, high), j)
            if stage > 2:
                flush(n - 2, j)
            before = [along_ref[q, at(j), :] for q in range(12)]
            for q in range(12):
                along_ref[q, at(j), :] = now[q]
            if stage == 0:
                continue
            weight = moduli_ref[n - 1, at(j), :]
            value = [None] * 24
            for k in range(3):
                for c in range(2):
                    for b in range(2):
                        q = 4 * k + 2 * c + b
                        value[3 * (2 * b + c) + k] = before[q] + now[q]
                        value[3 * (4 + 2 * b + c) + k] = now[q] - before[q]
            force = mode_forces(value, 1.0)
            done = {}
            weighted = []
            for i in range(24):
                f = force[i]
                if f is None:
                    weighted.append(None)
                    continue
                if id(f) not in done:
                    done[id(f)] = weight * f
                weighted.append(done[id(f)])
            totals = []
            for k in range(3):
                for c in range(2):
                    for b in range(2):
                        q = 4 * k + 2 * c + b
                        same = weighted[3 * (2 * b + c) + k]
                        change = weighted[3 * (4 + 2 * b + c) + k]
                        if stage > 1:
                            total = up_ref[q, at(j), :] - change
                            totals.append(total if same is None else total + same)
                        up_ref[q, at(j), :] = change if same is None else same + change
            if stage == 1:
                continue
            for k in range(3):
                parts = []
                for c in range(2):
                    same, change = totals[4 * k + 2 * c], totals[4 * k + 2 * c + 1]
                    over = rows(same + change, 1)
                    parts.append(same - change + jnp.where(first_row, carried[2 * k + c], over))
                    carried[2 * k + c] = over
                late_ref[2 * k, at(j), :] = parts[0] - parts[1]
                late_ref[2 * k + 1, at(j), :] = parts[0] + parts[1]

    for j in range(8):
        x_modes(low - 1, j)
    for stage in range(3):
        layer(low - 1 + stage, stage)

    def step(i, unused):
        layer(low + 2 + 2 * i, 3)
        layer(low + 3 + 2 * i, 3)
        return unused

    pairs = (high - low - 1) // 2
    lax.fori_loop(0, pairs, step, 0)
    if low + 2 + 2 * pairs == high:
        layer(high, 3)
    for j in range(8):
        flush(high - 1, j)


def block_forces(field, moduli_ref, along_ref, free, x_ref, total_ref):
    row = lax.broadcasted_iota(jnp.int32, (8, 128), 0)
    last_row = row == 7

    def x_modes(n, j):
        held = free(n, j)
        for k, value in enumerate(field(n, j)):
            value = value * held
            beside = lanes(value, -1)
            x_ref[2 * k, at(j), :] = value + beside
            x_ref[2 * k + 1, at(j), :] = beside - value

    def take(j):
        values = [x_ref[q, at(j), :] for q in range(6)]
        return values, [rows(v, -1) for v in values]

    def planes(following):
        here = take(0)
        zero = jnp.zeros((8, 128), jnp.float32)
        for j in range(8):
            after = take(j + 1) if j < 7 else ([zero] * 6, [zero] * 6)
            now = []
            for value, rolled, rolled_after in zip(here[0], here[1], after[1]):
                beside = jnp.where(last_row, rolled_after, rolled)
                now += [value + beside, beside - value]
            here = after
            x_modes(following, j)
            yield j, now

    def begin(n, following):
        for j in range(8):
            x_modes(n, j)
        for j, now in planes(following):
            for q in range(12):
                along_ref[q, at(j), :] = now[q]

    def add(n, following, kind):
        for j, now in planes(following):
            before = [along_ref[q, at(j), :] for q in range(12)]
            for q in range(12):
                along_ref[q, at(j), :] = now[q]
            weight = moduli_ref[n - 1, at(j), :]
            value = [None] * 24
            for k in range(3):
                for c in range(2):
                    for b in range(2):
                        q = 4 * k + 2 * c + b
                        value[3 * (2 * b + c) + k] = before[q] + now[q]
                        value[3 * (4 + 2 * b + c) + k] = now[q] - before[q]
            force = mode_forces(value, 1.0)
            for k in range(3):
                for c in range(2):
                    for b in range(2):
                        q = 4 * k + 2 * c + b
                        same = force[3 * (2 * b + c) + k]
                        change = force[3 * (4 + 2 * b + c) + k]
                        if kind == "inner":
                            if same is not None:
                                total_ref[12 + q, at(j), :] += (2.0 * weight) * same
                            continue
                        change = weight * change
                        same = 0.0 if same is None else weight * same
                        if kind == "below":
                            total_ref[q, at(j), :] = same + change
                        elif kind == "lowest":
                            total_ref[q, at(j), :] += same - change
                            total_ref[12 + q, at(j), :] += same + change
                        else:
                            total_ref[12 + q, at(j), :] += same - change

    return begin, add


def block_scatter(total_ref, base, finish):
    first_row = lax.broadcasted_iota(jnp.int32, (8, 128), 0) == 0
    carried = [jnp.zeros((8, 128), jnp.float32)] * 6
    for j in range(8):
        out = []
        for k in range(3):
            parts = []
            for c in range(2):
                same = total_ref[base + 4 * k + 2 * c, at(j), :]
                change = total_ref[base + 4 * k + 2 * c + 1, at(j), :]
                over = rows(same + change, 1)
                parts.append(same - change + jnp.where(first_row, carried[2 * k + c], over))
                carried[2 * k + c] = over
            out.append(parts[0] - parts[1] + lanes(parts[0] + parts[1], 1))
        finish(j, out)


def inner_layers(add):
    def step(i, unused):
        n = H + 2 + 2 * i
        add(n, n + 1, "inner")
        add(n + 1, n + 2, "inner")
        return unused

    lax.fori_loop(0, 3, step, 0)


def free_of(keep_ref, tile):
    def free(n, j):
        inside = jnp.where(tile * 8 + n == H, jnp.float32(0.0), jnp.float32(1.0))
        return jnp.maximum(keep_ref[at(j), :], inside)

    return free


def tile_index():
    return lax.axis_index("grp") * lax.axis_size("gz") + lax.axis_index("gz")


def coarse_pattern():
    fine = lax.broadcasted_iota(jnp.int32, (128, 128), 0)
    lane = lax.broadcasted_iota(jnp.int32, (128, 128), 1)
    return jnp.where((fine >> 3) == (lane & 15), 1.0, 0.0).astype(jnp.float32)


def exact_dot(a, b, contract):
    return lax.dot_general(
        a, b, (contract, ((), ())), precision=lax.Precision.HIGHEST,
        preferred_element_type=jnp.float32,
    )


def block_sums(planes):
    count = planes.shape[0] // 64
    summed = exact_dot(planes, coarse_pattern(), ((1,), (0,)))
    row = lax.broadcasted_iota(jnp.int32, (64, 128), 0)
    lane = lax.broadcasted_iota(jnp.int32, (64, 128), 1)
    own = (row >> 3) == (lane >> 4)
    return [
        jnp.sum(jnp.where(own, summed[64 * k : 64 * k + 64], 0.0), axis=0, keepdims=True)
        for k in range(count)
    ]


def send_rows(out_ref, four):
    block = jnp.concatenate(four + four, 0)
    for i in range(out_ref.shape[0] // 8):
        out_ref[at(i), :] = block


def coarse_solve(gathered_ref, coarse_ref, tile, window_ref, solved_ref, spread_ref):
    begin = window_begin(tile)
    window_ref[...] = gathered_ref[pl.ds(pl.multiple_of(4 * begin, 8), 4 * WINDOW), :]
    rhs = [window_ref[pl.ds(k, WINDOW, stride=4), :] for k in range(3)]
    if coarse_ref is None:
        moduli = window_ref[pl.ds(3, WINDOW, stride=4), :]
        row = lax.broadcasted_iota(jnp.int32, (WINDOW, 128), 0)
        moduli = jnp.where(row == WINDOW - 1, 0.0, moduli)
    else:
        moduli = coarse_ref[...]
    summed = moduli + lanes(moduli, 1)
    summed = summed + lanes(summed, 16)
    summed = DIAGONAL * COARSEN * (summed + rows(summed, 1))
    inverse = jnp.where(summed > 0.0, 1.0 / jnp.where(summed > 0.0, summed, 1.0), 0.0)

    def apply(field):
        value = [None] * 24
        for k in range(3):
            near = lanes(field[k], -1)
            for c, along_x in enumerate((field[k] + near, near - field[k])):
                near_y = lanes(along_x, -16)
                for b, along_y in enumerate((along_x + near_y, near_y - along_x)):
                    near_z = rows(along_y, -1)
                    value[3 * (2 * b + c) + k] = along_y + near_z
                    value[3 * (4 + 2 * b + c) + k] = near_z - along_y
        force = [None if f is None else moduli * f for f in mode_forces(value, COARSEN)]
        result = []
        for k in range(3):
            parts_x = []
            for c in range(2):
                parts_y = []
                for b in range(2):
                    same, change = force[3 * (2 * b + c) + k], force[3 * (4 + 2 * b + c) + k]
                    if same is None:
                        parts_y.append(rows(change, 1) - change)
                    else:
                        parts_y.append(same - change + rows(same + change, 1))
                parts_x.append(parts_y[0] - parts_y[1] + lanes(parts_y[0] + parts_y[1], 16))
            result.append(parts_x[0] - parts_x[1] + lanes(parts_x[0] + parts_x[1], 1))
        return result

    bottom = BOUND / 20.0
    center = 0.5 * (BOUND + bottom)
    radius = 0.5 * (BOUND - bottom)
    sigma = center / radius
    rho = 1.0 / sigma
    update = [inverse * (s * (1.0 / center)) for s in rhs]
    correction = update
    remainder = rhs
    for sweep in range(CHEB - 1):
        image = apply(update)
        remainder = [r - a for r, a in zip(remainder, image)]
        rho_next = 1.0 / (2.0 * sigma - rho)
        update = [
            (rho_next * rho) * u + (2.0 * rho_next / radius) * (inverse * r)
            for u, r in zip(update, remainder)
        ]
        correction = [c + u for c, u in zip(correction, update)]
        rho = rho_next
    row = lax.broadcasted_iota(jnp.int32, (8, 128), 0)
    lane = lax.broadcasted_iota(jnp.int32, (8, 128), 1)
    own = row == (lane >> 4)
    for k in range(3):
        solved_ref[WINDOW * k : WINDOW * (k + 1), :] = correction[k]
    blocks = []
    for which in range(3):
        place = jnp.clip(tile - begin + which - 1, 0, WINDOW - 1)
        for k in range(3):
            line = solved_ref[pl.ds(WINDOW * k + place, 1), :]
            blocks.append(jnp.where(own, jnp.broadcast_to(line, (8, 128)), 0.0))
    spread_ref[...] = exact_dot(
        jnp.concatenate(blocks, 0), coarse_pattern(), ((1,), (1,))
    )
    return moduli


def window_begin(tile):
    return 2 * jnp.minimum(jnp.maximum(tile - 7, 0) >> 1, (128 - WINDOW) // 2)


def correction_of(spread_ref):
    def correction(n, j):
        which = jnp.where(n < H, 0, jnp.where(n < H + 8, 1, 2))
        return [
            jnp.broadcast_to(spread_ref[pl.ds((3 * which + k) * 8 + j, 1), :], (8, 128))
            for k in range(3)
        ]

    return correction


def pack_kernel(load_hbm, phases_hbm, table_ref,
                chip_hbm, link_hbm, moduli_hbm,
                phases_ref, moduli_ref, arrived, sent):
    tile = tile_index()

    def fill(top_hbm, low_hbm):
        moves = []

        def move(source, target):
            copy = pltpu.make_async_copy(source, target, sent.at[len(moves)])
            copy.start()
            moves.append(copy)

        fetch = pltpu.make_async_copy(phases_hbm, phases_ref, arrived)
        fetch.start()
        for k in range(3):
            behind = slice(5 + 3 * k, 8 + 3 * k)
            move(load_hbm.at[k, 4:7], top_hbm.at[behind])
            move(load_hbm.at[k, 1:4], low_hbm.at[behind])
            move(load_hbm.at[k, 7], top_hbm.at[k])
            move(load_hbm.at[k, 0], low_hbm.at[k])
        row = lax.broadcasted_iota(jnp.int32, (64, 128), 0)
        lane = lax.broadcasted_iota(jnp.int32, (64, 128), 1)
        interior = (row < 63) & (lane < 127)
        table = [table_ref[i] for i in range(4)]
        fetch.wait()
        for n in range(8):
            value = jnp.zeros((64, 128), jnp.float32)
            for i in range(4):
                value = jnp.where(phases_ref[n] == i, table[i], value)
            inside = interior if n < 7 else interior & (tile < 127)
            moduli_ref[n] = jnp.where(inside, value, 0.0)
        move(moduli_ref.at[6:8], top_hbm.at[3:5])
        move(moduli_ref.at[3:6], top_hbm.at[14:17])
        move(moduli_ref.at[0:2], low_hbm.at[3:5])
        move(moduli_ref.at[1:4], low_hbm.at[14:17])
        move(moduli_ref, moduli_hbm)
        for copy in moves:
            copy.wait()

    @pl.when((tile & 1) == 0)
    def even():
        fill(chip_hbm, link_hbm)

    @pl.when((tile & 1) == 1)
    def odd():
        fill(link_hbm, chip_hbm)


def inverse_of(before, value, n, keep_ref, tile):
    depth = tile * 8 + n
    both = before + value
    both = both + rows(both, 1)
    both = DIAGONAL * (both + lanes(both, 1))
    inside = jnp.where(depth == 0, jnp.float32(0.0), jnp.float32(1.0))
    held = jnp.maximum(keep_ref[...], inside)
    both = held * both + 1.0 - held
    exists = (depth >= 0) & (depth < 1024)
    both = jnp.where(exists, both, 1.0)
    return jnp.where(exists, 1.0 / both, 0.0)


def first_of(rhs_ref, inverse_ref):
    def first(n, j):
        scaled = OMEGA * inverse_ref[n, at(j), :]
        return [rhs_ref[k, n, at(j), :] * scaled for k in range(3)]

    return first


def own_kernel(load_ref, own_ref, clamp_ref,
               rhs_ref, moduli_ref, inverse_ref, keep_ref, total_ref, sum_ref,
               along_ref, x_ref):
    tile = tile_index()
    keep_ref[...] = 1.0 - clamp_ref[...].astype(jnp.float32)
    total = jnp.zeros((64, 128), jnp.float32)
    before = None
    for n in range(8):
        value = own_ref[n]
        moduli_ref[H + n] = value
        total = total + value
        if n:
            inverse_ref[H + n] = inverse_of(before, value, n, keep_ref, tile)
        before = value
    sum_ref[3] = total
    held = jnp.where(tile == 0, keep_ref[...], 1.0)
    for k in range(3):
        total = held * load_ref[k, 0]
        rhs_ref[k, H] = total
        for n in range(1, 8):
            rhs_ref[k, H + n] = load_ref[k, n]
            total = total + load_ref[k, n]
        sum_ref[k] = total
    total_ref[...] = jnp.zeros_like(total_ref)
    inverse_ref[H + 8] = jnp.zeros((64, 128), jnp.float32)
    for k in range(3):
        rhs_ref[k, H + 8] = jnp.zeros((64, 128), jnp.float32)
    begin, add = block_forces(
        first_of(rhs_ref, inverse_ref), moduli_ref, along_ref, free_of(keep_ref, tile),
        x_ref, total_ref,
    )
    begin(H + 1, H + 2)
    inner_layers(add)


def set_up(link_ref, chip_ref, own_rhs_ref, own_moduli_ref, own_inverse_ref, keep_ref,
           rhs_ref, moduli_ref, inverse_ref, tile):
    even = (tile & 1) == 0

    def below(i):
        return jnp.where(even, link_ref[i], chip_ref[i])

    def above(i):
        return jnp.where(even, chip_ref[i], link_ref[i])

    def moduli(n):
        if n < -2:
            return below(14 + n + 5)
        if n < 0:
            return below(3 + n + 2)
        if n < 8:
            return own_moduli_ref[n + H]
        if n < 9:
            return above(3)
        return above(14 + n - 9)

    def load(k, n):
        if n < -1:
            return below(5 + 3 * k + n + 4)
        if n < 0:
            return below(k)
        if n < 9:
            return above(k)
        return above(5 + 3 * k + n - 9)

    before = None
    for n in range(-5, 12):
        value = moduli(n)
        moduli_ref[n + H] = value
        if 0 < n < 8:
            inverse_ref[n + H] = own_inverse_ref[n + H]
        elif n > -5:
            inverse_ref[n + H] = inverse_of(before, value, n, keep_ref, tile)
        before = value
        if n < -4:
            continue
        for k in range(3):
            if 0 <= n < 8:
                rhs_ref[k, n + H] = own_rhs_ref[k, n + H]
            else:
                depth = tile * 8 + n
                inside = jnp.where(depth == 0, jnp.float32(0.0), jnp.float32(1.0))
                rhs_ref[k, n + H] = jnp.maximum(keep_ref[...], inside) * load(k, n)


def first_kernel(link_ref, chip_ref, own_rhs_ref, own_moduli_ref, own_inverse_ref, keep_ref,
                 inner_ref, own_sum_ref,
                 send_ref, rhs_ref, moduli_ref, inverse_ref,
                 along_ref, x_ref, total_ref, sum_ref):
    tile = tile_index()
    set_up(link_ref, chip_ref, own_rhs_ref, own_moduli_ref, own_inverse_ref, keep_ref,
           rhs_ref, moduli_ref, inverse_ref, tile)
    free = free_of(keep_ref, tile)
    total_ref[...] = inner_ref[...]
    first = first_of(rhs_ref, inverse_ref)
    begin, add = block_forces(first, moduli_ref, along_ref, free, x_ref, total_ref)
    begin(H - 1, H)
    add(H, H + 1, "below")
    add(H + 1, H + 1, "lowest")
    begin(H + 7, H + 8)
    add(H + 8, H + 8, "above")

    def lowest(j, out):
        held = free(H, j) > 0.0
        value = first(H, j)
        for k in range(3):
            image = jnp.where(held, out[k], value[k])
            sum_ref[k, at(j), :] = own_sum_ref[k, at(j), :] - image

    def others(j, out):
        for k in range(3):
            sum_ref[k, at(j), :] -= out[k]

    block_scatter(total_ref, 0, lowest)
    block_scatter(total_ref, 12, others)
    sum_ref[3] = own_sum_ref[3]
    four = block_sums(sum_ref[...].reshape(256, 128))
    lane = lax.broadcasted_iota(jnp.int32, (1, 128), 1)
    edge = (lane >= 112) | ((lane & 15) == 15) | (lax.rem(tile, GROUP) == GROUP - 1)
    four[3] = jnp.where(edge, 0.0, four[3] * (1.0 / 512.0))
    send_rows(send_ref, four)


def middle_kernel(gathered_ref, rhs_ref, moduli_ref, inverse_ref, keep_ref,
                  ahead_ref, image_ref, coarse_ref, send_ref,
                  along_ref, up_ref, x_ref, late_ref, total_ref,
                  sum_ref, dots_ref, window_ref, solved_ref, spread_ref):
    tile = tile_index()
    free = free_of(keep_ref, tile)
    coarse_ref[...] = coarse_solve(gathered_ref, None, tile, window_ref, solved_ref, spread_ref)
    correction = correction_of(spread_ref)

    def second(n, j):
        scaled = OMEGA * inverse_ref[n, at(j), :]
        held = free(n, j)
        result = []
        for k, coarse_value in enumerate(correction(n, j)):
            value = rhs_ref[k, n, at(j), :] * scaled + held * coarse_value
            result.append(value)
        return result

    def smooth(n, j, out):
        held = free(n, j) > 0.0
        scaled = OMEGA * inverse_ref[n, at(j), :]
        for k, value in enumerate(second(n, j)):
            image = jnp.where(held, out[k], value)
            ahead_ref[k, n, at(j), :] = value + (rhs_ref[k, n, at(j), :] - image) * scaled

    stiff(2, 16, second, smooth, moduli_ref, along_ref, up_ref, free, x_ref, late_ref)

    def ahead(n, j):
        return [ahead_ref[k, n, at(j), :] for k in range(3)]

    def keep_image(n, j, out):
        held = free(n, j) > 0.0
        for k in range(3):
            image_ref[k, n, at(j), :] = jnp.where(
                held, out[k], ahead_ref[k, n, at(j), :]
            )

    stiff(3, 15, ahead, keep_image, moduli_ref, along_ref, up_ref, free, x_ref, late_ref)

    total_ref[12:24] = jnp.zeros((12, 64, 128), jnp.float32)
    first = first_of(image_ref, inverse_ref)
    begin, add = block_forces(first, moduli_ref, along_ref, free, x_ref, total_ref)
    begin(H - 1, H)
    add(H, H + 1, "below")
    add(H + 1, H + 2, "lowest")
    inner_layers(add)
    add(H + 8, H + 8, "above")

    def lowest(j, out):
        held = free(H, j) > 0.0
        value = first(H, j)
        for k in range(3):
            sum_ref[k, at(j), :] = -jnp.where(held, out[k], value[k])

    def others(j, out):
        for k in range(3):
            sum_ref[k, at(j), :] -= out[k]

    block_scatter(total_ref, 0, lowest)
    block_scatter(total_ref, 12, others)
    dots_ref[...] = jnp.zeros_like(dots_ref)

    def products(n, unused):
        for k in range(3):
            by_rhs, by_image = [], []
            for j in range(8):
                image = image_ref[k, n, at(j), :]
                now = ahead_ref[k, n, at(j), :]
                sum_ref[k, at(j), :] += image
                by_rhs.append(now * rhs_ref[k, n, at(j), :])
                by_image.append(now * image)
            dots_ref[0, k] += sum(by_rhs[1:], by_rhs[0])
            dots_ref[1, k] += sum(by_image[1:], by_image[0])
        return unused

    lax.fori_loop(H, H + 8, products, 0)
    three = block_sums(sum_ref[...].reshape(192, 128))
    lane = lax.broadcasted_iota(jnp.int32, (1, 128), 1)
    gamma = jnp.sum(dots_ref[0])
    energy = jnp.sum(dots_ref[1])
    dots = jnp.where(lane == 0, gamma, jnp.where(lane == 1, energy, 0.0))
    send_rows(send_ref, three + [dots])


def lane_value(line, i):
    lane = lax.broadcasted_iota(jnp.int32, line.shape, 1)
    return jnp.sum(jnp.where(lane == i, line, 0.0))


def last_kernel(gathered_ref, rhs_ref, moduli_ref, inverse_ref, keep_ref, ahead_ref, image_ref,
                coarse_ref,
                next_ref, next_image_ref, scalars_ref, send_ref,
                whole_ref, along_ref, up_ref, x_ref, late_ref, dots_ref, window_ref, solved_ref, spread_ref):
    tile = tile_index()
    free = free_of(keep_ref, tile)
    dots = jnp.sum(gathered_ref[pl.ds(3, 128, stride=4), :], axis=0, keepdims=True)
    scalars_ref[...] = jnp.broadcast_to(dots, (8, 128))
    alpha = lane_value(dots, 0) / lane_value(dots, 1)
    coarse_solve(gathered_ref, coarse_ref, tile, window_ref, solved_ref, spread_ref)
    correction = correction_of(spread_ref)

    def second(n, j):
        scaled = OMEGA * inverse_ref[n, at(j), :]
        held = free(n, j)
        result = []
        for k, coarse_value in enumerate(correction(n, j)):
            value = image_ref[k, n, at(j), :] * scaled + held * coarse_value
            result.append(value)
        return result

    def smooth(n, j, out):
        held = free(n, j) > 0.0
        scaled = OMEGA * inverse_ref[n, at(j), :]
        for k, value in enumerate(second(n, j)):
            image = jnp.where(held, out[k], value)
            value = value + (image_ref[k, n, at(j), :] - image) * scaled
            whole_ref[k, n, at(j), :] = ahead_ref[k, n, at(j), :] - alpha * value

    stiff(4, 14, second, smooth, moduli_ref, along_ref, up_ref, free, x_ref, late_ref)
    dots_ref[...] = jnp.zeros_like(dots_ref)

    def ahead(n, j):
        return [whole_ref[k, n, at(j), :] for k in range(3)]

    def finish(n, j, out):
        held = free(n, j) > 0.0
        for k in range(3):
            value = whole_ref[k, n, at(j), :]
            image = jnp.where(held, out[k], value)
            next_ref[k, n - H, at(j), :] = value
            next_image_ref[k, n - H, at(j), :] = image
            before = image_ref[k, n, at(j), :]
            dots_ref[0, k] += value * (rhs_ref[k, n, at(j), :] - alpha * before)
            dots_ref[1, k] += value * image
            dots_ref[2, k] += value * before

    stiff(5, 13, ahead, finish, moduli_ref, along_ref, up_ref, free, x_ref, late_ref)
    lane = lax.broadcasted_iota(jnp.int32, (8, 128), 1)
    line = jnp.zeros((8, 128), jnp.float32)
    for i in range(3):
        line = jnp.where(lane == i, jnp.sum(dots_ref[i]), line)
    for i in range(16):
        send_ref[at(i), :] = line


def close_kernel(gathered_ref, scalars_ref, rhs_ref, ahead_ref, image_ref, next_ref,
                 next_image_ref, displacement_hbm, residual_hbm,
                 displacement_ref, residual_ref, sent):
    before = scalars_ref[0:1, :]
    gamma, energy = lane_value(before, 0), lane_value(before, 1)
    dots = jnp.sum(gathered_ref[...], axis=0, keepdims=True)
    following, own, cross = (lane_value(dots, i) for i in range(3))
    alpha = gamma / energy
    beta = following / gamma
    alpha_next = following / (own + 2.0 * beta * cross + beta * beta * energy)

    def step(n, unused):
        for k in range(3):
            ahead = ahead_ref[k, n + H]
            image = image_ref[k, n + H]
            direction = next_ref[k, n] + beta * ahead
            displacement_ref[k, n] = alpha * ahead + alpha_next * direction
            residual = rhs_ref[k, n + H] - alpha * image
            residual_ref[k, n] = residual - alpha_next * (next_image_ref[k, n] + beta * image)
        return unused

    copies = []
    for part in range(4):
        lax.fori_loop(2 * part, 2 * part + 2, step, 0)
        there = slice(2 * part, 2 * part + 2)
        for source, target in ((displacement_ref, displacement_hbm), (residual_ref, residual_hbm)):
            copy = pltpu.make_async_copy(
                source.at[:, there], target.at[:, there], sent.at[len(copies)]
            )
            copy.start()
            copies.append(copy)
    for copy in copies:
        copy.wait()


def call(kernel, outs, scratch, *args, smem=(), cost=None):
    spaces = [
        pl.BlockSpec(memory_space=pltpu.SMEM if i in smem else pltpu.VMEM)
        for i in range(len(args))
    ]
    return pl.pallas_call(
        kernel,
        out_shape=[jax.ShapeDtypeStruct(s, jnp.float32) for s in outs],
        in_specs=spaces,
        out_specs=[pl.BlockSpec(memory_space=pltpu.VMEM)] * len(outs),
        scratch_shapes=[pltpu.VMEM(s, jnp.float32) for s in scratch],
        cost_estimate=cost,
        compiler_params=pltpu.CompilerParams(vmem_limit_bytes=14 * 2**20),
    )(*args)


def to_all(block):
    count = block.shape[0] // 128
    parts = lax.all_to_all(block.reshape(128, count, 128), BOTH, 0, 0)
    return parts.reshape(block.shape)


def body(load, phases, clamp, phase_moduli):
    size = lax.axis_size(BOTH)
    pairs = [(i, i ^ 1) for i in range(size)]
    links = [(i, i + (1 if i % 2 else -1)) for i in range(1, size - 1)]
    plane = (64, 128)
    field = (3, EXT) + plane
    ready = [field, (EXT,) + plane, (EXT,) + plane]
    work = [(12,) + plane, (12,) + plane, (6,) + plane, (6,) + plane]
    halo = (17,) + plane
    hbm = pl.BlockSpec(memory_space=pltpu.HBM)
    to_chip, to_link, moduli_own = pl.pallas_call(
        pack_kernel,
        out_shape=[jax.ShapeDtypeStruct(s, jnp.float32) for s in (halo, halo, (8,) + plane)],
        in_specs=[hbm, hbm, pl.BlockSpec(memory_space=pltpu.SMEM)],
        out_specs=[hbm, hbm, hbm],
        scratch_shapes=[
            pltpu.VMEM(phases.shape, jnp.int32),
            pltpu.VMEM((8,) + plane, jnp.float32),
            pltpu.SemaphoreType.DMA,
            pltpu.SemaphoreType.DMA((17,)),
        ],
        compiler_params=pltpu.CompilerParams(vmem_limit_bytes=60 * 2**20),
    )(load, phases, phase_moduli)
    from_link = lax.ppermute(to_link, BOTH, links)
    from_chip = lax.ppermute(to_chip, BOTH, pairs)
    own = (3, 8) + plane
    own_rhs, own_moduli, own_inverse, keep, inner, own_sum = call(
        own_kernel, ready + [plane, (24,) + plane, (4,) + plane],
        [(12,) + plane, (6,) + plane], load, moduli_own, clamp,
        cost=pl.CostEstimate(flops=20_000_000, bytes_accessed=20_000_000, transcendentals=0),
    )
    send, rhs, moduli, inverse = call(
        first_kernel, [(512, 128)] + ready,
        [(12,) + plane, (6,) + plane, (24,) + plane, (4,) + plane],
        from_link, from_chip, own_rhs, own_moduli, own_inverse, keep, inner, own_sum,
    )
    gathered = to_all(send)
    ahead, image, coarse, send = call(
        middle_kernel,
        [field, field, (WINDOW, 128), (512, 128)],
        work + [(24,) + plane, (3,) + plane, (2, 3, 8, 128), (4 * WINDOW, 128),
                (3 * WINDOW, 128), (72, 128)],
        gathered, rhs, moduli, inverse, keep,
    )
    gathered = to_all(send)
    following, following_image, scalars, send = call(
        last_kernel,
        [own, own, (8, 128), (128, 128)],
        [field] + work + [(3, 3, 8, 128), (4 * WINDOW, 128), (3 * WINDOW, 128), (72, 128)],
        gathered, rhs, moduli, inverse, keep, ahead, image, coarse,
    )
    gathered = to_all(send)
    last = [gathered, scalars, rhs, ahead, image, following, following_image]
    displacement, residual = pl.pallas_call(
        close_kernel,
        out_shape=[jax.ShapeDtypeStruct(own, jnp.float32)] * 2,
        in_specs=[pl.BlockSpec(memory_space=pltpu.VMEM)] * len(last),
        out_specs=[hbm, hbm],
        scratch_shapes=[
            pltpu.VMEM(own, jnp.float32),
            pltpu.VMEM(own, jnp.float32),
            pltpu.SemaphoreType.DMA((8,)),
        ],
        compiler_params=pltpu.CompilerParams(vmem_limit_bytes=14 * 2**20),
    )(*last)
    return displacement, residual


def solution(mesh):
    placed = (P(None, BOTH, None, None), P(BOTH, None, None), P(), P())
    return jax.shard_map(
        body,
        mesh=mesh,
        in_specs=placed,
        out_specs=(P(None, BOTH, None, None), P(None, BOTH, None, None)),
        check_vma=False,
    )
```

```python
import functools
import math

import jax
import jax.numpy as jnp
import numpy as np
from jax import lax
from jax.experimental import pallas as pl
from jax.experimental.pallas import tpu as pltpu
from jax.sharding import PartitionSpec as P

COARSEN = 8
CHEB = 4
BOTH = ("grp", "gz")
GROUP = 32
H = 5
EXT = 17
WINDOW = 16
CORNER_OFFSETS = [(a, b, c) for a in (0, 1) for b in (0, 1) for c in (0, 1)]


def element_matrix():
    poisson = 0.3
    lame_first = poisson / ((1.0 + poisson) * (1.0 - 2.0 * poisson))
    shear = 1.0 / (2.0 * (1.0 + poisson))
    elastic = np.zeros((6, 6))
    elastic[:3, :3] = lame_first
    for axis_one in range(3):
        elastic[axis_one, axis_one] = lame_first + 2.0 * shear
        elastic[axis_one + 3, axis_one + 3] = shear
    points = [0.5 - 0.5 / math.sqrt(3.0), 0.5 + 0.5 / math.sqrt(3.0)]
    pairs = [(0, 1), (1, 2), (0, 2)]
    matrix = np.zeros((24, 24))
    for first_point in points:
        for second_point in points:
            for third_point in points:
                spot = (first_point, second_point, third_point)
                strain = np.zeros((6, 24))
                for corner, offset in enumerate(CORNER_OFFSETS):
                    values = [spot[i] if offset[i] else 1.0 - spot[i] for i in range(3)]
                    slopes = [1.0 if offset[i] else -1.0 for i in range(3)]
                    slants = []
                    for axis_one in range(3):
                        others = [values[i] for i in range(3) if i != axis_one]
                        slants.append(slopes[axis_one] * others[0] * others[1])
                        strain[axis_one, 3 * corner + axis_one] = slants[axis_one]
                    for position, pair in enumerate(pairs):
                        strain[3 + position, 3 * corner + pair[0]] = slants[pair[1]]
                        strain[3 + position, 3 * corner + pair[1]] = slants[pair[0]]
                matrix = matrix + 0.125 * (strain.T @ elastic @ strain)
    return matrix


NUMBERS = element_matrix()
BOUND = float(np.max(np.sum(np.abs(NUMBERS), axis=1) / np.diag(NUMBERS)))
OMEGA = 1.2 / BOUND
DIAGONAL = float(np.mean(np.diag(NUMBERS)))


def mode_matrix():
    haar = np.array([[1.0, 1.0], [-1.0, 1.0]])
    change = np.kron(np.kron(np.kron(haar, haar), haar), np.eye(3))
    return change @ NUMBERS @ change.T / 64.0


def mode_groups():
    modes = mode_matrix()
    near = np.abs(modes) > 1e-9
    left = [i for i in range(24) if near[i].any()]
    groups = []
    while left:
        group = [left[0]]
        for i in group:
            group += [j for j in left if near[i, j] and j not in group]
        groups.append(sorted(group))
        left = [i for i in left if i not in group]
    return modes, groups


MODES, MODE_GROUPS = mode_groups()


def mode_forces(value, scale):
    force = [None] * 24
    for group in MODE_GROUPS:
        diagonal = [float(MODES[i, i]) * scale for i in group]
        if len(group) == 1:
            force[group[0]] = diagonal[0] * value[group[0]]
            continue
        across = float(MODES[group[0], group[1]]) * scale
        apart = diagonal[0] - across
        total = value[group[0]]
        for i in group[1:]:
            total = total + value[i]
        total = across * total
        for i in group:
            if abs(apart) < 1e-9:
                force[i] = total
            else:
                force[i] = apart * value[i] + total
    return force


def lanes(value, by):
    return pltpu.roll(value, by % value.shape[1], 1)


def rows(value, by):
    return pltpu.roll(value, by % value.shape[0], 0)


def at(j):
    return slice(8 * j, 8 * j + 8)


def stiff(low, high, field, finish, moduli_ref, along_ref, up_ref, free, x_ref, late_ref):
    row = lax.broadcasted_iota(jnp.int32, (8, 128), 0)
    first_row = row == 0
    last_row = row == 7

    def x_modes(n, j):
        held = free(n, j)
        for k, value in enumerate(field(n, j)):
            value = value * held
            beside = lanes(value, -1)
            x_ref[2 * k, at(j), :] = value + beside
            x_ref[2 * k + 1, at(j), :] = beside - value

    def take(j):
        values = [x_ref[q, at(j), :] for q in range(6)]
        return values, [rows(v, -1) for v in values]

    def xy_modes(here, after):
        result = []
        for value, rolled, rolled_after in zip(here[0], here[1], after[1]):
            beside = jnp.where(last_row, rolled_after, rolled)
            result += [value + beside, beside - value]
        return result

    def flush(n, j):
        late = [late_ref[q, at(j), :] for q in range(6)]
        finish(n, j, [late[2 * k] + lanes(late[2 * k + 1], 1) for k in range(3)])

    def layer(n, stage):
        here = take(0)
        carried = [jnp.zeros((8, 128), jnp.float32)] * 6
        zero = jnp.zeros((8, 128), jnp.float32)
        for j in range(8):
            after = take(j + 1) if j < 7 else ([zero] * 6, [zero] * 6)
            now = xy_modes(here, after)
            here = after
            x_modes(jnp.minimum(n + 1, high), j)
            if stage > 2:
                flush(n - 2, j)
            before = [along_ref[q, at(j), :] for q in range(12)]
            for q in range(12):
                along_ref[q, at(j), :] = now[q]
            if stage == 0:
                continue
            weight = moduli_ref[n - 1, at(j), :]
            value = [None] * 24
            for k in range(3):
                for c in range(2):
                    for b in range(2):
                        q = 4 * k + 2 * c + b
                        value[3 * (2 * b + c) + k] = before[q] + now[q]
                        value[3 * (4 + 2 * b + c) + k] = now[q] - before[q]
            force = mode_forces(value, 1.0)
            done = {}
            weighted = []
            for i in range(24):
                f = force[i]
                if f is None:
                    weighted.append(None)
                    continue
                if id(f) not in done:
                    done[id(f)] = weight * f
                weighted.append(done[id(f)])
            totals = []
            for k in range(3):
                for c in range(2):
                    for b in range(2):
                        q = 4 * k + 2 * c + b
                        same = weighted[3 * (2 * b + c) + k]
                        change = weighted[3 * (4 + 2 * b + c) + k]
                        if stage > 1:
                            total = up_ref[q, at(j), :] - change
                            totals.append(total if same is None else total + same)
                        up_ref[q, at(j), :] = change if same is None else same + change
            if stage == 1:
                continue
            for k in range(3):
                parts = []
                for c in range(2):
                    same, change = totals[4 * k + 2 * c], totals[4 * k + 2 * c + 1]
                    over = rows(same + change, 1)
                    parts.append(same - change + jnp.where(first_row, carried[2 * k + c], over))
                    carried[2 * k + c] = over
                late_ref[2 * k, at(j), :] = parts[0] - parts[1]
                late_ref[2 * k + 1, at(j), :] = parts[0] + parts[1]

    for j in range(8):
        x_modes(low - 1, j)
    for stage in range(3):
        layer(low - 1 + stage, stage)

    def step(i, unused):
        layer(low + 2 + 2 * i, 3)
        layer(low + 3 + 2 * i, 3)
        return unused

    pairs = (high - low - 1) // 2
    lax.fori_loop(0, pairs, step, 0)
    if low + 2 + 2 * pairs == high:
        layer(high, 3)
    for j in range(8):
        flush(high - 1, j)


def block_forces(field, moduli_ref, along_ref, free, x_ref, total_ref):
    row = lax.broadcasted_iota(jnp.int32, (8, 128), 0)
    last_row = row == 7

    def x_modes(n, j):
        held = free(n, j)
        for k, value in enumerate(field(n, j)):
            value = value * held
            beside = lanes(value, -1)
            x_ref[2 * k, at(j), :] = value + beside
            x_ref[2 * k + 1, at(j), :] = beside - value

    def take(j):
        values = [x_ref[q, at(j), :] for q in range(6)]
        return values, [rows(v, -1) for v in values]

    def planes(following):
        here = take(0)
        zero = jnp.zeros((8, 128), jnp.float32)
        for j in range(8):
            after = take(j + 1) if j < 7 else ([zero] * 6, [zero] * 6)
            now = []
            for value, rolled, rolled_after in zip(here[0], here[1], after[1]):
                beside = jnp.where(last_row, rolled_after, rolled)
                now += [value + beside, beside - value]
            here = after
            x_modes(following, j)
            yield j, now

    def begin(n, following):
        for j in range(8):
            x_modes(n, j)
        for j, now in planes(following):
            for q in range(12):
                along_ref[q, at(j), :] = now[q]

    def add(n, following, kind):
        for j, now in planes(following):
            before = [along_ref[q, at(j), :] for q in range(12)]
            for q in range(12):
                along_ref[q, at(j), :] = now[q]
            weight = moduli_ref[n - 1, at(j), :]
            value = [None] * 24
            for k in range(3):
                for c in range(2):
                    for b in range(2):
                        q = 4 * k + 2 * c + b
                        value[3 * (2 * b + c) + k] = before[q] + now[q]
                        value[3 * (4 + 2 * b + c) + k] = now[q] - before[q]
            force = mode_forces(value, 1.0)
            for k in range(3):
                for c in range(2):
                    for b in range(2):
                        q = 4 * k + 2 * c + b
                        same = force[3 * (2 * b + c) + k]
                        change = force[3 * (4 + 2 * b + c) + k]
                        if kind == "inner":
                            if same is not None:
                                total_ref[12 + q, at(j), :] += (2.0 * weight) * same
                            continue
                        change = weight * change
                        same = 0.0 if same is None else weight * same
                        if kind == "below":
                            total_ref[q, at(j), :] = same + change
                        elif kind == "lowest":
                            total_ref[q, at(j), :] += same - change
                            total_ref[12 + q, at(j), :] += same + change
                        else:
                            total_ref[12 + q, at(j), :] += same - change

    return begin, add


def block_scatter(total_ref, base, finish):
    first_row = lax.broadcasted_iota(jnp.int32, (8, 128), 0) == 0
    carried = [jnp.zeros((8, 128), jnp.float32)] * 6
    for j in range(8):
        out = []
        for k in range(3):
            parts = []
            for c in range(2):
                same = total_ref[base + 4 * k + 2 * c, at(j), :]
                change = total_ref[base + 4 * k + 2 * c + 1, at(j), :]
                over = rows(same + change, 1)
                parts.append(same - change + jnp.where(first_row, carried[2 * k + c], over))
                carried[2 * k + c] = over
            out.append(parts[0] - parts[1] + lanes(parts[0] + parts[1], 1))
        finish(j, out)


def inner_layers(add):
    def step(i, unused):
        n = H + 2 + 2 * i
        add(n, n + 1, "inner")
        add(n + 1, n + 2, "inner")
        return unused

    lax.fori_loop(0, 3, step, 0)


def free_of(keep_ref, tile):
    def free(n, j):
        inside = jnp.where(tile * 8 + n == H, jnp.float32(0.0), jnp.float32(1.0))
        return jnp.maximum(keep_ref[at(j), :], inside)

    return free


def tile_index():
    return lax.axis_index("grp") * lax.axis_size("gz") + lax.axis_index("gz")


def coarse_pattern():
    fine = lax.broadcasted_iota(jnp.int32, (128, 128), 0)
    lane = lax.broadcasted_iota(jnp.int32, (128, 128), 1)
    return jnp.where((fine >> 3) == (lane & 15), 1.0, 0.0).astype(jnp.float32)


def exact_dot(a, b, contract):
    return lax.dot_general(
        a, b, (contract, ((), ())), precision=lax.Precision.HIGHEST,
        preferred_element_type=jnp.float32,
    )


def block_sums(planes):
    count = planes.shape[0] // 64
    summed = exact_dot(planes, coarse_pattern(), ((1,), (0,)))
    row = lax.broadcasted_iota(jnp.int32, (64, 128), 0)
    lane = lax.broadcasted_iota(jnp.int32, (64, 128), 1)
    own = (row >> 3) == (lane >> 4)
    return [
        jnp.sum(jnp.where(own, summed[64 * k : 64 * k + 64], 0.0), axis=0, keepdims=True)
        for k in range(count)
    ]


def send_rows(out_ref, four):
    block = jnp.concatenate(four + four, 0)
    for i in range(out_ref.shape[0] // 8):
        out_ref[at(i), :] = block


def coarse_solve(gathered_ref, coarse_ref, tile, window_ref, solved_ref, spread_ref):
    begin = window_begin(tile)
    window_ref[...] = gathered_ref[pl.ds(pl.multiple_of(4 * begin, 8), 4 * WINDOW), :]
    rhs = [window_ref[pl.ds(k, WINDOW, stride=4), :] for k in range(3)]
    if coarse_ref is None:
        moduli = window_ref[pl.ds(3, WINDOW, stride=4), :]
        row = lax.broadcasted_iota(jnp.int32, (WINDOW, 128), 0)
        moduli = jnp.where(row == WINDOW - 1, 0.0, moduli)
    else:
        moduli = coarse_ref[...]
    summed = moduli + lanes(moduli, 1)
    summed = summed + lanes(summed, 16)
    summed = DIAGONAL * COARSEN * (summed + rows(summed, 1))
    inverse = jnp.where(summed > 0.0, 1.0 / jnp.where(summed > 0.0, summed, 1.0), 0.0)

    def apply(field):
        value = [None] * 24
        for k in range(3):
            near = lanes(field[k], -1)
            for c, along_x in enumerate((field[k] + near, near - field[k])):
                near_y = lanes(along_x, -16)
                for b, along_y in enumerate((along_x + near_y, near_y - along_x)):
                    near_z = rows(along_y, -1)
                    value[3 * (2 * b + c) + k] = along_y + near_z
                    value[3 * (4 + 2 * b + c) + k] = near_z - along_y
        force = [None if f is None else moduli * f for f in mode_forces(value, COARSEN)]
        result = []
        for k in range(3):
            parts_x = []
            for c in range(2):
                parts_y = []
                for b in range(2):
                    same, change = force[3 * (2 * b + c) + k], force[3 * (4 + 2 * b + c) + k]
                    if same is None:
                        parts_y.append(rows(change, 1) - change)
                    else:
                        parts_y.append(same - change + rows(same + change, 1))
                parts_x.append(parts_y[0] - parts_y[1] + lanes(parts_y[0] + parts_y[1], 16))
            result.append(parts_x[0] - parts_x[1] + lanes(parts_x[0] + parts_x[1], 1))
        return result

    bottom = BOUND / 20.0
    center = 0.5 * (BOUND + bottom)
    radius = 0.5 * (BOUND - bottom)
    sigma = center / radius
    rho = 1.0 / sigma
    update = [inverse * (s * (1.0 / center)) for s in rhs]
    correction = update
    remainder = rhs
    for sweep in range(CHEB - 1):
        image = apply(update)
        remainder = [r - a for r, a in zip(remainder, image)]
        rho_next = 1.0 / (2.0 * sigma - rho)
        update = [
            (rho_next * rho) * u + (2.0 * rho_next / radius) * (inverse * r)
            for u, r in zip(update, remainder)
        ]
        correction = [c + u for c, u in zip(correction, update)]
        rho = rho_next
    row = lax.broadcasted_iota(jnp.int32, (8, 128), 0)
    lane = lax.broadcasted_iota(jnp.int32, (8, 128), 1)
    own = row == (lane >> 4)
    for k in range(3):
        solved_ref[WINDOW * k : WINDOW * (k + 1), :] = correction[k]
    blocks = []
    for which in range(3):
        place = jnp.clip(tile - begin + which - 1, 0, WINDOW - 1)
        for k in range(3):
            line = solved_ref[pl.ds(WINDOW * k + place, 1), :]
            blocks.append(jnp.where(own, jnp.broadcast_to(line, (8, 128)), 0.0))
    spread_ref[...] = exact_dot(
        jnp.concatenate(blocks, 0), coarse_pattern(), ((1,), (1,))
    )
    return moduli


def window_begin(tile):
    return 2 * jnp.minimum(jnp.maximum(tile - 7, 0) >> 1, (128 - WINDOW) // 2)


def correction_of(spread_ref):
    def correction(n, j):
        which = jnp.where(n < H, 0, jnp.where(n < H + 8, 1, 2))
        return [
            jnp.broadcast_to(spread_ref[pl.ds((3 * which + k) * 8 + j, 1), :], (8, 128))
            for k in range(3)
        ]

    return correction


def pack_kernel(load_hbm, phases_hbm, table_ref,
                chip_hbm, link_hbm, moduli_hbm,
                load_ref, phases_ref, moduli_ref, arrived, sent):
    tile = tile_index()

    def fill(top_hbm, low_hbm):
        moves = []

        def move(source, target):
            copy = pltpu.make_async_copy(source, target, sent.at[len(moves)])
            copy.start()
            moves.append(copy)

        fetch = pltpu.make_async_copy(phases_hbm, phases_ref, arrived.at[3])
        fetch.start()
        parts = []
        for k in range(3):
            part = pltpu.make_async_copy(load_hbm.at[k], load_ref.at[k], arrived.at[k])
            part.start()
            parts.append(part)
        row = lax.broadcasted_iota(jnp.int32, (64, 128), 0)
        lane = lax.broadcasted_iota(jnp.int32, (64, 128), 1)
        interior = (row < 63) & (lane < 127)
        table = [table_ref[i] for i in range(4)]
        fetch.wait()
        for n in range(8):
            value = jnp.zeros((64, 128), jnp.float32)
            for i in range(4):
                value = jnp.where(phases_ref[n] == i, table[i], value)
            inside = interior if n < 7 else interior & (tile < 127)
            moduli_ref[n] = jnp.where(inside, value, 0.0)
        for k in range(3):
            behind = slice(5 + 3 * k, 8 + 3 * k)
            parts[k].wait()
            move(load_ref.at[k, 4:7], top_hbm.at[behind])
            move(load_ref.at[k, 1:4], low_hbm.at[behind])
            move(load_ref.at[k, 7], top_hbm.at[k])
            move(load_ref.at[k, 0], low_hbm.at[k])
        move(moduli_ref.at[6:8], top_hbm.at[3:5])
        move(moduli_ref.at[3:6], top_hbm.at[14:17])
        move(moduli_ref.at[0:2], low_hbm.at[3:5])
        move(moduli_ref.at[1:4], low_hbm.at[14:17])
        move(moduli_ref, moduli_hbm)
        for copy in moves:
            copy.wait()

    @pl.when((tile & 1) == 0)
    def even():
        fill(chip_hbm, link_hbm)

    @pl.when((tile & 1) == 1)
    def odd():
        fill(link_hbm, chip_hbm)


def inverse_of(before, value, n, keep_ref, tile):
    depth = tile * 8 + n
    both = before + value
    both = both + rows(both, 1)
    both = DIAGONAL * (both + lanes(both, 1))
    inside = jnp.where(depth == 0, jnp.float32(0.0), jnp.float32(1.0))
    held = jnp.maximum(keep_ref[...], inside)
    both = held * both + 1.0 - held
    exists = (depth >= 0) & (depth < 1024)
    both = jnp.where(exists, both, 1.0)
    return jnp.where(exists, 1.0 / both, 0.0)


def first_of(rhs_ref, inverse_ref):
    def first(n, j):
        scaled = OMEGA * inverse_ref[n, at(j), :]
        return [rhs_ref[k, n, at(j), :] * scaled for k in range(3)]

    return first


def own_kernel(load_ref, own_ref, clamp_ref,
               rhs_ref, moduli_ref, inverse_ref, keep_ref, total_ref, sum_ref,
               along_ref, x_ref):
    tile = tile_index()
    keep_ref[...] = 1.0 - clamp_ref[...].astype(jnp.float32)
    total = jnp.zeros((64, 128), jnp.float32)
    before = None
    for n in range(8):
        value = own_ref[n]
        moduli_ref[H + n] = value
        total = total + value
        if n:
            inverse_ref[H + n] = inverse_of(before, value, n, keep_ref, tile)
        before = value
    sum_ref[3] = total
    held = jnp.where(tile == 0, keep_ref[...], 1.0)
    for k in range(3):
        total = held * load_ref[k, 0]
        rhs_ref[k, H] = total
        for n in range(1, 8):
            rhs_ref[k, H + n] = load_ref[k, n]
            total = total + load_ref[k, n]
        sum_ref[k] = total
    total_ref[...] = jnp.zeros_like(total_ref)
    inverse_ref[H + 8] = jnp.zeros((64, 128), jnp.float32)
    for k in range(3):
        rhs_ref[k, H + 8] = jnp.zeros((64, 128), jnp.float32)
    begin, add = block_forces(
        first_of(rhs_ref, inverse_ref), moduli_ref, along_ref, free_of(keep_ref, tile),
        x_ref, total_ref,
    )
    begin(H + 1, H + 2)
    inner_layers(add)


def set_up(link_ref, chip_ref, own_rhs_ref, own_moduli_ref, own_inverse_ref, keep_ref,
           rhs_ref, moduli_ref, inverse_ref, tile):
    even = (tile & 1) == 0

    def below(i):
        return jnp.where(even, link_ref[i], chip_ref[i])

    def above(i):
        return jnp.where(even, chip_ref[i], link_ref[i])

    def moduli(n):
        if n < -2:
            return below(14 + n + 5)
        if n < 0:
            return below(3 + n + 2)
        if n < 8:
            return own_moduli_ref[n + H]
        if n < 9:
            return above(3)
        return above(14 + n - 9)

    def load(k, n):
        if n < -1:
            return below(5 + 3 * k + n + 4)
        if n < 0:
            return below(k)
        if n < 9:
            return above(k)
        return above(5 + 3 * k + n - 9)

    before = None
    for n in range(-5, 12):
        value = moduli(n)
        moduli_ref[n + H] = value
        if 0 < n < 8:
            inverse_ref[n + H] = own_inverse_ref[n + H]
        elif n > -5:
            inverse_ref[n + H] = inverse_of(before, value, n, keep_ref, tile)
        before = value
        if n < -4:
            continue
        for k in range(3):
            if 0 <= n < 8:
                rhs_ref[k, n + H] = own_rhs_ref[k, n + H]
            else:
                depth = tile * 8 + n
                inside = jnp.where(depth == 0, jnp.float32(0.0), jnp.float32(1.0))
                rhs_ref[k, n + H] = jnp.maximum(keep_ref[...], inside) * load(k, n)


def first_kernel(link_ref, chip_ref, own_rhs_ref, own_moduli_ref, own_inverse_ref, keep_ref,
                 inner_ref, own_sum_ref,
                 send_ref, rhs_ref, moduli_ref, inverse_ref,
                 along_ref, x_ref, total_ref, sum_ref):
    tile = tile_index()
    set_up(link_ref, chip_ref, own_rhs_ref, own_moduli_ref, own_inverse_ref, keep_ref,
           rhs_ref, moduli_ref, inverse_ref, tile)
    free = free_of(keep_ref, tile)
    total_ref[...] = inner_ref[...]
    first = first_of(rhs_ref, inverse_ref)
    begin, add = block_forces(first, moduli_ref, along_ref, free, x_ref, total_ref)
    begin(H - 1, H)
    add(H, H + 1, "below")
    add(H + 1, H + 1, "lowest")
    begin(H + 7, H + 8)
    add(H + 8, H + 8, "above")

    def lowest(j, out):
        held = free(H, j) > 0.0
        value = first(H, j)
        for k in range(3):
            image = jnp.where(held, out[k], value[k])
            sum_ref[k, at(j), :] = own_sum_ref[k, at(j), :] - image

    def others(j, out):
        for k in range(3):
            sum_ref[k, at(j), :] -= out[k]

    block_scatter(total_ref, 0, lowest)
    block_scatter(total_ref, 12, others)
    sum_ref[3] = own_sum_ref[3]
    four = block_sums(sum_ref[...].reshape(256, 128))
    lane = lax.broadcasted_iota(jnp.int32, (1, 128), 1)
    edge = (lane >= 112) | ((lane & 15) == 15) | (lax.rem(tile, GROUP) == GROUP - 1)
    four[3] = jnp.where(edge, 0.0, four[3] * (1.0 / 512.0))
    send_rows(send_ref, four)


def middle_kernel(gathered_ref, rhs_ref, moduli_ref, inverse_ref, keep_ref,
                  ahead_ref, image_ref, coarse_ref, send_ref,
                  along_ref, up_ref, x_ref, late_ref, total_ref,
                  sum_ref, dots_ref, window_ref, solved_ref, spread_ref):
    tile = tile_index()
    free = free_of(keep_ref, tile)
    coarse_ref[...] = coarse_solve(gathered_ref, None, tile, window_ref, solved_ref, spread_ref)
    correction = correction_of(spread_ref)

    def second(n, j):
        scaled = OMEGA * inverse_ref[n, at(j), :]
        held = free(n, j)
        result = []
        for k, coarse_value in enumerate(correction(n, j)):
            value = rhs_ref[k, n, at(j), :] * scaled + held * coarse_value
            result.append(value)
        return result

    def smooth(n, j, out):
        held = free(n, j) > 0.0
        scaled = OMEGA * inverse_ref[n, at(j), :]
        for k, value in enumerate(second(n, j)):
            image = jnp.where(held, out[k], value)
            ahead_ref[k, n, at(j), :] = value + (rhs_ref[k, n, at(j), :] - image) * scaled

    stiff(2, 16, second, smooth, moduli_ref, along_ref, up_ref, free, x_ref, late_ref)

    def ahead(n, j):
        return [ahead_ref[k, n, at(j), :] for k in range(3)]

    def keep_image(n, j, out):
        held = free(n, j) > 0.0
        for k in range(3):
            image_ref[k, n, at(j), :] = jnp.where(
                held, out[k], ahead_ref[k, n, at(j), :]
            )

    stiff(3, 15, ahead, keep_image, moduli_ref, along_ref, up_ref, free, x_ref, late_ref)

    total_ref[12:24] = jnp.zeros((12, 64, 128), jnp.float32)
    first = first_of(image_ref, inverse_ref)
    begin, add = block_forces(first, moduli_ref, along_ref, free, x_ref, total_ref)
    begin(H - 1, H)
    add(H, H + 1, "below")
    add(H + 1, H + 2, "lowest")
    inner_layers(add)
    add(H + 8, H + 8, "above")

    def lowest(j, out):
        held = free(H, j) > 0.0
        value = first(H, j)
        for k in range(3):
            sum_ref[k, at(j), :] = -jnp.where(held, out[k], value[k])

    def others(j, out):
        for k in range(3):
            sum_ref[k, at(j), :] -= out[k]

    block_scatter(total_ref, 0, lowest)
    block_scatter(total_ref, 12, others)
    dots_ref[...] = jnp.zeros_like(dots_ref)

    def products(n, unused):
        for k in range(3):
            by_rhs, by_image = [], []
            for j in range(8):
                image = image_ref[k, n, at(j), :]
                now = ahead_ref[k, n, at(j), :]
                sum_ref[k, at(j), :] += image
                by_rhs.append(now * rhs_ref[k, n, at(j), :])
                by_image.append(now * image)
            dots_ref[0, k] += sum(by_rhs[1:], by_rhs[0])
            dots_ref[1, k] += sum(by_image[1:], by_image[0])
        return unused

    lax.fori_loop(H, H + 8, products, 0)
    three = block_sums(sum_ref[...].reshape(192, 128))
    lane = lax.broadcasted_iota(jnp.int32, (1, 128), 1)
    gamma = jnp.sum(dots_ref[0])
    energy = jnp.sum(dots_ref[1])
    dots = jnp.where(lane == 0, gamma, jnp.where(lane == 1, energy, 0.0))
    send_rows(send_ref, three + [dots])


def lane_value(line, i):
    lane = lax.broadcasted_iota(jnp.int32, line.shape, 1)
    return jnp.sum(jnp.where(lane == i, line, 0.0))


def last_kernel(gathered_ref, rhs_ref, moduli_ref, inverse_ref, keep_ref, ahead_ref, image_ref,
                coarse_ref,
                next_ref, next_image_ref, scalars_ref, send_ref,
                whole_ref, along_ref, up_ref, x_ref, late_ref, dots_ref, window_ref, solved_ref, spread_ref):
    tile = tile_index()
    free = free_of(keep_ref, tile)
    dots = jnp.sum(gathered_ref[pl.ds(3, 128, stride=4), :], axis=0, keepdims=True)
    scalars_ref[...] = jnp.broadcast_to(dots, (8, 128))
    alpha = lane_value(dots, 0) / lane_value(dots, 1)
    coarse_solve(gathered_ref, coarse_ref, tile, window_ref, solved_ref, spread_ref)
    correction = correction_of(spread_ref)

    def second(n, j):
        scaled = OMEGA * inverse_ref[n, at(j), :]
        held = free(n, j)
        result = []
        for k, coarse_value in enumerate(correction(n, j)):
            value = image_ref[k, n, at(j), :] * scaled + held * coarse_value
            result.append(value)
        return result

    def smooth(n, j, out):
        held = free(n, j) > 0.0
        scaled = OMEGA * inverse_ref[n, at(j), :]
        for k, value in enumerate(second(n, j)):
            image = jnp.where(held, out[k], value)
            value = value + (image_ref[k, n, at(j), :] - image) * scaled
            whole_ref[k, n, at(j), :] = ahead_ref[k, n, at(j), :] - alpha * value

    stiff(4, 14, second, smooth, moduli_ref, along_ref, up_ref, free, x_ref, late_ref)
    dots_ref[...] = jnp.zeros_like(dots_ref)

    def ahead(n, j):
        return [whole_ref[k, n, at(j), :] for k in range(3)]

    def finish(n, j, out):
        held = free(n, j) > 0.0
        for k in range(3):
            value = whole_ref[k, n, at(j), :]
            image = jnp.where(held, out[k], value)
            next_ref[k, n - H, at(j), :] = value
            next_image_ref[k, n - H, at(j), :] = image
            before = image_ref[k, n, at(j), :]
            dots_ref[0, k] += value * (rhs_ref[k, n, at(j), :] - alpha * before)
            dots_ref[1, k] += value * image
            dots_ref[2, k] += value * before

    stiff(5, 13, ahead, finish, moduli_ref, along_ref, up_ref, free, x_ref, late_ref)
    lane = lax.broadcasted_iota(jnp.int32, (8, 128), 1)
    line = jnp.zeros((8, 128), jnp.float32)
    for i in range(3):
        line = jnp.where(lane == i, jnp.sum(dots_ref[i]), line)
    for i in range(16):
        send_ref[at(i), :] = line


def close_kernel(gathered_ref, scalars_ref, rhs_ref, ahead_ref, image_ref, next_ref,
                 next_image_ref, displacement_hbm, residual_hbm,
                 displacement_ref, residual_ref, sent):
    before = scalars_ref[0:1, :]
    gamma, energy = lane_value(before, 0), lane_value(before, 1)
    dots = jnp.sum(gathered_ref[...], axis=0, keepdims=True)
    following, own, cross = (lane_value(dots, i) for i in range(3))
    alpha = gamma / energy
    beta = following / gamma
    alpha_next = following / (own + 2.0 * beta * cross + beta * beta * energy)

    def step(n, unused):
        for k in range(3):
            ahead = ahead_ref[k, n + H]
            image = image_ref[k, n + H]
            direction = next_ref[k, n] + beta * ahead
            displacement_ref[k, n] = alpha * ahead + alpha_next * direction
            residual = rhs_ref[k, n + H] - alpha * image
            residual_ref[k, n] = residual - alpha_next * (next_image_ref[k, n] + beta * image)
        return unused

    copies = []
    for part in range(4):
        lax.fori_loop(2 * part, 2 * part + 2, step, 0)
        there = slice(2 * part, 2 * part + 2)
        for source, target in ((displacement_ref, displacement_hbm), (residual_ref, residual_hbm)):
            copy = pltpu.make_async_copy(
                source.at[:, there], target.at[:, there], sent.at[len(copies)]
            )
            copy.start()
            copies.append(copy)
    for copy in copies:
        copy.wait()


def call(kernel, outs, scratch, *args, smem=(), cost=None):
    spaces = [
        pl.BlockSpec(memory_space=pltpu.SMEM if i in smem else pltpu.VMEM)
        for i in range(len(args))
    ]
    return pl.pallas_call(
        kernel,
        out_shape=[jax.ShapeDtypeStruct(s, jnp.float32) for s in outs],
        in_specs=spaces,
        out_specs=[pl.BlockSpec(memory_space=pltpu.VMEM)] * len(outs),
        scratch_shapes=[pltpu.VMEM(s, jnp.float32) for s in scratch],
        cost_estimate=cost,
        compiler_params=pltpu.CompilerParams(vmem_limit_bytes=14 * 2**20),
    )(*args)


def to_all(block):
    count = block.shape[0] // 128
    parts = lax.all_to_all(block.reshape(128, count, 128), BOTH, 0, 0)
    return parts.reshape(block.shape)


def body(load, phases, clamp, phase_moduli):
    size = lax.axis_size(BOTH)
    pairs = [(i, i ^ 1) for i in range(size)]
    links = [(i, i + (1 if i % 2 else -1)) for i in range(1, size - 1)]
    plane = (64, 128)
    field = (3, EXT) + plane
    ready = [field, (EXT,) + plane, (EXT,) + plane]
    work = [(12,) + plane, (12,) + plane, (6,) + plane, (6,) + plane]
    halo = (17,) + plane
    hbm = pl.BlockSpec(memory_space=pltpu.HBM)
    to_chip, to_link, moduli_own = pl.pallas_call(
        pack_kernel,
        out_shape=[jax.ShapeDtypeStruct(s, jnp.float32) for s in (halo, halo, (8,) + plane)],
        in_specs=[hbm, hbm, pl.BlockSpec(memory_space=pltpu.SMEM)],
        out_specs=[hbm, hbm, hbm],
        scratch_shapes=[
            pltpu.VMEM(load.shape, jnp.float32),
            pltpu.VMEM(phases.shape, jnp.int32),
            pltpu.VMEM((8,) + plane, jnp.float32),
            pltpu.SemaphoreType.DMA((4,)),
            pltpu.SemaphoreType.DMA((17,)),
        ],
        compiler_params=pltpu.CompilerParams(vmem_limit_bytes=60 * 2**20),
    )(load, phases, phase_moduli)
    from_link = lax.ppermute(to_link, BOTH, links)
    from_chip = lax.ppermute(to_chip, BOTH, pairs)
    own = (3, 8) + plane
    own_rhs, own_moduli, own_inverse, keep, inner, own_sum = call(
        own_kernel, ready + [plane, (24,) + plane, (4,) + plane],
        [(12,) + plane, (6,) + plane], load, moduli_own, clamp,
        cost=pl.CostEstimate(flops=20_000_000, bytes_accessed=20_000_000, transcendentals=0),
    )
    send, rhs, moduli, inverse = call(
        first_kernel, [(512, 128)] + ready,
        [(12,) + plane, (6,) + plane, (24,) + plane, (4,) + plane],
        from_link, from_chip, own_rhs, own_moduli, own_inverse, keep, inner, own_sum,
    )
    gathered = to_all(send)
    ahead, image, coarse, send = call(
        middle_kernel,
        [field, field, (WINDOW, 128), (512, 128)],
        work + [(24,) + plane, (3,) + plane, (2, 3, 8, 128), (4 * WINDOW, 128),
                (3 * WINDOW, 128), (72, 128)],
        gathered, rhs, moduli, inverse, keep,
    )
    gathered = to_all(send)
    following, following_image, scalars, send = call(
        last_kernel,
        [own, own, (8, 128), (128, 128)],
        [field] + work + [(3, 3, 8, 128), (4 * WINDOW, 128), (3 * WINDOW, 128), (72, 128)],
        gathered, rhs, moduli, inverse, keep, ahead, image, coarse,
    )
    gathered = to_all(send)
    last = [gathered, scalars, rhs, ahead, image, following, following_image]
    displacement, residual = pl.pallas_call(
        close_kernel,
        out_shape=[jax.ShapeDtypeStruct(own, jnp.float32)] * 2,
        in_specs=[pl.BlockSpec(memory_space=pltpu.VMEM)] * len(last),
        out_specs=[hbm, hbm],
        scratch_shapes=[
            pltpu.VMEM(own, jnp.float32),
            pltpu.VMEM(own, jnp.float32),
            pltpu.SemaphoreType.DMA((8,)),
        ],
        compiler_params=pltpu.CompilerParams(vmem_limit_bytes=14 * 2**20),
    )(*last)
    return displacement, residual


def solution(mesh):
    placed = (P(None, BOTH, None, None), P(BOTH, None, None), P(), P())
    return jax.shard_map(
        body,
        mesh=mesh,
        in_specs=placed,
        out_specs=(P(None, BOTH, None, None), P(None, BOTH, None, None)),
        check_vma=False,
    )
```

```python
import functools
import math

import jax
import jax.numpy as jnp
import numpy as np
from jax import lax
from jax.experimental import pallas as pl
from jax.experimental.pallas import tpu as pltpu
from jax.sharding import PartitionSpec as P

COARSEN = 8
CHEB = 4
BOTH = ("grp", "gz")
GROUP = 32
H = 5
EXT = 17
WINDOW = 16
CORNER_OFFSETS = [(a, b, c) for a in (0, 1) for b in (0, 1) for c in (0, 1)]


def element_matrix():
    poisson = 0.3
    lame_first = poisson / ((1.0 + poisson) * (1.0 - 2.0 * poisson))
    shear = 1.0 / (2.0 * (1.0 + poisson))
    elastic = np.zeros((6, 6))
    elastic[:3, :3] = lame_first
    for axis_one in range(3):
        elastic[axis_one, axis_one] = lame_first + 2.0 * shear
        elastic[axis_one + 3, axis_one + 3] = shear
    points = [0.5 - 0.5 / math.sqrt(3.0), 0.5 + 0.5 / math.sqrt(3.0)]
    pairs = [(0, 1), (1, 2), (0, 2)]
    matrix = np.zeros((24, 24))
    for first_point in points:
        for second_point in points:
            for third_point in points:
                spot = (first_point, second_point, third_point)
                strain = np.zeros((6, 24))
                for corner, offset in enumerate(CORNER_OFFSETS):
                    values = [spot[i] if offset[i] else 1.0 - spot[i] for i in range(3)]
                    slopes = [1.0 if offset[i] else -1.0 for i in range(3)]
                    slants = []
                    for axis_one in range(3):
                        others = [values[i] for i in range(3) if i != axis_one]
                        slants.append(slopes[axis_one] * others[0] * others[1])
                        strain[axis_one, 3 * corner + axis_one] = slants[axis_one]
                    for position, pair in enumerate(pairs):
                        strain[3 + position, 3 * corner + pair[0]] = slants[pair[1]]
                        strain[3 + position, 3 * corner + pair[1]] = slants[pair[0]]
                matrix = matrix + 0.125 * (strain.T @ elastic @ strain)
    return matrix


NUMBERS = element_matrix()
BOUND = float(np.max(np.sum(np.abs(NUMBERS), axis=1) / np.diag(NUMBERS)))
OMEGA = 1.2 / BOUND
DIAGONAL = float(np.mean(np.diag(NUMBERS)))


def mode_matrix():
    haar = np.array([[1.0, 1.0], [-1.0, 1.0]])
    change = np.kron(np.kron(np.kron(haar, haar), haar), np.eye(3))
    return change @ NUMBERS @ change.T / 64.0


def mode_groups():
    modes = mode_matrix()
    near = np.abs(modes) > 1e-9
    left = [i for i in range(24) if near[i].any()]
    groups = []
    while left:
        group = [left[0]]
        for i in group:
            group += [j for j in left if near[i, j] and j not in group]
        groups.append(sorted(group))
        left = [i for i in left if i not in group]
    return modes, groups


MODES, MODE_GROUPS = mode_groups()


def mode_forces(value, scale):
    force = [None] * 24
    for group in MODE_GROUPS:
        diagonal = [float(MODES[i, i]) * scale for i in group]
        if len(group) == 1:
            force[group[0]] = diagonal[0] * value[group[0]]
            continue
        across = float(MODES[group[0], group[1]]) * scale
        apart = diagonal[0] - across
        total = value[group[0]]
        for i in group[1:]:
            total = total + value[i]
        total = across * total
        for i in group:
            if abs(apart) < 1e-9:
                force[i] = total
            else:
                force[i] = apart * value[i] + total
    return force


def lanes(value, by):
    return pltpu.roll(value, by % value.shape[1], 1)


def rows(value, by):
    return pltpu.roll(value, by % value.shape[0], 0)


def at(j):
    return slice(8 * j, 8 * j + 8)


def stiff(low, high, field, finish, moduli_ref, along_ref, up_ref, free, x_ref, late_ref):
    row = lax.broadcasted_iota(jnp.int32, (8, 128), 0)
    first_row = row == 0
    last_row = row == 7

    def x_modes(n, j):
        held = free(n, j)
        for k, value in enumerate(field(n, j)):
            value = value * held
            beside = lanes(value, -1)
            x_ref[2 * k, at(j), :] = value + beside
            x_ref[2 * k + 1, at(j), :] = beside - value

    def take(j):
        values = [x_ref[q, at(j), :] for q in range(6)]
        return values, [rows(v, -1) for v in values]

    def xy_modes(here, after):
        result = []
        for value, rolled, rolled_after in zip(here[0], here[1], after[1]):
            beside = jnp.where(last_row, rolled_after, rolled)
            result += [value + beside, beside - value]
        return result

    def flush(n, j):
        late = [late_ref[q, at(j), :] for q in range(6)]
        finish(n, j, [late[2 * k] + lanes(late[2 * k + 1], 1) for k in range(3)])

    def layer(n, stage):
        here = take(0)
        carried = [jnp.zeros((8, 128), jnp.float32)] * 6
        zero = jnp.zeros((8, 128), jnp.float32)
        for j in range(8):
            after = take(j + 1) if j < 7 else ([zero] * 6, [zero] * 6)
            now = xy_modes(here, after)
            here = after
            x_modes(jnp.minimum(n + 1, high), j)
            if stage > 2:
                flush(n - 2, j)
            before = [along_ref[q, at(j), :] for q in range(12)]
            for q in range(12):
                along_ref[q, at(j), :] = now[q]
            if stage == 0:
                continue
            weight = moduli_ref[n - 1, at(j), :]
            value = [None] * 24
            for k in range(3):
                for c in range(2):
                    for b in range(2):
                        q = 4 * k + 2 * c + b
                        value[3 * (2 * b + c) + k] = before[q] + now[q]
                        value[3 * (4 + 2 * b + c) + k] = now[q] - before[q]
            force = mode_forces(value, 1.0)
            done = {}
            weighted = []
            for i in range(24):
                f = force[i]
                if f is None:
                    weighted.append(None)
                    continue
                if id(f) not in done:
                    done[id(f)] = weight * f
                weighted.append(done[id(f)])
            totals = []
            for k in range(3):
                for c in range(2):
                    for b in range(2):
                        q = 4 * k + 2 * c + b
                        same = weighted[3 * (2 * b + c) + k]
                        change = weighted[3 * (4 + 2 * b + c) + k]
                        if stage > 1:
                            total = up_ref[q, at(j), :] - change
                            totals.append(total if same is None else total + same)
                        up_ref[q, at(j), :] = change if same is None else same + change
            if stage == 1:
                continue
            for k in range(3):
                parts = []
                for c in range(2):
                    same, change = totals[4 * k + 2 * c], totals[4 * k + 2 * c + 1]
                    over = rows(same + change, 1)
                    parts.append(same - change + jnp.where(first_row, carried[2 * k + c], over))
                    carried[2 * k + c] = over
                late_ref[2 * k, at(j), :] = parts[0] - parts[1]
                late_ref[2 * k + 1, at(j), :] = parts[0] + parts[1]

    for j in range(8):
        x_modes(low - 1, j)
    for stage in range(3):
        layer(low - 1 + stage, stage)

    def step(i, unused):
        layer(low + 2 + 2 * i, 3)
        layer(low + 3 + 2 * i, 3)
        return unused

    pairs = (high - low - 1) // 2
    lax.fori_loop(0, pairs, step, 0)
    if low + 2 + 2 * pairs == high:
        layer(high, 3)
    for j in range(8):
        flush(high - 1, j)


def block_forces(field, moduli_ref, along_ref, free, x_ref, total_ref):
    row = lax.broadcasted_iota(jnp.int32, (8, 128), 0)
    last_row = row == 7

    def x_modes(n, j):
        held = free(n, j)
        for k, value in enumerate(field(n, j)):
            value = value * held
            beside = lanes(value, -1)
            x_ref[2 * k, at(j), :] = value + beside
            x_ref[2 * k + 1, at(j), :] = beside - value

    def take(j):
        values = [x_ref[q, at(j), :] for q in range(6)]
        return values, [rows(v, -1) for v in values]

    def planes(following):
        here = take(0)
        zero = jnp.zeros((8, 128), jnp.float32)
        for j in range(8):
            after = take(j + 1) if j < 7 else ([zero] * 6, [zero] * 6)
            now = []
            for value, rolled, rolled_after in zip(here[0], here[1], after[1]):
                beside = jnp.where(last_row, rolled_after, rolled)
                now += [value + beside, beside - value]
            here = after
            x_modes(following, j)
            yield j, now

    def begin(n, following):
        for j in range(8):
            x_modes(n, j)
        for j, now in planes(following):
            for q in range(12):
                along_ref[q, at(j), :] = now[q]

    def add(n, following, kind):
        for j, now in planes(following):
            before = [along_ref[q, at(j), :] for q in range(12)]
            for q in range(12):
                along_ref[q, at(j), :] = now[q]
            weight = moduli_ref[n - 1, at(j), :]
            value = [None] * 24
            for k in range(3):
                for c in range(2):
                    for b in range(2):
                        q = 4 * k + 2 * c + b
                        value[3 * (2 * b + c) + k] = before[q] + now[q]
                        value[3 * (4 + 2 * b + c) + k] = now[q] - before[q]
            force = mode_forces(value, 1.0)
            for k in range(3):
                for c in range(2):
                    for b in range(2):
                        q = 4 * k + 2 * c + b
                        same = force[3 * (2 * b + c) + k]
                        change = force[3 * (4 + 2 * b + c) + k]
                        if kind == "inner":
                            if same is not None:
                                total_ref[12 + q, at(j), :] += (2.0 * weight) * same
                            continue
                        change = weight * change
                        same = 0.0 if same is None else weight * same
                        if kind == "below":
                            total_ref[q, at(j), :] = same + change
                        elif kind == "lowest":
                            total_ref[q, at(j), :] += same - change
                            total_ref[12 + q, at(j), :] += same + change
                        else:
                            total_ref[12 + q, at(j), :] += same - change

    return begin, add


def block_scatter(total_ref, base, finish):
    first_row = lax.broadcasted_iota(jnp.int32, (8, 128), 0) == 0
    carried = [jnp.zeros((8, 128), jnp.float32)] * 6
    for j in range(8):
        out = []
        for k in range(3):
            parts = []
            for c in range(2):
                same = total_ref[base + 4 * k + 2 * c, at(j), :]
                change = total_ref[base + 4 * k + 2 * c + 1, at(j), :]
                over = rows(same + change, 1)
                parts.append(same - change + jnp.where(first_row, carried[2 * k + c], over))
                carried[2 * k + c] = over
            out.append(parts[0] - parts[1] + lanes(parts[0] + parts[1], 1))
        finish(j, out)


def inner_layers(add):
    def step(i, unused):
        n = H + 2 + 2 * i
        add(n, n + 1, "inner")
        add(n + 1, n + 2, "inner")
        return unused

    lax.fori_loop(0, 3, step, 0)


def free_of(keep_ref, tile):
    def free(n, j):
        inside = jnp.where(tile * 8 + n == H, jnp.float32(0.0), jnp.float32(1.0))
        return jnp.maximum(keep_ref[at(j), :], inside)

    return free


def tile_index():
    return lax.axis_index("grp") * lax.axis_size("gz") + lax.axis_index("gz")


def coarse_pattern():
    fine = lax.broadcasted_iota(jnp.int32, (128, 128), 0)
    lane = lax.broadcasted_iota(jnp.int32, (128, 128), 1)
    return jnp.where((fine >> 3) == (lane & 15), 1.0, 0.0).astype(jnp.float32)


def exact_dot(a, b, contract):
    return lax.dot_general(
        a, b, (contract, ((), ())), precision=lax.Precision.HIGHEST,
        preferred_element_type=jnp.float32,
    )


def block_sums(planes):
    count = planes.shape[0] // 64
    summed = exact_dot(planes, coarse_pattern(), ((1,), (0,)))
    row = lax.broadcasted_iota(jnp.int32, (64, 128), 0)
    lane = lax.broadcasted_iota(jnp.int32, (64, 128), 1)
    own = (row >> 3) == (lane >> 4)
    return [
        jnp.sum(jnp.where(own, summed[64 * k : 64 * k + 64], 0.0), axis=0, keepdims=True)
        for k in range(count)
    ]


def send_rows(out_ref, four):
    block = jnp.concatenate(four + four, 0)
    for i in range(out_ref.shape[0] // 8):
        out_ref[at(i), :] = block


def coarse_solve(gathered_ref, coarse_ref, tile, window_ref, solved_ref, spread_ref):
    begin = window_begin(tile)
    window_ref[...] = gathered_ref[pl.ds(pl.multiple_of(4 * begin, 8), 4 * WINDOW), :]
    rhs = [window_ref[pl.ds(k, WINDOW, stride=4), :] for k in range(3)]
    if coarse_ref is None:
        moduli = window_ref[pl.ds(3, WINDOW, stride=4), :]
        row = lax.broadcasted_iota(jnp.int32, (WINDOW, 128), 0)
        moduli = jnp.where(row == WINDOW - 1, 0.0, moduli)
    else:
        moduli = coarse_ref[...]
    summed = moduli + lanes(moduli, 1)
    summed = summed + lanes(summed, 16)
    summed = DIAGONAL * COARSEN * (summed + rows(summed, 1))
    inverse = jnp.where(summed > 0.0, 1.0 / jnp.where(summed > 0.0, summed, 1.0), 0.0)

    def apply(field):
        value = [None] * 24
        for k in range(3):
            near = lanes(field[k], -1)
            for c, along_x in enumerate((field[k] + near, near - field[k])):
                near_y = lanes(along_x, -16)
                for b, along_y in enumerate((along_x + near_y, near_y - along_x)):
                    near_z = rows(along_y, -1)
                    value[3 * (2 * b + c) + k] = along_y + near_z
                    value[3 * (4 + 2 * b + c) + k] = near_z - along_y
        force = [None if f is None else moduli * f for f in mode_forces(value, COARSEN)]
        result = []
        for k in range(3):
            parts_x = []
            for c in range(2):
                parts_y = []
                for b in range(2):
                    same, change = force[3 * (2 * b + c) + k], force[3 * (4 + 2 * b + c) + k]
                    if same is None:
                        parts_y.append(rows(change, 1) - change)
                    else:
                        parts_y.append(same - change + rows(same + change, 1))
                parts_x.append(parts_y[0] - parts_y[1] + lanes(parts_y[0] + parts_y[1], 16))
            result.append(parts_x[0] - parts_x[1] + lanes(parts_x[0] + parts_x[1], 1))
        return result

    bottom = BOUND / 20.0
    center = 0.5 * (BOUND + bottom)
    radius = 0.5 * (BOUND - bottom)
    sigma = center / radius
    rho = 1.0 / sigma
    update = [inverse * (s * (1.0 / center)) for s in rhs]
    correction = update
    remainder = rhs
    for sweep in range(CHEB - 1):
        image = apply(update)
        remainder = [r - a for r, a in zip(remainder, image)]
        rho_next = 1.0 / (2.0 * sigma - rho)
        update = [
            (rho_next * rho) * u + (2.0 * rho_next / radius) * (inverse * r)
            for u, r in zip(update, remainder)
        ]
        correction = [c + u for c, u in zip(correction, update)]
        rho = rho_next
    row = lax.broadcasted_iota(jnp.int32, (8, 128), 0)
    lane = lax.broadcasted_iota(jnp.int32, (8, 128), 1)
    own = row == (lane >> 4)
    for k in range(3):
        solved_ref[WINDOW * k : WINDOW * (k + 1), :] = correction[k]
    blocks = []
    for which in range(3):
        place = jnp.clip(tile - begin + which - 1, 0, WINDOW - 1)
        for k in range(3):
            line = solved_ref[pl.ds(WINDOW * k + place, 1), :]
            blocks.append(jnp.where(own, jnp.broadcast_to(line, (8, 128)), 0.0))
    spread_ref[...] = exact_dot(
        jnp.concatenate(blocks, 0), coarse_pattern(), ((1,), (1,))
    )
    return moduli


def window_begin(tile):
    return 2 * jnp.minimum(jnp.maximum(tile - 7, 0) >> 1, (128 - WINDOW) // 2)


def correction_of(spread_ref):
    def correction(n, j):
        which = jnp.where(n < H, 0, jnp.where(n < H + 8, 1, 2))
        return [
            jnp.broadcast_to(spread_ref[pl.ds((3 * which + k) * 8 + j, 1), :], (8, 128))
            for k in range(3)
        ]

    return correction


def pack_kernel(load_hbm, phases_hbm, table_ref,
                chip_hbm, near_hbm, far_hbm, moduli_hbm,
                load_ref, phases_ref, moduli_ref, arrived, sent):
    tile = tile_index()

    def chip(first, last):
        return chip_hbm.at[first:last]

    def link(first, last):
        return near_hbm.at[first:last] if last <= 5 else far_hbm.at[first - 5 : last - 5]

    def fill(top, low):
        moves = []

        def move(source, target):
            copy = pltpu.make_async_copy(source, target, sent.at[len(moves)])
            copy.start()
            moves.append(copy)

        fetch = pltpu.make_async_copy(phases_hbm, phases_ref, arrived.at[3])
        fetch.start()
        parts = []
        for k in range(3):
            part = pltpu.make_async_copy(load_hbm.at[k], load_ref.at[k], arrived.at[k])
            part.start()
            parts.append(part)
        row = lax.broadcasted_iota(jnp.int32, (64, 128), 0)
        lane = lax.broadcasted_iota(jnp.int32, (64, 128), 1)
        interior = (row < 63) & (lane < 127)
        table = [table_ref[i] for i in range(4)]
        fetch.wait()
        for n in range(8):
            value = jnp.zeros((64, 128), jnp.float32)
            for i in range(4):
                value = jnp.where(phases_ref[n] == i, table[i], value)
            inside = interior if n < 7 else interior & (tile < 127)
            moduli_ref[n] = jnp.where(inside, value, 0.0)
        for k in range(3):
            parts[k].wait()
            move(load_ref.at[k, 7:8], top(k, k + 1))
            move(load_ref.at[k, 0:1], low(k, k + 1))
            move(load_ref.at[k, 4:7], top(5 + 3 * k, 8 + 3 * k))
            move(load_ref.at[k, 1:4], low(5 + 3 * k, 8 + 3 * k))
        move(moduli_ref.at[6:8], top(3, 5))
        move(moduli_ref.at[0:2], low(3, 5))
        move(moduli_ref.at[3:6], top(14, 17))
        move(moduli_ref.at[1:4], low(14, 17))
        move(moduli_ref, moduli_hbm)
        for copy in moves:
            copy.wait()

    @pl.when((tile & 1) == 0)
    def even():
        fill(chip, link)

    @pl.when((tile & 1) == 1)
    def odd():
        fill(link, chip)


def inverse_of(before, value, n, keep_ref, tile):
    depth = tile * 8 + n
    both = before + value
    both = both + rows(both, 1)
    both = DIAGONAL * (both + lanes(both, 1))
    inside = jnp.where(depth == 0, jnp.float32(0.0), jnp.float32(1.0))
    held = jnp.maximum(keep_ref[...], inside)
    both = held * both + 1.0 - held
    exists = (depth >= 0) & (depth < 1024)
    both = jnp.where(exists, both, 1.0)
    return jnp.where(exists, 1.0 / both, 0.0)


def first_of(rhs_ref, inverse_ref):
    def first(n, j):
        scaled = OMEGA * inverse_ref[n, at(j), :]
        return [rhs_ref[k, n, at(j), :] * scaled for k in range(3)]

    return first


def own_kernel(load_ref, own_ref, clamp_ref,
               rhs_ref, moduli_ref, inverse_ref, keep_ref, total_ref, sum_ref,
               along_ref, x_ref):
    tile = tile_index()
    keep_ref[...] = 1.0 - clamp_ref[...].astype(jnp.float32)
    total = jnp.zeros((64, 128), jnp.float32)
    before = None
    for n in range(8):
        value = own_ref[n]
        moduli_ref[H + n] = value
        total = total + value
        if n:
            inverse_ref[H + n] = inverse_of(before, value, n, keep_ref, tile)
        before = value
    sum_ref[3] = total
    held = jnp.where(tile == 0, keep_ref[...], 1.0)
    for k in range(3):
        total = held * load_ref[k, 0]
        rhs_ref[k, H] = total
        for n in range(1, 8):
            rhs_ref[k, H + n] = load_ref[k, n]
            total = total + load_ref[k, n]
        sum_ref[k] = total
    total_ref[...] = jnp.zeros_like(total_ref)
    inverse_ref[H + 8] = jnp.zeros((64, 128), jnp.float32)
    for k in range(3):
        rhs_ref[k, H + 8] = jnp.zeros((64, 128), jnp.float32)
    begin, add = block_forces(
        first_of(rhs_ref, inverse_ref), moduli_ref, along_ref, free_of(keep_ref, tile),
        x_ref, total_ref,
    )
    begin(H + 1, H + 2)
    inner_layers(add)


def set_up(low, high, near_ref, far_ref, chip_ref, own_rhs_ref, own_moduli_ref, own_inverse_ref, keep_ref,
           rhs_ref, moduli_ref, inverse_ref, tile):
    even = (tile & 1) == 0

    def link(i):
        return near_ref[i] if i < 5 else far_ref[i - 5]

    def below(i):
        return jnp.where(even, link(i), chip_ref[i])

    def above(i):
        return jnp.where(even, chip_ref[i], link(i))

    def moduli(n):
        if n < -2:
            return below(14 + n + 5)
        if n < 0:
            return below(3 + n + 2)
        if n < 8:
            return own_moduli_ref[n + H]
        if n < 9:
            return above(3)
        return above(14 + n - 9)

    def load(k, n):
        if n < -1:
            return below(5 + 3 * k + n + 4)
        if n < 0:
            return below(k)
        if n < 9:
            return above(k)
        return above(5 + 3 * k + n - 9)

    before = None
    for n in range(low - 1, high):
        value = moduli(n)
        moduli_ref[n + H] = value
        if 0 < n < 8:
            inverse_ref[n + H] = own_inverse_ref[n + H]
        elif n >= low:
            inverse_ref[n + H] = inverse_of(before, value, n, keep_ref, tile)
        before = value
        if n < low:
            continue
        for k in range(3):
            if 0 <= n < 8:
                rhs_ref[k, n + H] = own_rhs_ref[k, n + H]
            else:
                depth = tile * 8 + n
                inside = jnp.where(depth == 0, jnp.float32(0.0), jnp.float32(1.0))
                rhs_ref[k, n + H] = jnp.maximum(keep_ref[...], inside) * load(k, n)


def first_kernel(near_ref, chip_ref, own_rhs_ref, own_moduli_ref, own_inverse_ref, keep_ref,
                 inner_ref, own_sum_ref,
                 send_ref,
                 rhs_ref, moduli_ref, inverse_ref, along_ref, x_ref, total_ref, sum_ref):
    tile = tile_index()
    set_up(-1, 9, near_ref, None, chip_ref, own_rhs_ref, own_moduli_ref, own_inverse_ref,
           keep_ref, rhs_ref, moduli_ref, inverse_ref, tile)
    free = free_of(keep_ref, tile)
    total_ref[...] = inner_ref[...]
    first = first_of(rhs_ref, inverse_ref)
    begin, add = block_forces(first, moduli_ref, along_ref, free, x_ref, total_ref)
    begin(H - 1, H)
    add(H, H + 1, "below")
    add(H + 1, H + 1, "lowest")
    begin(H + 7, H + 8)
    add(H + 8, H + 8, "above")

    def lowest(j, out):
        held = free(H, j) > 0.0
        value = first(H, j)
        for k in range(3):
            image = jnp.where(held, out[k], value[k])
            sum_ref[k, at(j), :] = own_sum_ref[k, at(j), :] - image

    def others(j, out):
        for k in range(3):
            sum_ref[k, at(j), :] -= out[k]

    block_scatter(total_ref, 0, lowest)
    block_scatter(total_ref, 12, others)
    sum_ref[3] = own_sum_ref[3]
    four = block_sums(sum_ref[...].reshape(256, 128))
    lane = lax.broadcasted_iota(jnp.int32, (1, 128), 1)
    edge = (lane >= 112) | ((lane & 15) == 15) | (lax.rem(tile, GROUP) == GROUP - 1)
    four[3] = jnp.where(edge, 0.0, four[3] * (1.0 / 512.0))
    send_rows(send_ref, four)


def middle_kernel(gathered_ref, near_ref, far_ref, chip_ref, own_rhs_ref, own_moduli_ref,
                  own_inverse_ref, keep_ref,
                  ahead_ref, image_ref, coarse_ref, send_ref, rhs_ref, moduli_ref, inverse_ref,
                  along_ref, up_ref, x_ref, late_ref, total_ref,
                  sum_ref, dots_ref, window_ref, solved_ref, spread_ref):
    tile = tile_index()
    set_up(-4, 12, near_ref, far_ref, chip_ref, own_rhs_ref, own_moduli_ref, own_inverse_ref,
           keep_ref, rhs_ref, moduli_ref, inverse_ref, tile)
    free = free_of(keep_ref, tile)
    coarse_ref[...] = coarse_solve(gathered_ref, None, tile, window_ref, solved_ref, spread_ref)
    correction = correction_of(spread_ref)

    def second(n, j):
        scaled = OMEGA * inverse_ref[n, at(j), :]
        held = free(n, j)
        result = []
        for k, coarse_value in enumerate(correction(n, j)):
            value = rhs_ref[k, n, at(j), :] * scaled + held * coarse_value
            result.append(value)
        return result

    def smooth(n, j, out):
        held = free(n, j) > 0.0
        scaled = OMEGA * inverse_ref[n, at(j), :]
        for k, value in enumerate(second(n, j)):
            image = jnp.where(held, out[k], value)
            ahead_ref[k, n, at(j), :] = value + (rhs_ref[k, n, at(j), :] - image) * scaled

    stiff(2, 16, second, smooth, moduli_ref, along_ref, up_ref, free, x_ref, late_ref)

    def ahead(n, j):
        return [ahead_ref[k, n, at(j), :] for k in range(3)]

    def keep_image(n, j, out):
        held = free(n, j) > 0.0
        for k in range(3):
            image_ref[k, n, at(j), :] = jnp.where(
                held, out[k], ahead_ref[k, n, at(j), :]
            )

    stiff(3, 15, ahead, keep_image, moduli_ref, along_ref, up_ref, free, x_ref, late_ref)

    total_ref[12:24] = jnp.zeros((12, 64, 128), jnp.float32)
    first = first_of(image_ref, inverse_ref)
    begin, add = block_forces(first, moduli_ref, along_ref, free, x_ref, total_ref)
    begin(H - 1, H)
    add(H, H + 1, "below")
    add(H + 1, H + 2, "lowest")
    inner_layers(add)
    add(H + 8, H + 8, "above")

    def lowest(j, out):
        held = free(H, j) > 0.0
        value = first(H, j)
        for k in range(3):
            sum_ref[k, at(j), :] = -jnp.where(held, out[k], value[k])

    def others(j, out):
        for k in range(3):
            sum_ref[k, at(j), :] -= out[k]

    block_scatter(total_ref, 0, lowest)
    block_scatter(total_ref, 12, others)
    dots_ref[...] = jnp.zeros_like(dots_ref)

    def products(n, unused):
        for k in range(3):
            by_rhs, by_image = [], []
            for j in range(8):
                image = image_ref[k, n, at(j), :]
                now = ahead_ref[k, n, at(j), :]
                sum_ref[k, at(j), :] += image
                by_rhs.append(now * rhs_ref[k, n, at(j), :])
                by_image.append(now * image)
            dots_ref[0, k] += sum(by_rhs[1:], by_rhs[0])
            dots_ref[1, k] += sum(by_image[1:], by_image[0])
        return unused

    lax.fori_loop(H, H + 8, products, 0)
    three = block_sums(sum_ref[...].reshape(192, 128))
    lane = lax.broadcasted_iota(jnp.int32, (1, 128), 1)
    gamma = jnp.sum(dots_ref[0])
    energy = jnp.sum(dots_ref[1])
    dots = jnp.where(lane == 0, gamma, jnp.where(lane == 1, energy, 0.0))
    send_rows(send_ref, three + [dots])


def lane_value(line, i):
    lane = lax.broadcasted_iota(jnp.int32, line.shape, 1)
    return jnp.sum(jnp.where(lane == i, line, 0.0))


def last_kernel(gathered_ref, rhs_ref, moduli_ref, inverse_ref, keep_ref, ahead_ref, image_ref,
                coarse_ref,
                next_ref, next_image_ref, scalars_ref, send_ref,
                whole_ref, along_ref, up_ref, x_ref, late_ref, dots_ref, window_ref, solved_ref, spread_ref):
    tile = tile_index()
    free = free_of(keep_ref, tile)
    dots = jnp.sum(gathered_ref[pl.ds(3, 128, stride=4), :], axis=0, keepdims=True)
    scalars_ref[...] = jnp.broadcast_to(dots, (8, 128))
    alpha = lane_value(dots, 0) / lane_value(dots, 1)
    coarse_solve(gathered_ref, coarse_ref, tile, window_ref, solved_ref, spread_ref)
    correction = correction_of(spread_ref)

    def second(n, j):
        scaled = OMEGA * inverse_ref[n, at(j), :]
        held = free(n, j)
        result = []
        for k, coarse_value in enumerate(correction(n, j)):
            value = image_ref[k, n, at(j), :] * scaled + held * coarse_value
            result.append(value)
        return result

    def smooth(n, j, out):
        held = free(n, j) > 0.0
        scaled = OMEGA * inverse_ref[n, at(j), :]
        for k, value in enumerate(second(n, j)):
            image = jnp.where(held, out[k], value)
            value = value + (image_ref[k, n, at(j), :] - image) * scaled
            whole_ref[k, n, at(j), :] = ahead_ref[k, n, at(j), :] - alpha * value

    stiff(4, 14, second, smooth, moduli_ref, along_ref, up_ref, free, x_ref, late_ref)
    dots_ref[...] = jnp.zeros_like(dots_ref)

    def ahead(n, j):
        return [whole_ref[k, n, at(j), :] for k in range(3)]

    def finish(n, j, out):
        held = free(n, j) > 0.0
        for k in range(3):
            value = whole_ref[k, n, at(j), :]
            image = jnp.where(held, out[k], value)
            next_ref[k, n - H, at(j), :] = value
            next_image_ref[k, n - H, at(j), :] = image
            before = image_ref[k, n, at(j), :]
            dots_ref[0, k] += value * (rhs_ref[k, n, at(j), :] - alpha * before)
            dots_ref[1, k] += value * image
            dots_ref[2, k] += value * before

    stiff(5, 13, ahead, finish, moduli_ref, along_ref, up_ref, free, x_ref, late_ref)
    lane = lax.broadcasted_iota(jnp.int32, (8, 128), 1)
    line = jnp.zeros((8, 128), jnp.float32)
    for i in range(3):
        line = jnp.where(lane == i, jnp.sum(dots_ref[i]), line)
    for i in range(16):
        send_ref[at(i), :] = line


def close_kernel(gathered_ref, scalars_ref, rhs_ref, ahead_ref, image_ref, next_ref,
                 next_image_ref, displacement_hbm, residual_hbm,
                 displacement_ref, residual_ref, sent):
    before = scalars_ref[0:1, :]
    gamma, energy = lane_value(before, 0), lane_value(before, 1)
    dots = jnp.sum(gathered_ref[...], axis=0, keepdims=True)
    following, own, cross = (lane_value(dots, i) for i in range(3))
    alpha = gamma / energy
    beta = following / gamma
    alpha_next = following / (own + 2.0 * beta * cross + beta * beta * energy)

    def step(n, unused):
        for k in range(3):
            ahead = ahead_ref[k, n + H]
            image = image_ref[k, n + H]
            direction = next_ref[k, n] + beta * ahead
            displacement_ref[k, n] = alpha * ahead + alpha_next * direction
            residual = rhs_ref[k, n + H] - alpha * image
            residual_ref[k, n] = residual - alpha_next * (next_image_ref[k, n] + beta * image)
        return unused

    copies = []
    for part in range(4):
        lax.fori_loop(2 * part, 2 * part + 2, step, 0)
        there = slice(2 * part, 2 * part + 2)
        for source, target in ((displacement_ref, displacement_hbm), (residual_ref, residual_hbm)):
            copy = pltpu.make_async_copy(
                source.at[:, there], target.at[:, there], sent.at[len(copies)]
            )
            copy.start()
            copies.append(copy)
    for copy in copies:
        copy.wait()


def call(kernel, outs, scratch, *args, smem=(), cost=None):
    spaces = [
        pl.BlockSpec(memory_space=pltpu.SMEM if i in smem else pltpu.VMEM)
        for i in range(len(args))
    ]
    return pl.pallas_call(
        kernel,
        out_shape=[jax.ShapeDtypeStruct(s, jnp.float32) for s in outs],
        in_specs=spaces,
        out_specs=[pl.BlockSpec(memory_space=pltpu.VMEM)] * len(outs),
        scratch_shapes=[pltpu.VMEM(s, jnp.float32) for s in scratch],
        cost_estimate=cost,
        compiler_params=pltpu.CompilerParams(vmem_limit_bytes=14 * 2**20),
    )(*args)


def to_all(block):
    count = block.shape[0] // 128
    parts = lax.all_to_all(block.reshape(128, count, 128), BOTH, 0, 0)
    return parts.reshape(block.shape)


def body(load, phases, clamp, phase_moduli):
    size = lax.axis_size(BOTH)
    pairs = [(i, i ^ 1) for i in range(size)]
    links = [(i, i + (1 if i % 2 else -1)) for i in range(1, size - 1)]
    plane = (64, 128)
    field = (3, EXT) + plane
    ready = [field, (EXT,) + plane, (EXT,) + plane]
    work = [(12,) + plane, (12,) + plane, (6,) + plane, (6,) + plane]
    halo = (17,) + plane
    hbm = pl.BlockSpec(memory_space=pltpu.HBM)
    to_chip, to_near, to_far, moduli_own = pl.pallas_call(
        pack_kernel,
        out_shape=[jax.ShapeDtypeStruct(s, jnp.float32) for s in (halo, (5,) + plane, (12,) + plane, (8,) + plane)],
        in_specs=[hbm, hbm, pl.BlockSpec(memory_space=pltpu.SMEM)],
        out_specs=[hbm] * 4,
        scratch_shapes=[
            pltpu.VMEM(load.shape, jnp.float32),
            pltpu.VMEM(phases.shape, jnp.int32),
            pltpu.VMEM((8,) + plane, jnp.float32),
            pltpu.SemaphoreType.DMA((4,)),
            pltpu.SemaphoreType.DMA((17,)),
        ],
        compiler_params=pltpu.CompilerParams(vmem_limit_bytes=60 * 2**20),
    )(load, phases, phase_moduli)
    from_near = lax.ppermute(to_near, BOTH, links)
    from_far = lax.ppermute(to_far, BOTH, links)
    from_chip = lax.ppermute(to_chip, BOTH, pairs)
    own = (3, 8) + plane
    own_rhs, own_moduli, own_inverse, keep, inner, own_sum = call(
        own_kernel, ready + [plane, (24,) + plane, (4,) + plane],
        [(12,) + plane, (6,) + plane], load, moduli_own, clamp,
        cost=pl.CostEstimate(flops=20_000_000, bytes_accessed=20_000_000, transcendentals=0),
    )
    (send,) = call(
        first_kernel, [(512, 128)],
        ready + [(12,) + plane, (6,) + plane, (24,) + plane, (4,) + plane],
        from_near, from_chip, own_rhs, own_moduli, own_inverse, keep, inner, own_sum,
    )
    gathered = to_all(send)
    ahead, image, coarse, send, rhs, moduli, inverse = call(
        middle_kernel,
        [field, field, (WINDOW, 128), (512, 128)] + ready,
        work + [(24,) + plane, (3,) + plane, (2, 3, 8, 128), (4 * WINDOW, 128),
                (3 * WINDOW, 128), (72, 128)],
        gathered, from_near, from_far, from_chip, own_rhs, own_moduli, own_inverse, keep,
    )
    gathered = to_all(send)
    following, following_image, scalars, send = call(
        last_kernel,
        [own, own, (8, 128), (128, 128)],
        [field] + work + [(3, 3, 8, 128), (4 * WINDOW, 128), (3 * WINDOW, 128), (72, 128)],
        gathered, rhs, moduli, inverse, keep, ahead, image, coarse,
    )
    gathered = to_all(send)
    last = [gathered, scalars, rhs, ahead, image, following, following_image]
    displacement, residual = pl.pallas_call(
        close_kernel,
        out_shape=[jax.ShapeDtypeStruct(own, jnp.float32)] * 2,
        in_specs=[pl.BlockSpec(memory_space=pltpu.VMEM)] * len(last),
        out_specs=[hbm, hbm],
        scratch_shapes=[
            pltpu.VMEM(own, jnp.float32),
            pltpu.VMEM(own, jnp.float32),
            pltpu.SemaphoreType.DMA((8,)),
        ],
        compiler_params=pltpu.CompilerParams(vmem_limit_bytes=14 * 2**20),
    )(*last)
    return displacement, residual


def solution(mesh):
    placed = (P(None, BOTH, None, None), P(BOTH, None, None), P(), P())
    return jax.shard_map(
        body,
        mesh=mesh,
        in_specs=placed,
        out_specs=(P(None, BOTH, None, None), P(None, BOTH, None, None)),
        check_vma=False,
    )
```
